32 devices in a mesh: fsdp: 8 (over z, y), ctx: 4 (over x, core).
Axes of the slice: x: 2, y: 2, z: 4, core: 2. Of those that a mesh axis runs over, the one named last changes fastest.
Arguments:
- token_ids: int32 [8, 512], P('fsdp', 'ctx'), may hold values from 0 to 511
- embedding: bfloat16 [512, 4096], replicated, may hold values from -15 to 15
- norm_gain: float32 [4096], replicated, may hold values from 0.5 to 1.5
- in_proj: bfloat16 [3, 4096, 4096], P(None, None, 'fsdp'), may hold values from -0.09375 to 0.09375
- short_taps: float32 [3, 3, 4096], P(None, None, 'fsdp'), may hold values from -3 to 3
- conv_taps: bfloat16 [256, 128], P('fsdp'), may hold values from -0.6 to 0.6
- out_proj: bfloat16 [4096, 4096], P('fsdp'), may hold values from -0.09375 to 0.09375
Outputs:
- output: bfloat16 [8, 512, 4096], P('fsdp', 'ctx')
The draws below stay inside these ranges and needn't reach their ends.
All inputs are finite; a program needn't handle non-finite values.
Results may differ from the reference program's by a relative error of at most 0.02.
Values may be sent and summed in bfloat16 or wider, within the bound.
No kernel may reach another device: no remote copies, remote signals or barrier semaphores. Data moves between devices by JAX's collectives and lax.ppermute only.
A program may use at most 128 MiB of HBM per device.

```python
import math
import jax
import jax.numpy as jnp
import numpy as np
from jax import lax

D = 4096
VOCAB = 512
GROUP = 16
TAPS = 128
SHORT = 3
LEN = 512
WINDOWS = 8
GROUPS = 256
N_FSDP = 8


def draw_embedding(key, part):
    key_rows, key_cols, key_values = jax.random.split(key, 3)
    row_scale = jnp.exp(jax.random.uniform(key_rows, (VOCAB, 1), jnp.float32, math.log(0.3), math.log(3.0)))
    values = jnp.clip(jax.random.normal(key_values, (VOCAB, D), jnp.float32), -5.0, 5.0)
    col_scale = jnp.exp(jax.random.uniform(key_cols, (1, D), jnp.float32, math.log(0.5), math.log(1.0)))
    return (values * row_scale * col_scale).astype(jnp.bfloat16)


def draw_conv_taps(key, part):
    key_reach, key_rough = jax.random.split(key)
    lag_axis = jnp.arange(TAPS, dtype=jnp.float32)[None, :]
    log_reach = jax.random.uniform(key_reach, (GROUPS, 1), jnp.float32, math.log(TAPS * 0.25), math.log(TAPS * 5.0))
    rough_part = jnp.clip(jax.random.normal(key_rough, (GROUPS, TAPS), jnp.float32), -4.0, 4.0)
    return (0.15 * rough_part * jnp.exp(-lag_axis / jnp.exp(log_reach))).astype(jnp.bfloat16)


def touch_ends(array, rng, low, largest):
    longest = array.shape.index(max(array.shape))
    spots = []
    for shift in (0, 1):
        where = [jax.random.randint(jax.random.fold_in(rng, axis), (), 0, length) for axis, length in enumerate(array.shape)]
        where[longest] = (where[longest] + shift) % array.shape[longest]
        spots.append(tuple(where))
    return array.at[spots[0]].set(low).at[spots[1]].set(largest)


def block_scale(key, shape, cuts, least, high):
    loudness = 1.0
    for axis_at, blocks in cuts:
        heights = jax.random.uniform(jax.random.fold_in(jax.random.fold_in(key, 6), axis_at), (blocks,), jnp.float32, least / len(cuts), high / len(cuts))
        loudness = loudness * jnp.repeat(jnp.exp(heights), shape[axis_at] // blocks).reshape((-1,) + (1,) * (len(shape) - 1 - axis_at))
    return loudness


def rank_bounds(count, slope):
    portions = [(1 << 20) // math.isqrt(standing ** slope) + 1 for standing in range(1, count + 1)]
    scale = 1 + sum(portions) // (1 << 30)
    return np.cumsum(np.array([max(1, weight // scale) for weight in portions]))


def ranked_ids(stream_key, extent, count, lean):
    table = rank_bounds(count, lean)
    pick = jax.random.randint(jax.random.fold_in(stream_key, 1), extent, 0, int(table[count - 1]))
    rank = jnp.searchsorted(jnp.asarray(table, jnp.int32), pick, side="right")
    return jax.random.permutation(jax.random.fold_in(stream_key, 2), count)[rank].astype(jnp.int32)


def gaussian(rng, dims, spread, reach, cuts=(), kind=jnp.bfloat16):
    loudness = block_scale(rng, dims, cuts, -0.22, 0.18) if cuts else 1.0
    result = jax.random.normal(rng, dims, jnp.float32) * spread * loudness
    return jnp.minimum(jnp.maximum(result, -reach), reach).astype(kind)


def setup_inputs(seed: int = 0) -> dict:
    keys = jax.random.split(jax.random.key(seed), 8)
    token_ids = touch_ends(ranked_ids(keys[0], (WINDOWS, LEN), VOCAB, 2), jax.random.fold_in(keys[0], 3), 0, VOCAB - 1).astype(jnp.int32)
    embedding = draw_embedding(jax.random.fold_in(keys[7], 71), 0)
    norm_gain = jnp.clip(1.0 + 0.1 * jax.random.normal(keys[2], (D,), jnp.float32), 0.5, 1.5)
    in_proj = gaussian(keys[3], (3, D, D), D ** -0.5, 0.09375, ((2, 8),))
    short_taps = gaussian(keys[4], (SHORT, 3, D), 0.6, 3.0, ((2, 8),), jnp.float32)
    conv_taps = draw_conv_taps(jax.random.fold_in(keys[7], 71), 0)
    out_proj = gaussian(keys[6], (D, D), D ** -0.5, 0.09375, ((0, 8),))
    return dict(token_ids=token_ids, embedding=embedding, norm_gain=norm_gain, in_proj=in_proj, short_taps=short_taps, conv_taps=conv_taps, out_proj=out_proj)


def rms_rows(table_rows, norm_gain):
    values = table_rows.astype(jnp.float32)
    inverse_rms = lax.rsqrt(lax.optimization_barrier(jnp.mean(values * values, axis=-1, keepdims=True)) + 1e-06)
    return (values * inverse_rms * norm_gain).astype(jnp.bfloat16)

def reference(token_ids, embedding, norm_gain, in_proj, short_taps, conv_taps, out_proj):
    normed = rms_rows(embedding, norm_gain)
    proj_table = jnp.einsum('vd,ide->ive', normed.astype(jnp.float32), in_proj.astype(jnp.float32)).astype(jnp.bfloat16)
    lag_grid = (jnp.arange(LEN)[:, None] - jnp.arange(LEN)[None, :]).astype(jnp.int32)
    in_reach = (lag_grid >= 0) & (lag_grid < TAPS)
    taps_wide = conv_taps.astype(jnp.float32)
    toeplitz = jnp.where(in_reach[None], jnp.take(taps_wide, jnp.clip(lag_grid, 0, TAPS - 1), axis=1), jnp.float32(0.0))
    panel_width = D // N_FSDP
    short_reach = SHORT - 1

    def one_window(ids_row):
        projected = jnp.take(proj_table, ids_row, axis=1)
        padded = jnp.pad(projected.astype(jnp.float32), ((0, 0), (short_reach, 0), (0, 0)))
        featured = jnp.zeros(projected.shape, jnp.float32)
        for offset in range(SHORT):
            featured = featured + short_taps[offset][:, None, :] * padded[:, short_reach - offset:short_reach - offset + LEN, :]
        product = (featured[1] * featured[2]).astype(jnp.bfloat16)
        grouped = product.astype(jnp.float32).reshape(LEN, GROUPS, GROUP)
        filtered = jnp.einsum('gts,sgc->tgc', toeplitz, grouped).reshape(LEN, D)
        gated = (featured[0] * filtered).astype(jnp.bfloat16)

        def add_block(block_index, running):
            first = (block_index * panel_width).astype(jnp.int32)
            channel_cols = lax.dynamic_slice_in_dim(gated, first, panel_width, 1)
            weight_rows = lax.dynamic_slice_in_dim(out_proj, first, panel_width, 0)
            block_out = jnp.dot(channel_cols, weight_rows, preferred_element_type=jnp.float32).astype(jnp.bfloat16)
            block_out = lax.optimization_barrier(block_out)
            return running + block_out.astype(jnp.float32)
        summed = lax.fori_loop(0, N_FSDP, add_block, jnp.zeros((LEN, D), jnp.float32))
        residual = jnp.take(embedding, ids_row, axis=0).astype(jnp.float32)
        return (residual + summed).astype(jnp.bfloat16)
    return lax.map(one_window, token_ids)
```

```python
import functools

import jax
import jax.numpy as jnp
from jax import lax
from jax.experimental import pallas as pl
from jax.experimental.pallas import tpu as pltpu
from jax.sharding import PartitionSpec as P

GROUP = 16
TAPS = 128
SHORT = 3
LANES = 128
LEAD = 16


def from_behind(x, axis, by):
    peers = lax.axis_size(axis)
    return lax.ppermute(x, axis, [(i, i + by) for i in range(peers) if i + by < peers])


def swap(x, axis, mask):
    peers = lax.axis_size(axis)
    return lax.ppermute(x, axis, [(i, i ^ mask) for i in range(peers)])


def exchange_bits():
    peers = lax.axis_size("fsdp")
    return [1 << b for b in reversed(range(peers.bit_length() - 1))]


def normalize_rows(table_rows, norm_gain):
    values = table_rows.astype(jnp.float32)
    inverse_rms = lax.rsqrt(jnp.mean(values * values, axis=-1, keepdims=True) + 1e-06)
    return (values * inverse_rms * norm_gain).astype(jnp.bfloat16)


def gather_ids(token_ids):
    tok_len = token_ids.shape[1]
    place = lax.axis_index("ctx")
    one = from_behind(token_ids, "ctx", 1)
    two = from_behind(token_ids[:, tok_len - LEAD :], "ctx", 2)
    one = jnp.where(place >= 1, one, -1)
    two = jnp.where(place >= 2, two, -1)
    ids = jnp.concatenate([two, one, token_ids], axis=1)
    bits = exchange_bits()
    while bits:
        if len(bits) > 1:
            low, high = bits[:2]
            ids = jnp.concatenate([ids] + [swap(ids, "fsdp", mask) for mask in (low, high, low | high)], axis=0)
            bits = bits[2:]
        else:
            ids = jnp.concatenate([ids, swap(ids, "fsdp", bits[0])], axis=0)
            bits = []
    return ids


def mixer_kernel(ids_ref, table_ref, short_ref, base_ref, gated_ref, toeplitz, held):
    tok_len, panel = gated_ref.shape[1:]
    vocab = table_ref.shape[1]
    rows = ids_ref.shape[2]
    reach = 2 * tok_len
    tiles = panel // LANES
    per_tile = LANES // GROUP

    @pl.when(pl.program_id(0) == 0)
    def _():
        for tile in range(tiles):
            for k in range(per_tile):
                g = tile * per_tile + k
                wide = jnp.broadcast_to(base_ref[pl.ds(g, 1), :], (tok_len, reach))
                shifted = pltpu.roll(wide, 0, 1, stride=1, stride_axis=0)
                toeplitz[tile, pl.ds(k * tok_len, tok_len), :] = shifted.astype(jnp.bfloat16)

    names = lax.broadcasted_iota(jnp.int32, (vocab, rows), 0)
    lane_group = lax.broadcasted_iota(jnp.int32, (tok_len, 2 * LANES), 1) % LANES // GROUP
    for v in range(2):
        one_hot = (names == ids_ref[v]).astype(jnp.float32).astype(jnp.bfloat16)
        for i in range(3):
            held[v, i] = lax.dot_general(
                one_hot, table_ref[i], (((0,), (0,)), ((), ())), preferred_element_type=jnp.float32
            ).astype(jnp.bfloat16).astype(jnp.float32)

    def featured(v, i, first, count, cols):
        total = short_ref[0, i : i + 1, cols] * held[v, i, pl.ds(first, count), cols]
        for j in range(1, SHORT):
            total += short_ref[j, i : i + 1, cols] * held[v, i, pl.ds(first - j, count), cols]
        return total

    start = rows - reach
    for tile in range(tiles):
        cols = slice(tile * LANES, (tile + 1) * LANES)
        products = []
        for v in range(2):
            key = featured(v, 1, start, reach, cols)
            value = featured(v, 2, start, reach, cols)
            products.append((key * value).astype(jnp.bfloat16))
        both = jnp.concatenate(products, axis=1)
        filtered = None
        for k in range(per_tile):
            one = jnp.dot(
                toeplitz[tile, pl.ds(k * tok_len, tok_len), :], both, preferred_element_type=jnp.float32
            )
            filtered = one if k == 0 else jnp.where(lane_group == k, one, filtered)
        for v in range(2):
            query = featured(v, 0, rows - tok_len, tok_len, cols)
            gated_ref[v, :, cols] = (query * filtered[:, v * LANES : (v + 1) * LANES]).astype(jnp.bfloat16)


def mix(ids, table, short_taps, conv_taps, tok_len):
    windows, rows = ids.shape
    _, vocab, panel = table.shape
    groups = conv_taps.shape[0]
    reach = 2 * tok_len
    base = jnp.pad(conv_taps[:, ::-1].astype(jnp.float32), ((0, 0), (1, reach - TAPS - 1)))
    whole = lambda shape: pl.BlockSpec(shape, lambda p: (0,) * len(shape))
    return pl.pallas_call(
        mixer_kernel,
        grid=(windows // 2,),
        in_specs=[
            pl.BlockSpec((2, 1, rows), lambda p: (p, 0, 0)),
            whole((3, vocab, panel)),
            whole((SHORT, 3, panel)),
            whole((groups, reach)),
        ],
        out_specs=pl.BlockSpec((2, tok_len, panel), lambda p: (p, 0, 0)),
        out_shape=jax.ShapeDtypeStruct((windows, tok_len, panel), jnp.bfloat16),
        scratch_shapes=[
            pltpu.VMEM((panel // LANES, LANES // GROUP * tok_len, reach), jnp.bfloat16),
            pltpu.VMEM((2, 3, rows, panel), jnp.float32),
        ],
        compiler_params=pltpu.CompilerParams(vmem_limit_bytes=40 * 1024 * 1024),
        cost_estimate=pl.CostEstimate(flops=8_000_000_000, bytes_accessed=8_000_000, transcendentals=0),
    )(ids.reshape(windows, 1, rows), table, short_taps, base)


def per_device(token_ids, embedding, norm_gain, in_proj, short_taps, conv_taps, out_proj):
    tok_len = token_ids.shape[1]
    ids = gather_ids(token_ids)
    normed = normalize_rows(embedding, norm_gain)
    table = jnp.einsum("vd,idc->ivc", normed, in_proj, preferred_element_type=jnp.float32).astype(jnp.bfloat16)
    gated = mix(ids, table, short_taps, conv_taps, tok_len)
    partial = jnp.einsum("wtc,cd->wtd", gated, out_proj, preferred_element_type=jnp.float32).astype(jnp.bfloat16)
    for bit in reversed(exchange_bits()):
        half = partial.shape[0] // 2
        got = swap(partial[half:], "fsdp", bit)
        kind = jnp.bfloat16 if half > 1 else jnp.float32
        partial = (partial[:half].astype(jnp.float32) + got.astype(jnp.float32)).astype(kind)
    residual = jnp.take(embedding, token_ids[0], axis=0, mode="clip").astype(jnp.float32)
    return (residual + partial[0]).astype(jnp.bfloat16)[None]


def solution(mesh):
    return jax.shard_map(
        per_device,
        mesh=mesh,
        in_specs=(
            P("fsdp", "ctx"),
            P(),
            P(),
            P(None, None, "fsdp"),
            P(None, None, "fsdp"),
            P("fsdp", None),
            P("fsdp", None),
        ),
        out_specs=P("fsdp", "ctx", None),
        check_vma=False,
    )
```

```python
import functools

import jax
import jax.numpy as jnp
from jax import lax
from jax.experimental import pallas as pl
from jax.experimental.pallas import tpu as pltpu
from jax.sharding import PartitionSpec as P

GROUP = 16
TAPS = 128
SHORT = 3
LANES = 128
LEAD = 16
CHUNKS = 4


def from_behind(x, axis, by):
    peers = lax.axis_size(axis)
    return lax.ppermute(x, axis, [(i, i + by) for i in range(peers) if i + by < peers])


def swap(x, axis, mask):
    peers = lax.axis_size(axis)
    return lax.ppermute(x, axis, [(i, i ^ mask) for i in range(peers)])


def exchange_bits():
    peers = lax.axis_size("fsdp")
    return [1 << b for b in reversed(range(peers.bit_length() - 1))]


def normalize_rows(table_rows, norm_gain):
    values = table_rows.astype(jnp.float32)
    inverse_rms = lax.rsqrt(jnp.mean(values * values, axis=-1, keepdims=True) + 1e-06)
    return (values * inverse_rms * norm_gain).astype(jnp.bfloat16)


def gather_ids(token_ids):
    tok_len = token_ids.shape[1]
    place = lax.axis_index("ctx")
    one = from_behind(token_ids, "ctx", 1)
    two = from_behind(token_ids[:, tok_len - LEAD :], "ctx", 2)
    one = jnp.where(place >= 1, one, -1)
    two = jnp.where(place >= 2, two, -1)
    ids = jnp.concatenate([two, one, token_ids], axis=1)
    bits = exchange_bits()
    while bits:
        if len(bits) > 1:
            low, high = bits[:2]
            ids = jnp.concatenate([ids] + [swap(ids, "fsdp", mask) for mask in (low, high, low | high)], axis=0)
            bits = bits[2:]
        else:
            ids = jnp.concatenate([ids, swap(ids, "fsdp", bits[0])], axis=0)
            bits = []
    return ids


def toeplitz_kernel(base_ref, out_ref):
    per_tile = LANES // GROUP
    tok_len = out_ref.shape[1] // per_tile
    reach = out_ref.shape[2]
    for k in range(per_tile):
        wide = jnp.broadcast_to(base_ref[k : k + 1, :], (tok_len, reach))
        shifted = pltpu.roll(wide, 0, 1, stride=1, stride_axis=0)
        out_ref[0, pl.ds(k * tok_len, tok_len), :] = shifted.astype(jnp.bfloat16)


def build_toeplitz(conv_taps, tok_len):
    reach = 2 * tok_len
    per_tile = LANES // GROUP
    tiles = conv_taps.shape[0] // per_tile
    base = jnp.pad(conv_taps[:, ::-1].astype(jnp.float32), ((0, 0), (1, reach - TAPS - 1)))
    return pl.pallas_call(
        toeplitz_kernel,
        grid=(tiles,),
        in_specs=[pl.BlockSpec((per_tile, reach), lambda i: (i, 0))],
        out_specs=pl.BlockSpec((1, per_tile * tok_len, reach), lambda i: (i, 0, 0)),
        out_shape=jax.ShapeDtypeStruct((tiles, per_tile * tok_len, reach), jnp.bfloat16),
        cost_estimate=pl.CostEstimate(flops=0, bytes_accessed=4_000_000, transcendentals=0),
    )(base)


def mixer_kernel(ids_ref, table_ref, short_ref, toeplitz, gated_ref, held):
    tok_len, panel = gated_ref.shape[1:]
    vocab = table_ref.shape[1]
    rows = ids_ref.shape[2]
    reach = 2 * tok_len
    tiles = panel // LANES
    per_tile = LANES // GROUP
    names = lax.broadcasted_iota(jnp.int32, (vocab, rows), 0)
    lane_group = lax.broadcasted_iota(jnp.int32, (tok_len, 2 * LANES), 1) % LANES // GROUP
    for v in range(2):
        one_hot = (names == ids_ref[v]).astype(jnp.float32).astype(jnp.bfloat16)
        for i in range(3):
            held[v, i] = lax.dot_general(
                one_hot, table_ref[i], (((0,), (0,)), ((), ())), preferred_element_type=jnp.float32
            ).astype(jnp.bfloat16).astype(jnp.float32)

    def featured(v, i, first, count, cols):
        total = short_ref[0, i : i + 1, cols] * held[v, i, pl.ds(first, count), cols]
        for j in range(1, SHORT):
            total += short_ref[j, i : i + 1, cols] * held[v, i, pl.ds(first - j, count), cols]
        return total

    start = rows - reach
    for tile in range(tiles):
        cols = slice(tile * LANES, (tile + 1) * LANES)
        products = []
        for v in range(2):
            key = featured(v, 1, start, reach, cols)
            value = featured(v, 2, start, reach, cols)
            products.append((key * value).astype(jnp.bfloat16))
        both = jnp.concatenate(products, axis=1)
        filtered = None
        for k in range(per_tile):
            one = jnp.dot(
                toeplitz[tile, pl.ds(k * tok_len, tok_len), :], both, preferred_element_type=jnp.float32
            )
            filtered = one if k == 0 else jnp.where(lane_group == k, one, filtered)
        for v in range(2):
            query = featured(v, 0, rows - tok_len, tok_len, cols)
            gated_ref[v, :, cols] = (query * filtered[:, v * LANES : (v + 1) * LANES]).astype(jnp.bfloat16)


def mix(ids, table, short_taps, toeplitz, tok_len):
    windows, rows = ids.shape
    _, vocab, panel = table.shape
    whole = lambda array: pl.BlockSpec(array.shape, lambda p: (0,) * array.ndim)
    return pl.pallas_call(
        mixer_kernel,
        grid=(windows // 2,),
        in_specs=[
            pl.BlockSpec((2, 1, rows), lambda p: (p, 0, 0)),
            whole(table),
            whole(short_taps),
            whole(toeplitz),
        ],
        out_specs=pl.BlockSpec((2, tok_len, panel), lambda p: (p, 0, 0)),
        out_shape=jax.ShapeDtypeStruct((windows, tok_len, panel), jnp.bfloat16),
        scratch_shapes=[pltpu.VMEM((2, 3, rows, panel), jnp.float32)],
        compiler_params=pltpu.CompilerParams(vmem_limit_bytes=40 * 1024 * 1024),
        cost_estimate=pl.CostEstimate(flops=4_000_000_000, bytes_accessed=4_000_000, transcendentals=0),
    )(ids.reshape(windows, 1, rows), table, short_taps, toeplitz)


def panel_kernel(place_ref, mine_ref, other_ref, w0, w1, w2, w3, even_ref, odd_ref, out_ref):
    own = (w0, w1, w2, w3)
    for k in range(4):
        beside = (even_ref, odd_ref)[k % 2]
        total = jnp.dot(mine_ref[...], own[k][...], preferred_element_type=jnp.float32)
        total += jnp.dot(other_ref[...], beside[k // 2], preferred_element_type=jnp.float32)
        out_ref[k] = total.astype(out_ref.dtype)


def panel(place, mine, other, out_proj, even, odd, chunk):
    count, tok_len, depth = mine.shape
    rows = count * tok_len
    quarter = even.shape[2]
    whole = lambda shape: pl.BlockSpec(shape, lambda s, place: (0,) * len(shape))
    at = lambda k: pl.BlockSpec((depth, quarter), lambda s, place: (0, chunk * 4 + (place[0] ^ k)))
    return pl.pallas_call(
        panel_kernel,
        grid_spec=pltpu.PrefetchScalarGridSpec(
            num_scalar_prefetch=1,
            grid=(1,),
            in_specs=[whole((rows, depth)), whole((rows, depth))]
            + [at(k) for k in range(4)]
            + [whole(even.shape), whole(odd.shape)],
            out_specs=whole((4, rows, quarter)),
        ),
        out_shape=jax.ShapeDtypeStruct((4, rows, quarter), jnp.bfloat16),
        compiler_params=pltpu.CompilerParams(vmem_limit_bytes=32 * 1024 * 1024),
        cost_estimate=pl.CostEstimate(
            flops=16 * rows * depth * quarter, bytes_accessed=16 * depth * quarter, transcendentals=0
        ),
    )(
        place,
        mine.reshape(rows, depth),
        other.reshape(rows, depth),
        *[out_proj] * 4,
        even,
        odd,
    ).reshape(4, count, tok_len, quarter)


def add(a, b):
    return (a.astype(jnp.float32) + b.astype(jnp.float32)).astype(jnp.bfloat16)


def place_kernel(place_ref, so_far_ref, near_ref, far_ref, out_ref):
    total = near_ref[0, 0].astype(jnp.float32) + far_ref[0, 0].astype(jnp.float32)
    out_ref[...] = (so_far_ref[...].astype(jnp.float32) + total).astype(jnp.bfloat16)


def place_quarters(place, so_far, near, far, chunk):
    _, _, tok_len, quarter = near.shape
    at = pl.BlockSpec((tok_len, quarter), lambda k, place: (0, chunk * 4 + (place[0] ^ k)))
    one = pl.BlockSpec((1, 1, tok_len, quarter), lambda k, place: (k, 0, 0, 0))
    return pl.pallas_call(
        place_kernel,
        grid_spec=pltpu.PrefetchScalarGridSpec(
            num_scalar_prefetch=1, grid=(4,), in_specs=[at, one, one], out_specs=at
        ),
        out_shape=jax.ShapeDtypeStruct(so_far.shape, so_far.dtype),
        input_output_aliases={1: 0},
        cost_estimate=pl.CostEstimate(flops=0, bytes_accessed=16 * tok_len * quarter, transcendentals=0),
    )(place, so_far, near, far)


def per_device(token_ids, embedding, norm_gain, in_proj, short_taps, conv_taps, out_proj):
    tok_len = token_ids.shape[1]
    depth, width = out_proj.shape
    place = lax.axis_index("ctx")
    quarter = width // CHUNKS // 4
    bits = exchange_bits()

    beside = []
    for j in range(CHUNKS):
        piece = lax.dynamic_slice_in_dim(out_proj, (j * 4 + place) * quarter, quarter, axis=1)
        piece = swap(piece, "fsdp", bits[-2])
        even = jnp.stack([piece, swap(piece, "ctx", 2)])
        beside.append((even, swap(even, "ctx", 1)))

    ids = gather_ids(token_ids)
    toeplitz = build_toeplitz(conv_taps, tok_len)
    normed = normalize_rows(embedding, norm_gain)
    table = jnp.einsum("vd,idc->ivc", normed, in_proj, preferred_element_type=jnp.float32).astype(jnp.bfloat16)

    half = ids.shape[0] // 2
    mine, other = [], []
    for first in (half, 0):
        gated = mix(ids[first : first + half], table, short_taps, toeplitz, tok_len)
        mine.append(gated[: half // 2])
        other.append(swap(gated[half // 2 :], "fsdp", bits[-2]))

    at = place.reshape(1).astype(jnp.int32)
    out = jnp.take(embedding, token_ids[0], axis=0, mode="clip")
    for j in range(CHUNKS):
        away = panel(at, mine[0], other[0], out_proj, *beside[j], j)
        got = swap(away, "fsdp", bits[-1])
        total = add(panel(at, mine[1], other[1], out_proj, *beside[j], j), got)
        for bit in reversed(bits[:-2]):
            half = total.shape[1] // 2
            got = swap(total[:, half:], "fsdp", bit)
            total = add(total[:, :half], got) if half > 1 else total[:, :half]
        out = place_quarters(at, out, total, got, j)
    return out[None]


def solution(mesh):
    return jax.shard_map(
        per_device,
        mesh=mesh,
        in_specs=(
            P("fsdp", "ctx"),
            P(),
            P(),
            P(None, None, "fsdp"),
            P(None, None, "fsdp"),
            P("fsdp", None),
            P("fsdp", None),
        ),
        out_specs=P("fsdp", "ctx", None),
        check_vma=False,
    )
```

```python
import functools

import jax
import jax.numpy as jnp
from jax import lax
from jax.experimental import pallas as pl
from jax.experimental.pallas import tpu as pltpu
from jax.sharding import PartitionSpec as P

GROUP = 16
TAPS = 128
SHORT = 3
LANES = 128
LEAD = 16
SPLITS = 2
STEPS = 2


def from_behind(x, axis, by):
    peers = lax.axis_size(axis)
    return lax.ppermute(x, axis, [(i, i + by) for i in range(peers) if i + by < peers])


def swap(x, axis, mask):
    peers = lax.axis_size(axis)
    return lax.ppermute(x, axis, [(i, i ^ mask) for i in range(peers)])


def exchange_bits():
    peers = lax.axis_size("fsdp")
    return [1 << b for b in reversed(range(peers.bit_length() - 1))]


def params(mib=40):
    return pltpu.CompilerParams(vmem_limit_bytes=mib * 1024 * 1024)


def cost(flops, bytes_accessed):
    return pl.CostEstimate(flops=flops, bytes_accessed=bytes_accessed, transcendentals=0)


def whole(array):
    return pl.BlockSpec(array.shape, lambda *_: (0,) * array.ndim)


def gather_ids(token_ids):
    tok_len = token_ids.shape[1]
    place = lax.axis_index("ctx")
    one = jnp.where(place >= 1, from_behind(token_ids, "ctx", 1), -1)
    two = jnp.where(place >= 2, from_behind(token_ids, "ctx", 2), -1)
    ids = jnp.concatenate([two[:, tok_len - LEAD :], one, token_ids], axis=1)
    bits = exchange_bits()
    while bits:
        if len(bits) > 1:
            low, high = bits[:2]
            ids = jnp.concatenate([ids] + [swap(ids, "fsdp", mask) for mask in (low, high, low | high)], axis=0)
            bits = bits[2:]
        else:
            ids = jnp.concatenate([ids, swap(ids, "fsdp", bits[0])], axis=0)
            bits = []
    return ids


def norm_kernel(rows_ref, gain_ref, base_ref, normed_ref, toeplitz_ref):
    values = rows_ref[...].astype(jnp.float32)
    inverse_rms = lax.rsqrt(jnp.mean(values * values, axis=-1, keepdims=True) + 1e-06)
    normed_ref[...] = (values * inverse_rms * gain_ref[...]).astype(jnp.bfloat16)
    per_tile, reach = base_ref.shape
    tok_len = toeplitz_ref.shape[1] // per_tile
    for k in range(per_tile):
        wide = jnp.broadcast_to(base_ref[k : k + 1, :], (tok_len, reach))
        shifted = pltpu.roll(wide, 0, 1, stride=1, stride_axis=0)
        toeplitz_ref[0, pl.ds(k * tok_len, tok_len), :] = shifted.astype(jnp.bfloat16)


def norm_and_toeplitz(embedding, norm_gain, conv_taps, tok_len):
    vocab, width = embedding.shape
    reach = 2 * tok_len
    per_tile = LANES // GROUP
    tiles = conv_taps.shape[0] // per_tile
    base = jnp.pad(conv_taps[:, ::-1].astype(jnp.float32), ((0, 0), (1, reach - TAPS - 1)))
    return pl.pallas_call(
        norm_kernel,
        grid=(tiles,),
        in_specs=[
            pl.BlockSpec((vocab // tiles, width), lambda i: (i, 0)),
            pl.BlockSpec((1, width), lambda i: (0, 0)),
            pl.BlockSpec((per_tile, reach), lambda i: (i, 0)),
        ],
        out_specs=[
            pl.BlockSpec((vocab // tiles, width), lambda i: (i, 0)),
            pl.BlockSpec((1, per_tile * tok_len, reach), lambda i: (i, 0, 0)),
        ],
        out_shape=[
            jax.ShapeDtypeStruct((vocab, width), jnp.bfloat16),
            jax.ShapeDtypeStruct((tiles, per_tile * tok_len, reach), jnp.bfloat16),
        ],
        compiler_params=params(),
        cost_estimate=cost(2_000_000_000, 10_000_000),
    )(embedding, norm_gain.reshape(1, width), base)


def table_kernel(normed_ref, weight_ref, out_ref):
    out_ref[0] = jnp.dot(normed_ref[...], weight_ref[0], preferred_element_type=jnp.float32).astype(jnp.bfloat16)


def project(normed, in_proj, first, count):
    vocab, width = normed.shape
    panel_width = in_proj.shape[2]
    cols = min(256, panel_width)
    per = panel_width // cols
    return pl.pallas_call(
        table_kernel,
        grid=(count * per,),
        in_specs=[
            whole(normed),
            pl.BlockSpec((1, width, cols), lambda s: (first + s // per, 0, s % per)),
        ],
        out_specs=pl.BlockSpec((1, vocab, cols), lambda s: (s // per, 0, s % per)),
        out_shape=jax.ShapeDtypeStruct((count, vocab, panel_width), jnp.bfloat16),
        compiler_params=params(),
        cost_estimate=cost(2 * vocab * width * panel_width * count, 2 * width * panel_width * count),
    )(normed, in_proj)


def mixer_kernel(ids_ref, query_ref, kv_ref, short_ref, toeplitz, gated_ref, held_query, held):
    tok_len, panel_width = gated_ref.shape[1:]
    vocab = kv_ref.shape[1]
    rows = ids_ref.shape[2]
    reach = 2 * tok_len
    lead = rows - reach
    tiles = panel_width // LANES
    per_tile = LANES // GROUP
    names = lax.broadcasted_iota(jnp.int32, (vocab, rows), 0)
    lane_group = lax.broadcasted_iota(jnp.int32, (tok_len, 2 * LANES), 1) % LANES // GROUP

    def look_up(one_hot, table):
        found = lax.dot_general(one_hot, table, (((0,), (0,)), ((), ())), preferred_element_type=jnp.float32)
        return found.astype(jnp.bfloat16).astype(jnp.float32)

    for v in range(2):
        one_hot = (names == ids_ref[v]).astype(jnp.float32).astype(jnp.bfloat16)
        held[v, 0] = look_up(one_hot, kv_ref[0])
        held[v, 1] = look_up(one_hot, kv_ref[1])
        held_query[v] = look_up(one_hot[:, rows - lead - tok_len :], query_ref[0])

    def featured(source, i, count, cols):
        total = short_ref[0, i : i + 1, cols] * source[pl.ds(lead, count), cols]
        for j in range(1, SHORT):
            total += short_ref[j, i : i + 1, cols] * source[pl.ds(lead - j, count), cols]
        return total

    for tile in range(tiles):
        cols = slice(tile * LANES, (tile + 1) * LANES)
        products = []
        for v in range(2):
            key = featured(held.at[v, 0], 1, reach, cols)
            value = featured(held.at[v, 1], 2, reach, cols)
            products.append((key * value).astype(jnp.bfloat16))
        both = jnp.concatenate(products, axis=1)
        filtered = None
        for k in range(per_tile):
            one = jnp.dot(
                toeplitz[tile, pl.ds(k * tok_len, tok_len), :], both, preferred_element_type=jnp.float32
            )
            filtered = one if k == 0 else jnp.where(lane_group == k, one, filtered)
        for v in range(2):
            query = featured(held_query.at[v], 0, tok_len, cols)
            gated_ref[v, :, cols] = (query * filtered[:, v * LANES : (v + 1) * LANES]).astype(jnp.bfloat16)


def mix(ids, query, key_value, short_taps, toeplitz, tok_len):
    windows, rows = ids.shape
    panel_width = query.shape[2]
    return pl.pallas_call(
        mixer_kernel,
        grid=(windows // 2,),
        in_specs=[pl.BlockSpec((2, 1, rows), lambda p: (p, 0, 0))]
        + [whole(array) for array in (query, key_value, short_taps, toeplitz)],
        out_specs=pl.BlockSpec((2, tok_len, panel_width), lambda p: (p, 0, 0)),
        out_shape=jax.ShapeDtypeStruct((windows, tok_len, panel_width), jnp.bfloat16),
        scratch_shapes=[
            pltpu.VMEM((2, LEAD + tok_len, panel_width), jnp.float32),
            pltpu.VMEM((2, 2, rows, panel_width), jnp.float32),
        ],
        compiler_params=params(),
        cost_estimate=cost(4_000_000_000, 4_000_000),
    )(ids.reshape(windows, 1, rows), query, key_value, short_taps, toeplitz)


def panel_kernel(place_ref, mine_ref, other_ref, w0, w1, w2, w3, even_ref, odd_ref, out_ref):
    own = (w0, w1, w2, w3)
    count, _, tok_len, _ = out_ref.shape
    for k in range(4):
        beside = (even_ref, odd_ref)[k % 2]
        total = jnp.dot(mine_ref[...], own[k][...], preferred_element_type=jnp.float32)
        total += jnp.dot(other_ref[...], beside[k // 2], preferred_element_type=jnp.float32)
        for w in range(count):
            out_ref[w, k] = total[w * tok_len : (w + 1) * tok_len].astype(out_ref.dtype)


def panel(place, mine, other, out_proj, even, odd, split, step):
    count, tok_len, depth = mine.shape
    rows = count * tok_len
    cols = even.shape[2] // STEPS
    fixed = lambda shape: pl.BlockSpec(shape, lambda s, place: (0,) * len(shape))
    at = lambda k: pl.BlockSpec((depth, cols), lambda s, place: (0, (split * 4 + (place[0] ^ k)) * STEPS + step))
    beside = pl.BlockSpec((2, depth, cols), lambda s, place: (0, 0, step))
    return pl.pallas_call(
        panel_kernel,
        grid_spec=pltpu.PrefetchScalarGridSpec(
            num_scalar_prefetch=1,
            grid=(1,),
            in_specs=[fixed((rows, depth))] * 2 + [at(k) for k in range(4)] + [beside] * 2,
            out_specs=fixed((count, 4, tok_len, cols)),
        ),
        out_shape=jax.ShapeDtypeStruct((count, 4, tok_len, cols), jnp.bfloat16),
        compiler_params=params(),
        cost_estimate=cost(16 * rows * depth * cols, 16 * depth * cols),
    )(place, mine.reshape(rows, depth), other.reshape(rows, depth), *[out_proj] * 4, even, odd)


def residual_kernel(ids_ref, rows_ref, out_ref):
    names = lax.broadcasted_iota(jnp.int32, (rows_ref.shape[0], ids_ref.shape[1]), 0)
    one_hot = (names == ids_ref[...]).astype(jnp.float32).astype(jnp.bfloat16)
    out_ref[...] = lax.dot_general(
        one_hot, rows_ref[...], (((0,), (0,)), ((), ())), preferred_element_type=jnp.float32
    ).astype(jnp.bfloat16)


def residual(token_ids, embedding):
    vocab, width = embedding.shape
    tok_len = token_ids.shape[1]
    cols = width // 4
    return pl.pallas_call(
        residual_kernel,
        grid=(4,),
        in_specs=[whole(token_ids), pl.BlockSpec((vocab, cols), lambda i: (0, i))],
        out_specs=pl.BlockSpec((tok_len, cols), lambda i: (0, i)),
        out_shape=jax.ShapeDtypeStruct((tok_len, width), jnp.bfloat16),
        cost_estimate=cost(2 * vocab * tok_len * width, 2 * vocab * width),
    )(token_ids, embedding)


def place_kernel(step, place_ref, so_far_ref, near_ref, far_ref, out_ref):
    tok_len, cols = near_ref.shape[2:]
    out_ref[...] = so_far_ref[...]
    for k in range(4):
        first = pl.multiple_of(((place_ref[0] ^ k) * STEPS + step) * cols, LANES)
        total = near_ref[0, k].astype(jnp.float32) + far_ref[0, k].astype(jnp.float32)
        at = pl.ds(first, cols)
        out_ref[:, at] = (so_far_ref[:, at].astype(jnp.float32) + total).astype(jnp.bfloat16)


def place_quarters(place, so_far, near, far, split, step):
    _, _, tok_len, cols = near.shape
    part = pl.BlockSpec((tok_len, 4 * STEPS * cols), lambda s, place: (0, split))
    one = pl.BlockSpec((1, 4, tok_len, cols), lambda s, place: (0, 0, 0, 0))
    return pl.pallas_call(
        functools.partial(place_kernel, step),
        grid_spec=pltpu.PrefetchScalarGridSpec(
            num_scalar_prefetch=1, grid=(1,), in_specs=[part, one, one], out_specs=part
        ),
        out_shape=jax.ShapeDtypeStruct(so_far.shape, so_far.dtype),
        input_output_aliases={1: 0},
        cost_estimate=cost(0, 16 * tok_len * cols * STEPS),
    )(place, so_far, near, far)


def add(a, b):
    return (a.astype(jnp.float32) + b.astype(jnp.float32)).astype(jnp.bfloat16)


def per_device(token_ids, embedding, norm_gain, in_proj, short_taps, conv_taps, out_proj):
    tok_len = token_ids.shape[1]
    width = out_proj.shape[1]
    place = lax.axis_index("ctx")
    quarter = width // SPLITS // 4
    bits = exchange_bits()

    beside = []
    for j in range(SPLITS):
        piece = lax.dynamic_slice_in_dim(out_proj, (j * 4 + place) * quarter, quarter, axis=1)
        piece = swap(piece, "fsdp", bits[-2])
        even = jnp.stack([piece, swap(piece, "ctx", 2)])
        beside.append((even, swap(even, "ctx", 1)))

    ids = gather_ids(token_ids)
    normed, toeplitz = norm_and_toeplitz(embedding, norm_gain, conv_taps, tok_len)
    key_value = project(normed, in_proj, 1, 2)
    query = project(normed, in_proj, 0, 1)

    half = ids.shape[0] // 2
    mine, other = [], []
    for first in (half, 0):
        gated = mix(ids[first : first + half], query, key_value, short_taps, toeplitz, tok_len)
        mine.append(gated[: half // 2])
        other.append(swap(gated[half // 2 :], "fsdp", bits[-2]))

    at = place.reshape(1).astype(jnp.int32)
    out = residual(token_ids, embedding)
    for j in range(SPLITS):
        for step in range(STEPS):
            away = panel(at, mine[0], other[0], out_proj, *beside[j], j, step)
            got = swap(away, "fsdp", bits[-1])
            total = add(panel(at, mine[1], other[1], out_proj, *beside[j], j, step), got)
            for bit in reversed(bits[:-2]):
                half = total.shape[0] // 2
                got = swap(total[half:], "fsdp", bit)
                total = add(total[:half], got) if half > 1 else total[:half]
            out = place_quarters(at, out, total, got, j, step)
    return out[None]


def solution(mesh):
    return jax.shard_map(
        per_device,
        mesh=mesh,
        in_specs=(
            P("fsdp", "ctx"),
            P(),
            P(),
            P(None, None, "fsdp"),
            P(None, None, "fsdp"),
            P("fsdp", None),
            P("fsdp", None),
        ),
        out_specs=P("fsdp", "ctx", None),
        check_vma=False,
    )
```

```python
import functools

import jax
import jax.numpy as jnp
from jax import lax
from jax.experimental import pallas as pl
from jax.experimental.pallas import tpu as pltpu
from jax.sharding import PartitionSpec as P

GROUP = 16
TAPS = 128
SHORT = 3
LANES = 128
LEAD = 16
SPLITS = ((0, 4, 2, ((0, 4),)), (4, 4, 4, ((0, 4),)), (8, 8, 2, ((0, 4), (4, 4))))
SIXTEENTHS = 16


def from_behind(x, axis, by):
    peers = lax.axis_size(axis)
    return lax.ppermute(x, axis, [(i, i + by) for i in range(peers) if i + by < peers])


def swap(x, axis, mask):
    peers = lax.axis_size(axis)
    return lax.ppermute(x, axis, [(i, i ^ mask) for i in range(peers)])


def exchange_bits():
    peers = lax.axis_size("fsdp")
    return [1 << b for b in reversed(range(peers.bit_length() - 1))]


def params(mib=24):
    return pltpu.CompilerParams(vmem_limit_bytes=mib * 1024 * 1024)


def cost(flops, bytes_accessed):
    return pl.CostEstimate(flops=flops, bytes_accessed=bytes_accessed, transcendentals=0)


def whole(array):
    return pl.BlockSpec(array.shape, lambda *_: (0,) * array.ndim)


def level_ids(ids, group):
    masks = [0]
    for bit in group:
        masks += [mask | bit for mask in masks]
    return jnp.concatenate([ids] + [swap(ids, "fsdp", mask) for mask in masks[1:]], axis=0)


def with_lead(ids):
    tok_len = ids.shape[1]
    place = lax.axis_index("ctx")
    one = jnp.where(place >= 1, from_behind(ids, "ctx", 1), -1)
    two = jnp.where(place >= 2, from_behind(ids, "ctx", 2), -1)
    return jnp.concatenate([two[:, tok_len - LEAD :], one, ids], axis=1)


def norm_kernel(rows_ref, gain_ref, normed_ref):
    values = rows_ref[...].astype(jnp.float32)
    inverse_rms = lax.rsqrt(jnp.mean(values * values, axis=-1, keepdims=True) + 1e-06)
    normed_ref[...] = (values * inverse_rms * gain_ref[...]).astype(jnp.bfloat16)


def normalize(embedding, norm_gain):
    vocab, width = embedding.shape
    rows = pl.BlockSpec((vocab // 4, width), lambda i: (i, 0))
    return pl.pallas_call(
        norm_kernel,
        grid=(4,),
        in_specs=[rows, pl.BlockSpec((1, width), lambda i: (0, 0))],
        out_specs=rows,
        out_shape=jax.ShapeDtypeStruct((vocab, width), jnp.bfloat16),
        compiler_params=params(),
        cost_estimate=cost(0, 2_000_000),
    )(embedding, norm_gain.reshape(1, width))


def table_kernel(normed_ref, weight_ref, out_ref):
    out_ref[0] = jnp.dot(normed_ref[...], weight_ref[0], preferred_element_type=jnp.float32).astype(jnp.bfloat16)


def project(normed, in_proj):
    vocab, width = normed.shape
    count, _, panel_width = in_proj.shape
    cols = min(256, panel_width)
    per = panel_width // cols
    return pl.pallas_call(
        table_kernel,
        grid=(count * per,),
        in_specs=[
            whole(normed),
            pl.BlockSpec((1, width, cols), lambda s: (s // per, 0, s % per)),
        ],
        out_specs=pl.BlockSpec((1, vocab, cols), lambda s: (s // per, 0, s % per)),
        out_shape=jax.ShapeDtypeStruct((count, vocab, panel_width), jnp.bfloat16),
        compiler_params=params(),
        cost_estimate=cost(3_000_000_000, 0),
    )(normed, in_proj)


def mixer_kernel(ids_ref, table_ref, short_ref, toeplitz, gated_ref, held_query, held):
    tok_len, panel_width = gated_ref.shape[1:]
    vocab = table_ref.shape[1]
    rows = ids_ref.shape[2]
    reach = 2 * tok_len
    lead = rows - reach
    tiles = panel_width // LANES
    per_tile = LANES // GROUP
    names = lax.broadcasted_iota(jnp.int32, (vocab, rows), 0)
    lane_group = lax.broadcasted_iota(jnp.int32, (tok_len, 2 * LANES), 1) % LANES // GROUP

    def look_up(one_hot, table):
        found = lax.dot_general(one_hot, table, (((0,), (0,)), ((), ())), preferred_element_type=jnp.float32)
        return found.astype(jnp.bfloat16).astype(jnp.float32)

    for v in range(2):
        one_hot = (names == ids_ref[v]).astype(jnp.float32).astype(jnp.bfloat16)
        held[v, 0] = look_up(one_hot, table_ref[1])
        held[v, 1] = look_up(one_hot, table_ref[2])
        held_query[v] = look_up(one_hot[:, rows - lead - tok_len :], table_ref[0])

    def featured(source, i, count, cols):
        total = short_ref[0, i : i + 1, cols] * source[pl.ds(lead, count), cols]
        for j in range(1, SHORT):
            total += short_ref[j, i : i + 1, cols] * source[pl.ds(lead - j, count), cols]
        return total

    for tile in range(tiles):
        cols = slice(tile * LANES, (tile + 1) * LANES)
        products = []
        for v in range(2):
            key = featured(held.at[v, 0], 1, reach, cols)
            value = featured(held.at[v, 1], 2, reach, cols)
            products.append((key * value).astype(jnp.bfloat16))
        both = jnp.concatenate(products, axis=1)
        filtered = None
        for k in range(per_tile):
            one = jnp.dot(
                toeplitz[tile, pl.ds(k * tok_len, tok_len), :], both, preferred_element_type=jnp.float32
            )
            filtered = one if k == 0 else jnp.where(lane_group == k, one, filtered)
        for v in range(2):
            query = featured(held_query.at[v], 0, tok_len, cols)
            gated_ref[v, :, cols] = (query * filtered[:, v * LANES : (v + 1) * LANES]).astype(jnp.bfloat16)


def mix(ids, table, short_taps, toeplitz, tok_len):
    windows, rows = ids.shape
    panel_width = table.shape[2]
    return pl.pallas_call(
        mixer_kernel,
        grid=(windows // 2,),
        in_specs=[pl.BlockSpec((2, 1, rows), lambda p: (p, 0, 0))]
        + [whole(array) for array in (table, short_taps, toeplitz)],
        out_specs=pl.BlockSpec((2, tok_len, panel_width), lambda p: (p, 0, 0)),
        out_shape=jax.ShapeDtypeStruct((windows, tok_len, panel_width), jnp.bfloat16),
        scratch_shapes=[
            pltpu.VMEM((2, LEAD + tok_len, panel_width), jnp.float32),
            pltpu.VMEM((2, 2, rows, panel_width), jnp.float32),
        ],
        compiler_params=params(),
        cost_estimate=cost(1_500_000_000, 0),
    )(ids.reshape(windows, 1, rows), table, short_taps, toeplitz)


def prepare_kernel(place_ref, base_ref, *refs):
    count = len(refs) // 2
    for source, piece in zip(refs[:count], refs[count:]):
        piece[...] = source[...]
    toeplitz_ref = refs[-1]
    tiles, stacked, reach = toeplitz_ref.shape
    per_tile = base_ref.shape[0] // tiles
    tok_len = stacked // per_tile
    for tile in range(tiles):
        for k in range(per_tile):
            g = tile * per_tile + k
            wide = jnp.broadcast_to(base_ref[g : g + 1, :], (tok_len, reach))
            shifted = pltpu.roll(wide, 0, 1, stride=1, stride_axis=0)
            toeplitz_ref[tile, pl.ds(k * tok_len, tok_len), :] = shifted.astype(jnp.bfloat16)


def prepare(place, out_proj, conv_taps, tok_len):
    depth, width = out_proj.shape
    unit = width // SIXTEENTHS
    reach = 2 * tok_len
    per_tile = LANES // GROUP
    tiles = conv_taps.shape[0] // per_tile
    base = jnp.pad(conv_taps[:, ::-1].astype(jnp.float32), ((0, 0), (1, reach - TAPS - 1)))
    ins, outs, shapes = [pl.BlockSpec(base.shape, lambda s, place: (0, 0))], [], []
    for first, extent, sharers, _ in SPLITS:
        cols = extent * unit // sharers
        start = first * unit // cols
        ins.append(pl.BlockSpec((depth, cols), lambda s, place, start=start, n=sharers: (0, start + place[0] % n)))
        outs.append(pl.BlockSpec((depth, cols), lambda s, place: (0, 0)))
        shapes.append(jax.ShapeDtypeStruct((depth, cols), out_proj.dtype))
    shapes.append(jax.ShapeDtypeStruct((tiles, per_tile * tok_len, reach), jnp.bfloat16))
    outs.append(pl.BlockSpec(shapes[-1].shape, lambda s, place: (0, 0, 0)))
    return pl.pallas_call(
        prepare_kernel,
        grid_spec=pltpu.PrefetchScalarGridSpec(num_scalar_prefetch=1, grid=(1,), in_specs=ins, out_specs=outs),
        out_shape=shapes,
        compiler_params=params(),
        cost_estimate=cost(0, 2_000_000),
    )(place, base, *[out_proj] * len(SPLITS))


def panel_kernel(place_ref, mine_ref, other_ref, *refs):
    out_ref = refs[-1]
    count, sharers, tok_len, _ = out_ref.shape
    beside = [ref.at[i] for ref in refs[sharers:-1] for i in range(ref.shape[0])]
    for k in range(sharers):
        total = jnp.dot(mine_ref[...], refs[k][...], preferred_element_type=jnp.float32)
        total += jnp.dot(other_ref[...], beside[k][...], preferred_element_type=jnp.float32)
        for w in range(count):
            out_ref[w, k] = total[w * tok_len : (w + 1) * tok_len].astype(out_ref.dtype)


def panel(place, mine, other, out_proj, beside, split, step):
    count, tok_len, depth = mine.shape
    rows = count * tok_len
    unit = out_proj.shape[1] // SIXTEENTHS
    base, extent, sharers, _ = split
    piece_cols = extent * unit // sharers
    offset, cols = (part * unit // sharers for part in step)
    order = range(sharers)
    fixed = lambda shape: pl.BlockSpec(shape, lambda s, place: (0,) * len(shape))

    def own(k):
        start, per = (base * unit + offset) // cols, piece_cols // cols
        return pl.BlockSpec((depth, cols), lambda s, place: (0, start + (place[0] % sharers ^ k) * per))

    near = lambda a: pl.BlockSpec((a.shape[0], depth, cols), lambda s, place: (0, 0, offset // cols))
    return pl.pallas_call(
        panel_kernel,
        grid_spec=pltpu.PrefetchScalarGridSpec(
            num_scalar_prefetch=1,
            grid=(1,),
            in_specs=[fixed((rows, depth))] * 2 + [own(k) for k in order] + [near(a) for a in beside],
            out_specs=fixed((count, sharers, tok_len, cols)),
        ),
        out_shape=jax.ShapeDtypeStruct((count, sharers, tok_len, cols), jnp.bfloat16),
        compiler_params=params(),
        cost_estimate=cost(400_000_000, 0),
    )(place, mine.reshape(rows, depth), other.reshape(rows, depth), *[out_proj] * sharers, *beside)


def residual_kernel(ids_ref, rows_ref, out_ref):
    names = lax.broadcasted_iota(jnp.int32, (rows_ref.shape[0], ids_ref.shape[1]), 0)
    one_hot = (names == ids_ref[...]).astype(jnp.float32).astype(jnp.bfloat16)
    out_ref[...] = lax.dot_general(
        one_hot, rows_ref[...], (((0,), (0,)), ((), ())), preferred_element_type=jnp.float32
    ).astype(jnp.bfloat16)


def residual(token_ids, embedding):
    vocab, width = embedding.shape
    tok_len = token_ids.shape[1]
    cols = width // 4
    return pl.pallas_call(
        residual_kernel,
        grid=(4,),
        in_specs=[whole(token_ids), pl.BlockSpec((vocab, cols), lambda i: (0, i))],
        out_specs=pl.BlockSpec((tok_len, cols), lambda i: (0, i)),
        out_shape=jax.ShapeDtypeStruct((tok_len, width), jnp.bfloat16),
        compiler_params=params(),
        cost_estimate=cost(400_000_000, 0),
    )(token_ids, embedding)


def place_kernel(split, step, place_ref, so_far_ref, near_ref, far_ref, out_ref):
    _, sharers, _, cols = near_ref.shape
    piece_cols = so_far_ref.shape[1] // sharers
    offset = step[0] * cols // step[1]
    out_ref[...] = so_far_ref[...]
    for k in range(sharers):
        first = (place_ref[0] % sharers ^ k) * piece_cols + offset
        total = near_ref[0, k].astype(jnp.float32) + far_ref[0, k].astype(jnp.float32)
        at = pl.ds(pl.multiple_of(first, LANES), cols)
        out_ref[:, at] = (so_far_ref[:, at].astype(jnp.float32) + total).astype(jnp.bfloat16)


def place_pieces(place, so_far, near, far, split, step):
    tok_len, width = so_far.shape
    base, extent, _, _ = split
    part = pl.BlockSpec((tok_len, extent * width // SIXTEENTHS), lambda s, place: (0, base // extent))
    one = pl.BlockSpec(near.shape, lambda s, place: (0, 0, 0, 0))
    return pl.pallas_call(
        functools.partial(place_kernel, split, step),
        grid_spec=pltpu.PrefetchScalarGridSpec(
            num_scalar_prefetch=1, grid=(1,), in_specs=[part, one, one], out_specs=part
        ),
        out_shape=jax.ShapeDtypeStruct(so_far.shape, so_far.dtype),
        input_output_aliases={1: 0},
        compiler_params=params(),
        cost_estimate=cost(0, 1_000_000),
    )(place, so_far, near, far)


def add(a, b):
    return (a.astype(jnp.float32) + b.astype(jnp.float32)).astype(jnp.bfloat16)


def per_device(token_ids, embedding, norm_gain, in_proj, short_taps, conv_taps, out_proj):
    tok_len = token_ids.shape[1]
    at = lax.axis_index("ctx").reshape(1).astype(jnp.int32)
    bits = exchange_bits()
    tie = lax.optimization_barrier

    *pieces, toeplitz = prepare(at, out_proj, conv_taps, tok_len)
    ids = level_ids(token_ids, bits[:2])
    ids, embedding_then, toeplitz = tie((ids, embedding, toeplitz))
    normed = normalize(embedding_then, norm_gain)
    for group in [bits[i : i + 2] for i in range(2, len(bits), 2)]:
        ids = level_ids(ids, group)
    normed, ids = tie((normed, ids))
    ids = with_lead(ids)
    table = project(normed, in_proj)
    pieces[:2] = [swap(piece, "fsdp", bits[-2]) for piece in pieces[:2]]
    table, pieces[0], pieces[2:] = tie((table, pieces[0], pieces[2:]))
    pieces[2:] = [swap(piece, "fsdp", bits[-2]) for piece in pieces[2:]]

    half = ids.shape[0] // 2
    mine, other = [], []
    for first in (half, 0):
        if first == 0:
            ids, pieces[1], mine[0] = tie((ids, pieces[1], mine[0]))
        gated = mix(ids[first : first + half], table, short_taps, toeplitz, tok_len)
        mine.append(gated[: half // 2])
        other.append(swap(gated[half // 2 :], "fsdp", bits[-2]) if first else None)

    def spread(piece):
        pair = jnp.concatenate([piece[None], swap(piece, "ctx", 1)[None]], axis=0)
        return pair, swap(pair, "ctx", 2)

    other[0], gated = tie((other[0], gated))
    other[1] = swap(gated[half // 2 :], "fsdp", bits[-2])
    beside = [(pieces[0][None], swap(pieces[0], "ctx", 1)[None]), spread(pieces[1])]
    steps = [(split, number, step) for number, split in enumerate(SPLITS) for step in split[3]]

    def send(number, then):
        split, shared, step = steps[number]
        ready, _ = tie((mine[0], then))
        return panel(at, ready, other[0], out_proj, beside[shared], split, step)

    away = [send(0, other[0]), send(1, other[0])]
    own_ids, other[1], away[1] = tie((token_ids, other[1], away[1]))
    out = residual(own_ids, embedding)
    behind = []
    for number, (split, shared, step) in enumerate(steps):
        got = swap(away[number], "fsdp", bits[-1])
        if number >= 2:
            out = place_pieces(at, out, *behind[number - 2])
            got, out = tie((got, out))
        total = panel(at, mine[1], other[1], out_proj, beside[shared], split, step)
        for bit in reversed(bits[:-2]):
            half = total.shape[0] // 2
            far = add(total[half:], got[half:])
            total, got = add(total[:half], got[:half]), swap(far, "fsdp", bit)
        behind.append((total, got, split, step))
        if number == 0:
            last, _ = tie((pieces[2], total))
            beside.append((last[None], swap(last, "ctx", 1)[None]))
        if number + 2 < len(steps):
            away.append(send(number + 2, total if number == 0 else (total, behind[number - 1][1])))
    behind = behind[-2:]
    for last in behind:
        out = place_pieces(at, out, *last)
    return out[None]


def solution(mesh):
    return jax.shard_map(
        per_device,
        mesh=mesh,
        in_specs=(
            P("fsdp", "ctx"),
            P(),
            P(),
            P(None, None, "fsdp"),
            P(None, None, "fsdp"),
            P("fsdp", None),
            P("fsdp", None),
        ),
        out_specs=P("fsdp", "ctx", None),
        check_vma=False,
    )
```

```python
import functools

import jax
import jax.numpy as jnp
from jax import lax
from jax.experimental import pallas as pl
from jax.experimental.pallas import tpu as pltpu
from jax.sharding import PartitionSpec as P

GROUP = 16
TAPS = 128
SHORT = 3
LANES = 128
LEAD = 16
SPLITS = ((0, 4, 2, ((0, 4),)), (4, 4, 4, ((0, 4),)), (8, 8, 4, ((0, 4), (4, 4))))
SIXTEENTHS = 16
ORDER = {2: (0, 1), 4: (0, 2, 1, 3)}


def from_behind(x, axis, by):
    peers = lax.axis_size(axis)
    return lax.ppermute(x, axis, [(i, i + by) for i in range(peers) if i + by < peers])


def swap(x, axis, mask):
    peers = lax.axis_size(axis)
    return lax.ppermute(x, axis, [(i, i ^ mask) for i in range(peers)])


def exchange_bits():
    peers = lax.axis_size("fsdp")
    return [1 << b for b in reversed(range(peers.bit_length() - 1))]


def params(mib=24):
    return pltpu.CompilerParams(vmem_limit_bytes=mib * 1024 * 1024)


def cost(flops, bytes_accessed):
    return pl.CostEstimate(flops=flops, bytes_accessed=bytes_accessed, transcendentals=0)


def whole(array):
    return pl.BlockSpec(array.shape, lambda *_: (0,) * len(array.shape))


def level_ids(ids, group):
    masks = [0]
    for bit in group:
        masks += [mask | bit for mask in masks]
    return jnp.concatenate([ids] + [swap(ids, "fsdp", mask) for mask in masks[1:]], axis=0)


def with_lead(ids):
    tok_len = ids.shape[1]
    place = lax.axis_index("ctx")
    one = jnp.where(place >= 1, from_behind(ids, "ctx", 1), -1)
    two = jnp.where(place >= 2, from_behind(ids, "ctx", 2), -1)
    return jnp.concatenate([two[:, tok_len - LEAD :], one, ids], axis=1)


def norm_kernel(rows_ref, gain_ref, normed_ref):
    values = rows_ref[...].astype(jnp.float32)
    inverse_rms = lax.rsqrt(jnp.mean(values * values, axis=-1, keepdims=True) + 1e-06)
    normed_ref[...] = (values * inverse_rms * gain_ref[...]).astype(jnp.bfloat16)


def normalize(embedding, norm_gain):
    vocab, width = embedding.shape
    rows = pl.BlockSpec((vocab // 4, width), lambda i: (i, 0))
    return pl.pallas_call(
        norm_kernel,
        grid=(4,),
        in_specs=[rows, pl.BlockSpec((1, width), lambda i: (0, 0))],
        out_specs=rows,
        out_shape=jax.ShapeDtypeStruct((vocab, width), jnp.bfloat16),
        compiler_params=params(60),
        cost_estimate=cost(0, 2_000_000),
    )(embedding, norm_gain.reshape(1, width))


def table_kernel(normed_ref, weight_ref, out_ref, total_ref):
    part = jnp.dot(normed_ref[...], weight_ref[0], preferred_element_type=jnp.float32)
    step, last = pl.program_id(1), pl.num_programs(1) - 1

    @pl.when(step == 0)
    def _():
        total_ref[...] = part

    @pl.when((step > 0) & (step < last))
    def _():
        total_ref[...] += part

    @pl.when(step == last)
    def _():
        out_ref[0] = (total_ref[...] + part).astype(jnp.bfloat16)


def project(normed, in_proj):
    vocab, width = normed.shape
    count, _, panel_width = in_proj.shape
    deep = width // 4
    return pl.pallas_call(
        table_kernel,
        grid=(count, width // deep),
        in_specs=[
            pl.BlockSpec((vocab, deep), lambda i, k: (0, k)),
            pl.BlockSpec((1, deep, panel_width), lambda i, k: (i, k, 0)),
        ],
        out_specs=pl.BlockSpec((1, vocab, panel_width), lambda i, k: (i, 0, 0)),
        out_shape=jax.ShapeDtypeStruct((count, vocab, panel_width), jnp.bfloat16),
        scratch_shapes=[pltpu.VMEM((vocab, panel_width), jnp.float32)],
        compiler_params=params(60),
        cost_estimate=cost(3_000_000_000, 0),
    )(normed, in_proj)


def mixer_kernel(ids_ref, table_ref, short_ref, toeplitz, gated_ref, held_query, held):
    tok_len, panel_width = gated_ref.shape[1:]
    vocab = table_ref.shape[1]
    rows = ids_ref.shape[2]
    reach = 2 * tok_len
    lead = rows - reach
    tiles = panel_width // LANES
    per_tile = LANES // GROUP
    names = lax.broadcasted_iota(jnp.int32, (vocab, rows), 0)
    lane_group = lax.broadcasted_iota(jnp.int32, (tok_len, 2 * LANES), 1) % LANES // GROUP

    def look_up(one_hot, table):
        found = lax.dot_general(one_hot, table, (((0,), (0,)), ((), ())), preferred_element_type=jnp.float32)
        return found.astype(jnp.bfloat16).astype(jnp.float32)

    for v in range(2):
        one_hot = (names == ids_ref[v]).astype(jnp.float32).astype(jnp.bfloat16)
        held[v, 0] = look_up(one_hot, table_ref[1])
        held[v, 1] = look_up(one_hot, table_ref[2])
        held_query[v] = look_up(one_hot[:, rows - lead - tok_len :], table_ref[0])

    def featured(source, i, count, cols):
        total = short_ref[0, i : i + 1, cols] * source[pl.ds(lead, count), cols]
        for j in range(1, SHORT):
            total += short_ref[j, i : i + 1, cols] * source[pl.ds(lead - j, count), cols]
        return total

    for tile in range(tiles):
        cols = slice(tile * LANES, (tile + 1) * LANES)
        products = []
        for v in range(2):
            key = featured(held.at[v, 0], 1, reach, cols)
            value = featured(held.at[v, 1], 2, reach, cols)
            products.append((key * value).astype(jnp.bfloat16))
        both = jnp.concatenate(products, axis=1)
        filtered = None
        for k in range(per_tile):
            one = jnp.dot(
                toeplitz[tile, pl.ds(k * tok_len, tok_len), :], both, preferred_element_type=jnp.float32
            )
            filtered = one if k == 0 else jnp.where(lane_group == k, one, filtered)
        for v in range(2):
            query = featured(held_query.at[v], 0, tok_len, cols)
            gated_ref[v, :, cols] = (query * filtered[:, v * LANES : (v + 1) * LANES]).astype(jnp.bfloat16)


def mix(ids, table, short_taps, toeplitz, tok_len):
    windows, rows = ids.shape
    panel_width = table.shape[2]
    return pl.pallas_call(
        mixer_kernel,
        grid=(windows // 2,),
        in_specs=[pl.BlockSpec((2, 1, rows), lambda p: (p, 0, 0))]
        + [whole(array) for array in (table, short_taps, toeplitz)],
        out_specs=pl.BlockSpec((2, tok_len, panel_width), lambda p: (p, 0, 0)),
        out_shape=jax.ShapeDtypeStruct((windows, tok_len, panel_width), jnp.bfloat16),
        scratch_shapes=[
            pltpu.VMEM((2, LEAD + tok_len, panel_width), jnp.float32),
            pltpu.VMEM((2, 2, rows, panel_width), jnp.float32),
        ],
        compiler_params=params(),
        cost_estimate=cost(1_500_000_000, 0),
    )(ids.reshape(windows, 1, rows), table, short_taps, toeplitz)


def cut_kernel(place_ref, *refs):
    count = len(refs) // 2
    for source, piece in zip(refs[:count], refs[count:]):
        piece[...] = source[...]


def cut_pieces(place, out_proj):
    depth, width = out_proj.shape
    unit = width // SIXTEENTHS
    ins, outs, shapes = [], [], []
    for first, extent, sharers, _ in SPLITS:
        cols = extent * unit // sharers
        start = first * unit // cols
        ins.append(pl.BlockSpec((depth, cols), lambda s, place, start=start, n=sharers: (0, start + place[0] % n)))
        outs.append(pl.BlockSpec((depth, cols), lambda s, place: (0, 0)))
        shapes.append(jax.ShapeDtypeStruct((depth, cols), out_proj.dtype))
    return pl.pallas_call(
        cut_kernel,
        grid_spec=pltpu.PrefetchScalarGridSpec(num_scalar_prefetch=1, grid=(1,), in_specs=ins, out_specs=outs),
        out_shape=shapes,
        compiler_params=params(60),
        cost_estimate=cost(0, 2_000_000),
    )(place, *[out_proj] * len(SPLITS))


def toeplitz_kernel(base_ref, toeplitz_ref):
    tiles, stacked, reach = toeplitz_ref.shape
    per_tile = base_ref.shape[0] // tiles
    tok_len = stacked // per_tile
    for tile in range(tiles):
        for k in range(per_tile):
            g = tile * per_tile + k
            wide = jnp.broadcast_to(base_ref[g : g + 1, :], (tok_len, reach))
            shifted = pltpu.roll(wide, 0, 1, stride=1, stride_axis=0)
            toeplitz_ref[tile, pl.ds(k * tok_len, tok_len), :] = shifted.astype(jnp.bfloat16)


def build_toeplitz(conv_taps, tok_len):
    reach = 2 * tok_len
    per_tile = LANES // GROUP
    tiles = conv_taps.shape[0] // per_tile
    base = jnp.pad(conv_taps[:, ::-1].astype(jnp.float32), ((0, 0), (1, reach - TAPS - 1)))
    shape = jax.ShapeDtypeStruct((tiles, per_tile * tok_len, reach), jnp.bfloat16)
    return pl.pallas_call(
        toeplitz_kernel,
        grid=(1,),
        in_specs=[whole(base)],
        out_specs=whole(shape),
        out_shape=shape,
        compiler_params=params(60),
        cost_estimate=cost(0, 2_000_000),
    )(base)


def panel_kernel(place_ref, mine_ref, other_ref, *refs):
    out_ref = refs[-1]
    count, sharers, tok_len, _ = out_ref.shape
    beside = [ref.at[i] for ref in refs[sharers:-1] for i in range(ref.shape[0])]
    for k in range(sharers):
        total = jnp.dot(mine_ref[...], refs[k][...], preferred_element_type=jnp.float32)
        total += jnp.dot(other_ref[...], beside[k][...], preferred_element_type=jnp.float32)
        for w in range(count):
            out_ref[w, k] = total[w * tok_len : (w + 1) * tok_len].astype(out_ref.dtype)


def panel(place, mine, other, out_proj, beside, split, step):
    count, tok_len, depth = mine.shape
    rows = count * tok_len
    unit = out_proj.shape[1] // SIXTEENTHS
    base, extent, sharers, _ = split
    piece_cols = extent * unit // sharers
    offset, cols = (part * unit // sharers for part in step)
    order = ORDER[sharers]
    fixed = lambda shape: pl.BlockSpec(shape, lambda s, place: (0,) * len(shape))

    def own(k):
        start, per = (base * unit + offset) // cols, piece_cols // cols
        return pl.BlockSpec((depth, cols), lambda s, place: (0, start + (place[0] % sharers ^ k) * per))

    near = lambda a: pl.BlockSpec((a.shape[0], depth, cols), lambda s, place: (0, 0, offset // cols))
    return pl.pallas_call(
        panel_kernel,
        grid_spec=pltpu.PrefetchScalarGridSpec(
            num_scalar_prefetch=1,
            grid=(1,),
            in_specs=[fixed((rows, depth))] * 2 + [own(k) for k in order] + [near(a) for a in beside],
            out_specs=fixed((count, sharers, tok_len, cols)),
        ),
        out_shape=jax.ShapeDtypeStruct((count, sharers, tok_len, cols), jnp.bfloat16),
        compiler_params=params(),
        cost_estimate=cost(400_000_000, 0),
    )(place, mine.reshape(rows, depth), other.reshape(rows, depth), *[out_proj] * sharers, *beside)


def residual_kernel(ids_ref, rows_ref, out_ref):
    names = lax.broadcasted_iota(jnp.int32, (rows_ref.shape[0], ids_ref.shape[1]), 0)
    one_hot = (names == ids_ref[...]).astype(jnp.float32).astype(jnp.bfloat16)
    out_ref[...] = lax.dot_general(
        one_hot, rows_ref[...], (((0,), (0,)), ((), ())), preferred_element_type=jnp.float32
    ).astype(jnp.bfloat16)


def residual(token_ids, embedding):
    vocab, width = embedding.shape
    tok_len = token_ids.shape[1]
    cols = width // 4
    return pl.pallas_call(
        residual_kernel,
        grid=(4,),
        in_specs=[whole(token_ids), pl.BlockSpec((vocab, cols), lambda i: (0, i))],
        out_specs=pl.BlockSpec((tok_len, cols), lambda i: (0, i)),
        out_shape=jax.ShapeDtypeStruct((tok_len, width), jnp.bfloat16),
        compiler_params=params(),
        cost_estimate=cost(400_000_000, 0),
    )(token_ids, embedding)


def place_kernel(split, step, place_ref, so_far_ref, near_ref, far_ref, out_ref):
    _, sharers, _, cols = near_ref.shape
    piece_cols = so_far_ref.shape[1] // sharers
    offset = step[0] * cols // step[1]
    out_ref[...] = so_far_ref[...]
    for i, k in enumerate(ORDER[sharers]):
        first = (place_ref[0] % sharers ^ k) * piece_cols + offset
        total = near_ref[0, i].astype(jnp.float32) + far_ref[0, i].astype(jnp.float32)
        at = pl.ds(pl.multiple_of(first, LANES), cols)
        out_ref[:, at] = (so_far_ref[:, at].astype(jnp.float32) + total).astype(jnp.bfloat16)


def place_pieces(place, so_far, near, far, split, step):
    tok_len, width = so_far.shape
    base, extent, _, _ = split
    part = pl.BlockSpec((tok_len, extent * width // SIXTEENTHS), lambda s, place: (0, base // extent))
    one = pl.BlockSpec(near.shape, lambda s, place: (0, 0, 0, 0))
    return pl.pallas_call(
        functools.partial(place_kernel, split, step),
        grid_spec=pltpu.PrefetchScalarGridSpec(
            num_scalar_prefetch=1, grid=(1,), in_specs=[part, one, one], out_specs=part
        ),
        out_shape=jax.ShapeDtypeStruct(so_far.shape, so_far.dtype),
        input_output_aliases={1: 0},
        compiler_params=params(),
        cost_estimate=cost(0, 1_000_000),
    )(place, so_far, near, far)


def add(a, b):
    return (a.astype(jnp.float32) + b.astype(jnp.float32)).astype(jnp.bfloat16)


def per_device(token_ids, embedding, norm_gain, in_proj, short_taps, conv_taps, out_proj):
    tok_len = token_ids.shape[1]
    at = lax.axis_index("ctx").reshape(1).astype(jnp.int32)
    bits = exchange_bits()
    tie = lax.optimization_barrier
    beside_bit = bits[-2]

    pieces = list(cut_pieces(at, out_proj))
    pieces[0], token_ids, conv_taps = tie((pieces[0], token_ids, conv_taps))
    toeplitz = build_toeplitz(conv_taps, tok_len)
    ids = level_ids(token_ids, bits[:2])
    ids, embedding_then, toeplitz = tie((ids, embedding, toeplitz))
    normed = normalize(embedding_then, norm_gain)
    for group in [bits[i : i + 2] for i in range(2, len(bits), 2)]:
        ids = level_ids(ids, group)
    normed, ids = tie((normed, ids))
    ids = with_lead(ids)
    table = project(normed, in_proj)
    pieces = [swap(piece, "fsdp", beside_bit) for piece in pieces]
    table, pieces[:2] = tie((table, pieces[:2]))
    across = [None, swap(pieces[1], "ctx", 2)]

    half = ids.shape[0] // 2
    gated = mix(ids[half:], table, short_taps, toeplitz, tok_len)
    near = swap(pieces[0], "ctx", 1)
    ids, gated, near = tie((ids, gated, near))
    mine = [gated[: half // 2]]
    other = [swap(gated[half // 2 :], "fsdp", beside_bit)]
    gated = mix(ids[:half], table, short_taps, toeplitz, tok_len)
    pieces[2], across[1], other[0], gated = tie((pieces[2], across[1], other[0], gated))
    mine.append(gated[: half // 2])
    other.append(swap(gated[half // 2 :], "fsdp", beside_bit))

    second = jnp.stack([pieces[1], across[1]])
    third = jnp.stack([pieces[2], swap(pieces[2], "ctx", 2)])
    beside = [(pieces[0][None], near[None]), (second, swap(second, "ctx", 1)), None]
    other[0], beside[1] = tie((other[0], beside[1]))
    steps = [(split, number, step) for number, split in enumerate(SPLITS) for step in split[3]]
    away = [panel(at, mine[0], other[0], out_proj, beside[n], split, step) for split, n, step in steps[:2]]
    own_ids, other[1], away[1] = tie((token_ids, other[1], away[1]))
    out = residual(own_ids, embedding)
    own = [panel(at, mine[1], other[1], out_proj, beside[n], split, step) for split, n, step in steps[:2]]
    arrived = [swap(away[0], "fsdp", bits[-1]), None]
    third, arrived[0], own[0] = tie((third, arrived[0], own[0]))
    beside[2] = (third, swap(third, "ctx", 1))
    arrived[1] = swap(away[1], "fsdp", bits[-1])
    away += [panel(at, mine[0], other[0], out_proj, beside[n], split, step) for split, n, step in steps[2:3]]
    own += [panel(at, mine[1], other[1], out_proj, beside[n], split, step) for split, n, step in steps[2:]]

    arrived.append(swap(away[2], "fsdp", bits[-1]))
    behind = []
    for number, (split, _, step) in enumerate(steps):
        got, total = arrived[number], own[number]
        if number >= 2:
            out = place_pieces(at, out, *behind[number - 2])
            got, out = tie((got, out))
        for bit in reversed(bits[:-2]):
            half = total.shape[0] // 2
            far = add(total[half:], got[half:])
            total, got = add(total[:half], got[:half]), swap(far, "fsdp", bit)
        behind.append((total, got, split, step))
        if number + 3 < len(steps):
            split, n, step = steps[number + 3]
            ready, _ = tie((mine[0], got))
            arrived.append(swap(panel(at, ready, other[0], out_proj, beside[n], split, step), "fsdp", bits[-1]))
    for last in behind[-2:]:
        out = place_pieces(at, out, *last)
    return out[None]


def solution(mesh):
    return jax.shard_map(
        per_device,
        mesh=mesh,
        in_specs=(
            P("fsdp", "ctx"),
            P(),
            P(),
            P(None, None, "fsdp"),
            P(None, None, "fsdp"),
            P("fsdp", None),
            P("fsdp", None),
        ),
        out_specs=P("fsdp", "ctx", None),
        check_vma=False,
    )
```

```python
import functools

import jax
import jax.numpy as jnp
from jax import lax
from jax.experimental import pallas as pl
from jax.experimental.pallas import tpu as pltpu
from jax.sharding import PartitionSpec as P

GROUP = 16
TAPS = 128
SHORT = 3
LANES = 128
LEAD = 16
SPLITS = ((0, 8, 4, ((0, 4), (4, 4))), (8, 8, 4, ((0, 4), (4, 4))))
SIXTEENTHS = 16
ORDER = {2: (0, 1), 4: (0, 2, 1, 3)}


def from_behind(x, axis, by):
    peers = lax.axis_size(axis)
    return lax.ppermute(x, axis, [(i, i + by) for i in range(peers) if i + by < peers])


def swap(x, axis, mask):
    peers = lax.axis_size(axis)
    return lax.ppermute(x, axis, [(i, i ^ mask) for i in range(peers)])


def exchange_bits():
    peers = lax.axis_size("fsdp")
    return [1 << b for b in reversed(range(peers.bit_length() - 1))]


def params(mib=24):
    return pltpu.CompilerParams(vmem_limit_bytes=mib * 1024 * 1024)


def cost(flops, bytes_accessed):
    return pl.CostEstimate(flops=flops, bytes_accessed=bytes_accessed, transcendentals=0)


def whole(array):
    return pl.BlockSpec(array.shape, lambda *_: (0,) * len(array.shape))


def level_ids(ids, group):
    masks = [0]
    for bit in group:
        masks += [mask | bit for mask in masks]
    return jnp.concatenate([ids] + [swap(ids, "fsdp", mask) for mask in masks[1:]], axis=0)


def with_lead(ids):
    tok_len = ids.shape[1]
    place = lax.axis_index("ctx")
    one = jnp.where(place >= 1, from_behind(ids, "ctx", 1), -1)
    two = jnp.where(place >= 2, from_behind(ids, "ctx", 2), -1)
    return jnp.concatenate([two[:, tok_len - LEAD :], one, ids], axis=1)


def table_kernel(rows_hbm, weight_hbm, gain_ref, table_ref, rows, weight, row_sems, weight_sems):
    count, width, panel_width = weight.shape
    parts, blocks = row_sems.shape[0], weight_sems.shape[1]
    each, deep = rows.shape[0] // parts, width // blocks
    row_copies = [
        pltpu.make_async_copy(rows_hbm.at[pl.ds(r * each, each)], rows.at[pl.ds(r * each, each)], row_sems.at[r])
        for r in range(parts)
    ]
    weight_copies = [
        [
            pltpu.make_async_copy(
                weight_hbm.at[i, pl.ds(k * deep, deep)], weight.at[i, pl.ds(k * deep, deep)], weight_sems.at[i, k]
            )
            for k in range(blocks)
        ]
        for i in range(count)
    ]
    for copy in row_copies + sum(weight_copies, []):
        copy.start()
    for r in range(parts):
        row_copies[r].wait()
        at = pl.ds(r * each, each)
        values = rows[at, :].astype(jnp.float32)
        inverse_rms = lax.rsqrt(jnp.mean(values * values, axis=-1, keepdims=True) + 1e-06)
        rows[at, :] = (values * inverse_rms * gain_ref[...]).astype(jnp.bfloat16)
    cols = min(256, panel_width)
    for i in range(count):
        for copy in weight_copies[i]:
            copy.wait()
        for first in range(0, panel_width, cols):
            at = slice(first, first + cols)
            part = jnp.dot(rows[...], weight[i, :, at], preferred_element_type=jnp.float32)
            table_ref[i, :, at] = part.astype(jnp.bfloat16)


def project(embedding, norm_gain, in_proj):
    vocab, width = embedding.shape
    count, _, panel_width = in_proj.shape
    hbm = pl.BlockSpec(memory_space=pltpu.HBM)
    shape = jax.ShapeDtypeStruct((count, vocab, panel_width), jnp.bfloat16)
    return pl.pallas_call(
        table_kernel,
        grid=(1,),
        in_specs=[hbm, hbm, pl.BlockSpec((1, width), lambda s: (0, 0))],
        out_specs=whole(shape),
        out_shape=shape,
        scratch_shapes=[
            pltpu.VMEM(embedding.shape, jnp.bfloat16),
            pltpu.VMEM(in_proj.shape, jnp.bfloat16),
            pltpu.SemaphoreType.DMA((8,)),
            pltpu.SemaphoreType.DMA((count, 4)),
        ],
        compiler_params=params(40),
        cost_estimate=cost(3_000_000_000, 0),
    )(embedding, in_proj, norm_gain.reshape(1, width))


def mixer_kernel(ids_ref, table_ref, short_ref, toeplitz, gated_ref, held_query, held):
    tok_len, panel_width = gated_ref.shape[1:]
    vocab = table_ref.shape[1]
    rows = ids_ref.shape[2]
    reach = 2 * tok_len
    lead = rows - reach
    tiles = panel_width // LANES
    per_tile = LANES // GROUP
    names = lax.broadcasted_iota(jnp.int32, (vocab, rows), 0)
    lane_group = lax.broadcasted_iota(jnp.int32, (tok_len, 2 * LANES), 1) % LANES // GROUP

    def look_up(one_hot, table):
        found = lax.dot_general(one_hot, table, (((0,), (0,)), ((), ())), preferred_element_type=jnp.float32)
        return found.astype(jnp.bfloat16).astype(jnp.float32)

    for v in range(2):
        one_hot = (names == ids_ref[v]).astype(jnp.float32).astype(jnp.bfloat16)
        held[v, 0] = look_up(one_hot, table_ref[1])
        held[v, 1] = look_up(one_hot, table_ref[2])
        held_query[v] = look_up(one_hot[:, rows - lead - tok_len :], table_ref[0])

    def featured(source, i, count, cols):
        total = short_ref[0, i : i + 1, cols] * source[pl.ds(lead, count), cols]
        for j in range(1, SHORT):
            total += short_ref[j, i : i + 1, cols] * source[pl.ds(lead - j, count), cols]
        return total

    for tile in range(tiles):
        cols = slice(tile * LANES, (tile + 1) * LANES)
        products = []
        for v in range(2):
            key = featured(held.at[v, 0], 1, reach, cols)
            value = featured(held.at[v, 1], 2, reach, cols)
            products.append((key * value).astype(jnp.bfloat16))
        both = jnp.concatenate(products, axis=1)
        filtered = None
        for k in range(per_tile):
            one = jnp.dot(
                toeplitz[tile, pl.ds(k * tok_len, tok_len), :], both, preferred_element_type=jnp.float32
            )
            filtered = one if k == 0 else jnp.where(lane_group == k, one, filtered)
        for v in range(2):
            query = featured(held_query.at[v], 0, tok_len, cols)
            gated_ref[v, :, cols] = (query * filtered[:, v * LANES : (v + 1) * LANES]).astype(jnp.bfloat16)


def mix(ids, table, short_taps, toeplitz, tok_len):
    windows, rows = ids.shape
    panel_width = table.shape[2]
    return pl.pallas_call(
        mixer_kernel,
        grid=(windows // 2,),
        in_specs=[pl.BlockSpec((2, 1, rows), lambda p: (p, 0, 0))]
        + [whole(array) for array in (table, short_taps, toeplitz)],
        out_specs=pl.BlockSpec((2, tok_len, panel_width), lambda p: (p, 0, 0)),
        out_shape=jax.ShapeDtypeStruct((windows, tok_len, panel_width), jnp.bfloat16),
        scratch_shapes=[
            pltpu.VMEM((2, LEAD + tok_len, panel_width), jnp.float32),
            pltpu.VMEM((2, 2, rows, panel_width), jnp.float32),
        ],
        compiler_params=params(),
        cost_estimate=cost(1_500_000_000, 0),
    )(ids.reshape(windows, 1, rows), table, short_taps, toeplitz)


def cut_kernel(place_ref, source, *refs):
    pieces, sems = refs[:-1], refs[-1]
    unit = source.shape[1] // SIXTEENTHS
    copies = []
    for n, ((base, _, sharers, _), piece) in enumerate(zip(SPLITS, pieces)):
        cols = piece.shape[1]
        first = pl.multiple_of(base * unit + place_ref[0] % sharers * cols, LANES)
        copies.append(pltpu.make_async_copy(source.at[:, pl.ds(first, cols)], piece, sems.at[n]))
    for copy in copies:
        copy.start()
    for copy in copies:
        copy.wait()


def cut_pieces(place, out_proj):
    depth, width = out_proj.shape
    hbm = pl.BlockSpec(memory_space=pltpu.HBM)
    shapes = [
        jax.ShapeDtypeStruct((depth, extent * width // SIXTEENTHS // sharers), out_proj.dtype)
        for _, extent, sharers, _ in SPLITS
    ]
    return pl.pallas_call(
        cut_kernel,
        in_specs=[pl.BlockSpec(memory_space=pltpu.SMEM), hbm],
        out_specs=[hbm] * len(shapes),
        out_shape=shapes,
        scratch_shapes=[pltpu.SemaphoreType.DMA((len(shapes),))],
        cost_estimate=cost(0, 2_000_000),
    )(place, out_proj)


def toeplitz_kernel(base_ref, toeplitz_ref):
    tiles, stacked, reach = toeplitz_ref.shape
    per_tile = base_ref.shape[0] // tiles
    tok_len = stacked // per_tile
    for tile in range(tiles):
        for k in range(per_tile):
            g = tile * per_tile + k
            wide = jnp.broadcast_to(base_ref[g : g + 1, :], (tok_len, reach))
            shifted = pltpu.roll(wide, 0, 1, stride=1, stride_axis=0)
            toeplitz_ref[tile, pl.ds(k * tok_len, tok_len), :] = shifted.astype(jnp.bfloat16)


def build_toeplitz(conv_taps, tok_len):
    reach = 2 * tok_len
    per_tile = LANES // GROUP
    tiles = conv_taps.shape[0] // per_tile
    base = jnp.pad(conv_taps[:, ::-1].astype(jnp.float32), ((0, 0), (1, reach - TAPS - 1)))
    shape = jax.ShapeDtypeStruct((tiles, per_tile * tok_len, reach), jnp.bfloat16)
    return pl.pallas_call(
        toeplitz_kernel,
        grid=(1,),
        in_specs=[whole(base)],
        out_specs=whole(shape),
        out_shape=shape,
        compiler_params=params(8),
        cost_estimate=cost(0, 2_000_000),
    )(base)


def panel_kernel(place_ref, mine_ref, other_ref, *refs):
    out_ref = refs[-1]
    count, sharers, tok_len, _ = out_ref.shape
    beside = [ref.at[i] for ref in refs[sharers:-1] for i in range(ref.shape[0])]
    for k in range(sharers):
        total = jnp.dot(mine_ref[...], refs[k][...], preferred_element_type=jnp.float32)
        total += jnp.dot(other_ref[...], beside[k][...], preferred_element_type=jnp.float32)
        for w in range(count):
            out_ref[w, k] = total[w * tok_len : (w + 1) * tok_len].astype(out_ref.dtype)


def panel(place, mine, other, out_proj, beside, split, step):
    count, tok_len, depth = mine.shape
    rows = count * tok_len
    unit = out_proj.shape[1] // SIXTEENTHS
    base, extent, sharers, _ = split
    piece_cols = extent * unit // sharers
    offset, cols = (part * unit // sharers for part in step)
    order = ORDER[sharers]
    fixed = lambda shape: pl.BlockSpec(shape, lambda s, place: (0,) * len(shape))

    def own(k):
        start, per = (base * unit + offset) // cols, piece_cols // cols
        return pl.BlockSpec((depth, cols), lambda s, place: (0, start + (place[0] % sharers ^ k) * per))

    near = lambda a: pl.BlockSpec((a.shape[0], depth, cols), lambda s, place: (0, 0, offset // cols))
    return pl.pallas_call(
        panel_kernel,
        grid_spec=pltpu.PrefetchScalarGridSpec(
            num_scalar_prefetch=1,
            grid=(1,),
            in_specs=[fixed((rows, depth))] * 2 + [own(k) for k in order] + [near(a) for a in beside],
            out_specs=fixed((count, sharers, tok_len, cols)),
        ),
        out_shape=jax.ShapeDtypeStruct((count, sharers, tok_len, cols), jnp.bfloat16),
        compiler_params=params(),
        cost_estimate=cost(400_000_000, 0),
    )(place, mine.reshape(rows, depth), other.reshape(rows, depth), *[out_proj] * sharers, *beside)


def residual_kernel(ids_ref, rows_ref, out_ref):
    names = lax.broadcasted_iota(jnp.int32, (rows_ref.shape[0], ids_ref.shape[1]), 0)
    one_hot = (names == ids_ref[...]).astype(jnp.float32).astype(jnp.bfloat16)
    out_ref[...] = lax.dot_general(
        one_hot, rows_ref[...], (((0,), (0,)), ((), ())), preferred_element_type=jnp.float32
    ).astype(jnp.bfloat16)


def residual(token_ids, embedding):
    vocab, width = embedding.shape
    tok_len = token_ids.shape[1]
    cols = width // 4
    return pl.pallas_call(
        residual_kernel,
        grid=(4,),
        in_specs=[whole(token_ids), pl.BlockSpec((vocab, cols), lambda i: (0, i))],
        out_specs=pl.BlockSpec((tok_len, cols), lambda i: (0, i)),
        out_shape=jax.ShapeDtypeStruct((tok_len, width), jnp.bfloat16),
        compiler_params=params(),
        cost_estimate=cost(400_000_000, 0),
    )(token_ids, embedding)


def place_kernel(split, step, place_ref, so_far_ref, near_ref, far_ref, out_ref):
    _, sharers, _, cols = near_ref.shape
    piece_cols = so_far_ref.shape[1] // sharers
    offset = step[0] * cols // step[1]
    out_ref[...] = so_far_ref[...]
    for i, k in enumerate(ORDER[sharers]):
        first = (place_ref[0] % sharers ^ k) * piece_cols + offset
        total = near_ref[0, i].astype(jnp.float32) + far_ref[0, i].astype(jnp.float32)
        at = pl.ds(pl.multiple_of(first, LANES), cols)
        out_ref[:, at] = (so_far_ref[:, at].astype(jnp.float32) + total).astype(jnp.bfloat16)


def place_pieces(place, so_far, near, far, split, step):
    tok_len, width = so_far.shape
    base, extent, _, _ = split
    part = pl.BlockSpec((tok_len, extent * width // SIXTEENTHS), lambda s, place: (0, base // extent))
    one = pl.BlockSpec(near.shape, lambda s, place: (0, 0, 0, 0))
    return pl.pallas_call(
        functools.partial(place_kernel, split, step),
        grid_spec=pltpu.PrefetchScalarGridSpec(
            num_scalar_prefetch=1, grid=(1,), in_specs=[part, one, one], out_specs=part
        ),
        out_shape=jax.ShapeDtypeStruct(so_far.shape, so_far.dtype),
        input_output_aliases={1: 0},
        compiler_params=params(),
        cost_estimate=cost(0, 1_000_000),
    )(place, so_far, near, far)


def add(a, b):
    return (a.astype(jnp.float32) + b.astype(jnp.float32)).astype(jnp.bfloat16)


def per_device(token_ids, embedding, norm_gain, in_proj, short_taps, conv_taps, out_proj):
    tok_len = token_ids.shape[1]
    at = lax.axis_index("ctx").reshape(1).astype(jnp.int32)
    bits = exchange_bits()
    tie = lax.optimization_barrier
    beside_bit = bits[-2]

    early, late = cut_pieces(at, out_proj)
    early, late, token_ids, conv_taps = tie((early, late, token_ids, conv_taps))
    toeplitz = build_toeplitz(conv_taps, tok_len)
    ids = level_ids(token_ids, bits[:2])
    ids, toeplitz = tie((ids, toeplitz))
    for group in [bits[i : i + 2] for i in range(2, len(bits), 2)]:
        ids = level_ids(ids, group)
    early, late = swap(early, "fsdp", beside_bit), swap(late, "fsdp", beside_bit)
    ids, embedding_then, early = tie((ids, embedding, early))
    ids = with_lead(ids)
    early_across = swap(early, "ctx", 2)
    table = project(embedding_then, norm_gain, in_proj)
    table, late = tie((table, late))
    late_across = swap(late, "ctx", 2)

    half = ids.shape[0] // 2
    gated = mix(ids[half:], table, short_taps, toeplitz, tok_len)
    ids, gated, early, early_across = tie((ids, gated, early, early_across))
    pair = jnp.stack([early, early_across])
    beside = [(pair, swap(pair, "ctx", 1))]
    mine = [gated[: half // 2]]
    other = [swap(gated[half // 2 :], "fsdp", beside_bit)]
    gated = mix(ids[:half], table, short_taps, toeplitz, tok_len)
    late, late_across, other[0], gated = tie((late, late_across, other[0], gated))
    pair = jnp.stack([late, late_across])
    beside.append((pair, swap(pair, "ctx", 1)))
    mine.append(gated[: half // 2])
    other.append(swap(gated[half // 2 :], "fsdp", beside_bit))

    out = residual(token_ids, embedding)
    behind = []
    for split, shared in zip(SPLITS, beside):
        for step in split[3]:
            away = panel(at, mine[0], other[0], out_proj, shared, split, step)
            away, mine[0] = tie((away, mine[0]))
            got = swap(away, "fsdp", bits[-1])
            total = panel(at, mine[1], other[1], out_proj, shared, split, step)
            if not behind:
                total, out = tie((total, out))
            for bit in reversed(bits[:-2]):
                half = total.shape[0] // 2
                far = add(total[half:], got[half:])
                total, got = add(total[:half], got[:half]), swap(far, "fsdp", bit)
            behind.append((total, got, split, step))
    for last in behind:
        out = place_pieces(at, out, *last)
    return out[None]


def solution(mesh):
    return jax.shard_map(
        per_device,
        mesh=mesh,
        in_specs=(
            P("fsdp", "ctx"),
            P(),
            P(),
            P(None, None, "fsdp"),
            P(None, None, "fsdp"),
            P("fsdp", None),
            P("fsdp", None),
        ),
        out_specs=P("fsdp", "ctx", None),
        check_vma=False,
    )
```

```python
import functools

import jax
import jax.numpy as jnp
from jax import lax
from jax.experimental import pallas as pl
from jax.experimental.pallas import tpu as pltpu
from jax.sharding import PartitionSpec as P

GROUP = 16
TAPS = 128
SHORT = 3
LANES = 128
LEAD = 16
SPLITS = ((0, 8, (0, 2, 1, 3), ((0, 2), (2, 2), (4, 4))), (8, 8, (0, 1, 2, 3), ((0, 4), (4, 2), (6, 2))))
SIXTEENTHS = 16


def from_behind(x, axis, by):
    peers = lax.axis_size(axis)
    return lax.ppermute(x, axis, [(i, i + by) for i in range(peers) if i + by < peers])


def swap(x, axis, mask):
    peers = lax.axis_size(axis)
    return lax.ppermute(x, axis, [(i, i ^ mask) for i in range(peers)])


def exchange_bits():
    peers = lax.axis_size("fsdp")
    return [1 << b for b in reversed(range(peers.bit_length() - 1))]


def params(mib=24):
    return pltpu.CompilerParams(vmem_limit_bytes=mib * 1024 * 1024)


def cost(flops, bytes_accessed):
    return pl.CostEstimate(flops=flops, bytes_accessed=bytes_accessed, transcendentals=0)


def whole(array):
    return pl.BlockSpec(array.shape, lambda *_: (0,) * len(array.shape))


def level_ids(ids, group):
    masks = [0]
    for bit in group:
        masks += [mask | bit for mask in masks]
    return jnp.concatenate([ids] + [swap(ids, "fsdp", mask) for mask in masks[1:]], axis=0)


def with_lead(ids):
    tok_len = ids.shape[1]
    place = lax.axis_index("ctx")
    one = jnp.where(place >= 1, from_behind(ids, "ctx", 1), -1)
    two = jnp.where(place >= 2, from_behind(ids, "ctx", 2), -1)
    return jnp.concatenate([two[:, tok_len - LEAD :], one, ids], axis=1)


def table_kernel(rows_hbm, weight_hbm, gain_ref, table_ref, rows, weight, row_sems, weight_sems):
    count, width, panel_width = weight.shape
    parts, blocks = row_sems.shape[0], weight_sems.shape[1]
    each, deep = rows.shape[0] // parts, width // blocks
    row_copies = [
        pltpu.make_async_copy(rows_hbm.at[pl.ds(r * each, each)], rows.at[pl.ds(r * each, each)], row_sems.at[r])
        for r in range(parts)
    ]
    weight_copies = [
        [
            pltpu.make_async_copy(
                weight_hbm.at[i, pl.ds(k * deep, deep)], weight.at[i, pl.ds(k * deep, deep)], weight_sems.at[i, k]
            )
            for k in range(blocks)
        ]
        for i in range(count)
    ]
    for copy in row_copies + sum(weight_copies, []):
        copy.start()
    for r in range(parts):
        row_copies[r].wait()
        at = pl.ds(r * each, each)
        values = rows[at, :].astype(jnp.float32)
        inverse_rms = lax.rsqrt(jnp.mean(values * values, axis=-1, keepdims=True) + 1e-06)
        rows[at, :] = (values * inverse_rms * gain_ref[...]).astype(jnp.bfloat16)
    cols = min(256, panel_width)
    for i in range(count):
        for copy in weight_copies[i]:
            copy.wait()
        for first in range(0, panel_width, cols):
            at = slice(first, first + cols)
            part = jnp.dot(rows[...], weight[i, :, at], preferred_element_type=jnp.float32)
            table_ref[i, :, at] = part.astype(jnp.bfloat16)


def project(embedding, norm_gain, in_proj):
    vocab, width = embedding.shape
    count, _, panel_width = in_proj.shape
    hbm = pl.BlockSpec(memory_space=pltpu.HBM)
    shape = jax.ShapeDtypeStruct((count, vocab, panel_width), jnp.bfloat16)
    return pl.pallas_call(
        table_kernel,
        grid=(1,),
        in_specs=[hbm, hbm, pl.BlockSpec((1, width), lambda s: (0, 0))],
        out_specs=whole(shape),
        out_shape=shape,
        scratch_shapes=[
            pltpu.VMEM(embedding.shape, jnp.bfloat16),
            pltpu.VMEM(in_proj.shape, jnp.bfloat16),
            pltpu.SemaphoreType.DMA((8,)),
            pltpu.SemaphoreType.DMA((count, 4)),
        ],
        compiler_params=params(40),
        cost_estimate=cost(3_000_000_000, 0),
    )(embedding, in_proj, norm_gain.reshape(1, width))


def mixer_kernel(ids_ref, table_ref, short_ref, toeplitz, gated_ref, held_query, held):
    tok_len, panel_width = gated_ref.shape[1:]
    vocab = table_ref.shape[1]
    rows = ids_ref.shape[2]
    reach = 2 * tok_len
    lead = rows - reach
    tiles = panel_width // LANES
    per_tile = LANES // GROUP
    names = lax.broadcasted_iota(jnp.int32, (vocab, rows), 0)
    lane_group = lax.broadcasted_iota(jnp.int32, (tok_len, 2 * LANES), 1) % LANES // GROUP

    def look_up(one_hot, table):
        found = lax.dot_general(one_hot, table, (((0,), (0,)), ((), ())), preferred_element_type=jnp.float32)
        return found.astype(jnp.bfloat16).astype(jnp.float32)

    for v in range(2):
        one_hot = (names == ids_ref[v]).astype(jnp.float32).astype(jnp.bfloat16)
        held[v, 0] = look_up(one_hot, table_ref[1])
        held[v, 1] = look_up(one_hot, table_ref[2])
        held_query[v] = look_up(one_hot[:, rows - lead - tok_len :], table_ref[0])

    def featured(source, i, count, cols):
        total = short_ref[0, i : i + 1, cols] * source[pl.ds(lead, count), cols]
        for j in range(1, SHORT):
            total += short_ref[j, i : i + 1, cols] * source[pl.ds(lead - j, count), cols]
        return total

    for tile in range(tiles):
        cols = slice(tile * LANES, (tile + 1) * LANES)
        products = []
        for v in range(2):
            key = featured(held.at[v, 0], 1, reach, cols)
            value = featured(held.at[v, 1], 2, reach, cols)
            products.append((key * value).astype(jnp.bfloat16))
        both = jnp.concatenate(products, axis=1)
        filtered = None
        for k in range(per_tile):
            one = jnp.dot(
                toeplitz[tile, pl.ds(k * tok_len, tok_len), :], both, preferred_element_type=jnp.float32
            )
            filtered = one if k == 0 else jnp.where(lane_group == k, one, filtered)
        for v in range(2):
            query = featured(held_query.at[v], 0, tok_len, cols)
            gated_ref[v, :, cols] = (query * filtered[:, v * LANES : (v + 1) * LANES]).astype(jnp.bfloat16)


def mix(ids, table, short_taps, toeplitz, tok_len):
    windows, rows = ids.shape
    panel_width = table.shape[2]
    return pl.pallas_call(
        mixer_kernel,
        grid=(windows // 2,),
        in_specs=[pl.BlockSpec((2, 1, rows), lambda p: (p, 0, 0))]
        + [whole(array) for array in (table, short_taps, toeplitz)],
        out_specs=pl.BlockSpec((2, tok_len, panel_width), lambda p: (p, 0, 0)),
        out_shape=jax.ShapeDtypeStruct((windows, tok_len, panel_width), jnp.bfloat16),
        scratch_shapes=[
            pltpu.VMEM((2, LEAD + tok_len, panel_width), jnp.float32),
            pltpu.VMEM((2, 2, rows, panel_width), jnp.float32),
        ],
        compiler_params=params(),
        cost_estimate=cost(1_500_000_000, 0),
    )(ids.reshape(windows, 1, rows), table, short_taps, toeplitz)


def cut_kernel(place_ref, *refs):
    count = len(refs) // 2
    for source, piece in zip(refs[:count], refs[count:]):
        piece[...] = source[...]


def cut_pieces(place, out_proj):
    depth, width = out_proj.shape
    unit = width // SIXTEENTHS
    ins, outs, shapes = [], [], []
    for first, extent, order, _ in SPLITS:
        sharers = len(order)
        cols = extent * unit // sharers
        start = first * unit // cols
        ins.append(pl.BlockSpec((depth, cols), lambda s, place, start=start, n=sharers: (0, start + place[0] % n)))
        outs.append(pl.BlockSpec((depth, cols), lambda s, place: (0, 0)))
        shapes.append(jax.ShapeDtypeStruct((depth, cols), out_proj.dtype))
    return pl.pallas_call(
        cut_kernel,
        grid_spec=pltpu.PrefetchScalarGridSpec(num_scalar_prefetch=1, grid=(1,), in_specs=ins, out_specs=outs),
        out_shape=shapes,
        compiler_params=params(60),
        cost_estimate=cost(0, 2_000_000),
    )(place, *[out_proj] * len(SPLITS))


def toeplitz_kernel(base_ref, toeplitz_ref):
    tiles, stacked, reach = toeplitz_ref.shape
    per_tile = base_ref.shape[0] // tiles
    tok_len = stacked // per_tile
    for tile in range(tiles):
        for k in range(per_tile):
            g = tile * per_tile + k
            wide = jnp.broadcast_to(base_ref[g : g + 1, :], (tok_len, reach))
            shifted = pltpu.roll(wide, 0, 1, stride=1, stride_axis=0)
            toeplitz_ref[tile, pl.ds(k * tok_len, tok_len), :] = shifted.astype(jnp.bfloat16)


def build_toeplitz(conv_taps, tok_len):
    reach = 2 * tok_len
    per_tile = LANES // GROUP
    tiles = conv_taps.shape[0] // per_tile
    base = jnp.pad(conv_taps[:, ::-1].astype(jnp.float32), ((0, 0), (1, reach - TAPS - 1)))
    shape = jax.ShapeDtypeStruct((tiles, per_tile * tok_len, reach), jnp.bfloat16)
    return pl.pallas_call(
        toeplitz_kernel,
        grid=(1,),
        in_specs=[whole(base)],
        out_specs=whole(shape),
        out_shape=shape,
        compiler_params=params(8),
        cost_estimate=cost(0, 2_000_000),
    )(base)


def panel_kernel(place_ref, mine_ref, other_ref, *refs):
    out_ref = refs[-1]
    count, sharers, tok_len, _ = out_ref.shape
    beside = [ref.at[i] for ref in refs[sharers:-1] for i in range(ref.shape[0])]
    for k in range(sharers):
        total = jnp.dot(mine_ref[...], refs[k][...], preferred_element_type=jnp.float32)
        total += jnp.dot(other_ref[...], beside[k][...], preferred_element_type=jnp.float32)
        for w in range(count):
            out_ref[w, k] = total[w * tok_len : (w + 1) * tok_len].astype(out_ref.dtype)


def panel(place, mine, other, out_proj, beside, split, step):
    count, tok_len, depth = mine.shape
    rows = count * tok_len
    unit = out_proj.shape[1] // SIXTEENTHS
    base, extent, order, _ = split
    sharers = len(order)
    piece_cols = extent * unit // sharers
    offset, cols = (part * unit // sharers for part in step)
    fixed = lambda shape: pl.BlockSpec(shape, lambda s, place: (0,) * len(shape))

    def own(k):
        start, per = (base * unit + offset) // cols, piece_cols // cols
        return pl.BlockSpec((depth, cols), lambda s, place: (0, start + (place[0] % sharers ^ k) * per))

    near = lambda a: pl.BlockSpec((a.shape[0], depth, cols), lambda s, place: (0, 0, offset // cols))
    return pl.pallas_call(
        panel_kernel,
        grid_spec=pltpu.PrefetchScalarGridSpec(
            num_scalar_prefetch=1,
            grid=(1,),
            in_specs=[fixed((rows, depth))] * 2 + [own(k) for k in order] + [near(a) for a in beside],
            out_specs=fixed((count, sharers, tok_len, cols)),
        ),
        out_shape=jax.ShapeDtypeStruct((count, sharers, tok_len, cols), jnp.bfloat16),
        compiler_params=params(),
        cost_estimate=cost(400_000_000, 0),
    )(place, mine.reshape(rows, depth), other.reshape(rows, depth), *[out_proj] * sharers, *beside)


def residual_kernel(ids_ref, rows_ref, out_ref):
    names = lax.broadcasted_iota(jnp.int32, (rows_ref.shape[0], ids_ref.shape[1]), 0)
    one_hot = (names == ids_ref[...]).astype(jnp.float32).astype(jnp.bfloat16)
    out_ref[...] = lax.dot_general(
        one_hot, rows_ref[...], (((0,), (0,)), ((), ())), preferred_element_type=jnp.float32
    ).astype(jnp.bfloat16)


def residual(token_ids, embedding):
    vocab, width = embedding.shape
    tok_len = token_ids.shape[1]
    cols = width // 4
    return pl.pallas_call(
        residual_kernel,
        grid=(4,),
        in_specs=[whole(token_ids), pl.BlockSpec((vocab, cols), lambda i: (0, i))],
        out_specs=pl.BlockSpec((tok_len, cols), lambda i: (0, i)),
        out_shape=jax.ShapeDtypeStruct((tok_len, width), jnp.bfloat16),
        compiler_params=params(),
        cost_estimate=cost(400_000_000, 0),
    )(token_ids, embedding)


def place_kernel(split, step, place_ref, so_far_ref, near_ref, far_ref, out_ref):
    _, sharers, _, cols = near_ref.shape
    piece_cols = so_far_ref.shape[1] // sharers
    offset = step[0] * cols // step[1]
    out_ref[...] = so_far_ref[...]
    for i, k in enumerate(split[2]):
        first = (place_ref[0] % sharers ^ k) * piece_cols + offset
        total = near_ref[0, i].astype(jnp.float32) + far_ref[0, i].astype(jnp.float32)
        at = pl.ds(pl.multiple_of(first, LANES), cols)
        out_ref[:, at] = (so_far_ref[:, at].astype(jnp.float32) + total).astype(jnp.bfloat16)


def place_pieces(place, so_far, near, far, split, step):
    tok_len, width = so_far.shape
    base, extent, _, _ = split
    part = pl.BlockSpec((tok_len, extent * width // SIXTEENTHS), lambda s, place: (0, base // extent))
    one = pl.BlockSpec(near.shape, lambda s, place: (0, 0, 0, 0))
    return pl.pallas_call(
        functools.partial(place_kernel, split, step),
        grid_spec=pltpu.PrefetchScalarGridSpec(
            num_scalar_prefetch=1, grid=(1,), in_specs=[part, one, one], out_specs=part
        ),
        out_shape=jax.ShapeDtypeStruct(so_far.shape, so_far.dtype),
        input_output_aliases={1: 0},
        compiler_params=params(),
        cost_estimate=cost(0, 1_000_000),
    )(place, so_far, near, far)


def add(a, b):
    return (a.astype(jnp.float32) + b.astype(jnp.float32)).astype(jnp.bfloat16)


def per_device(token_ids, embedding, norm_gain, in_proj, short_taps, conv_taps, out_proj):
    tok_len = token_ids.shape[1]
    at = lax.axis_index("ctx").reshape(1).astype(jnp.int32)
    bits = exchange_bits()
    tie = lax.optimization_barrier
    beside_bit = bits[-2]

    early, late = cut_pieces(at, out_proj)
    ids = level_ids(token_ids, bits[:2])
    ids, early, late, conv_taps = tie((ids, early, late, conv_taps))
    toeplitz = build_toeplitz(conv_taps, tok_len)
    for group in [bits[i : i + 2] for i in range(2, len(bits), 2)]:
        ids = level_ids(ids, group)
    ids, toeplitz = tie((ids, toeplitz))
    early, late = swap(early, "fsdp", beside_bit), swap(late, "fsdp", beside_bit)
    ids, embedding_then = tie((ids, embedding))
    ids = with_lead(ids)
    table = project(embedding_then, norm_gain, in_proj)
    table, early = tie((table, early))
    early_across = swap(early, "ctx", 2)

    part = ids.shape[0] // 4
    sent = mix(ids[3 * part :], table, short_taps, toeplitz, tok_len)
    ids, sent = tie((ids, sent))
    other = [swap(sent, "fsdp", beside_bit)]
    gated = mix(ids[: 3 * part], table, short_taps, toeplitz, tok_len)
    gated, other[0], early, early_across, late = tie((gated, other[0], early, early_across, late))
    mine = [gated[2 * part :], gated[:part]]
    other.append(swap(gated[part : 2 * part], "fsdp", beside_bit))
    pair = jnp.stack([early, early_across])
    beside = [(pair, swap(pair, "ctx", 1))]
    pair = jnp.stack([late, swap(late, "ctx", 1)])
    beside.append((pair, swap(pair, "ctx", 2)))

    out = residual(token_ids, embedding)
    away, arrived, behind = [], [], []

    def send(number, step):
        part = panel(at, mine[0], other[0], out_proj, beside[number], SPLITS[number], step)
        part, mine[0] = tie((part, mine[0]))
        away.append(part)
        arrived.append(swap(part, "fsdp", bits[-1]))

    def sum_up(number, step):
        got, total = arrived[len(behind)], panel(at, mine[1], other[1], out_proj, beside[number], SPLITS[number], step)
        if behind:
            got, _ = tie((got, behind[-1][-1]))
        for bit in reversed(bits[:-2]):
            half = total.shape[0] // 2
            far = add(total[half:], got[half:])
            total, got = add(total[:half], got[:half]), swap(far, "fsdp", bit)
        behind.append((total, got, SPLITS[number], step, far))

    first, second, *rest = SPLITS[0][3]
    send(0, first)
    send(0, second)
    other[1], out, _ = tie((other[1], out, away[1]))
    mine[0], arrived[0] = tie((mine[0], arrived[0]))
    for step in rest:
        send(0, step)
    for step in SPLITS[0][3]:
        sum_up(0, step)
    beside[1], _ = tie((beside[1], (behind[0][1], behind[1][1])))
    for step in SPLITS[1][3]:
        send(1, step)
    for step in SPLITS[1][3]:
        sum_up(1, step)
    for last in behind:
        out = place_pieces(at, out, *last[:-1])
    return out[None]


def solution(mesh):
    return jax.shard_map(
        per_device,
        mesh=mesh,
        in_specs=(
            P("fsdp", "ctx"),
            P(),
            P(),
            P(None, None, "fsdp"),
            P(None, None, "fsdp"),
            P("fsdp", None),
            P("fsdp", None),
        ),
        out_specs=P("fsdp", "ctx", None),
        check_vma=False,
    )
```

```python
import functools

import jax
import jax.numpy as jnp
from jax import lax
from jax.experimental import pallas as pl
from jax.experimental.pallas import tpu as pltpu
from jax.sharding import PartitionSpec as P

GROUP = 16
TAPS = 128
SHORT = 3
LANES = 128
LEAD = 16
SPLITS = ((0, 8, (0, 2, 1, 3), ((0, 4), (4, 4))), (8, 8, (0, 1, 2, 3), ((0, 4), (4, 2), (6, 2))))
SIXTEENTHS = 16


def from_behind(x, axis, by):
    peers = lax.axis_size(axis)
    return lax.ppermute(x, axis, [(i, (i + by) % peers) for i in range(peers)])


def swap(x, axis, mask):
    peers = lax.axis_size(axis)
    return lax.ppermute(x, axis, [(i, i ^ mask) for i in range(peers)])


def exchange_bits():
    peers = lax.axis_size("fsdp")
    return [1 << b for b in reversed(range(peers.bit_length() - 1))]


def params(mib=24):
    return pltpu.CompilerParams(vmem_limit_bytes=mib * 1024 * 1024)


def cost(flops, bytes_accessed):
    return pl.CostEstimate(flops=flops, bytes_accessed=bytes_accessed, transcendentals=0)


def whole(array):
    return pl.BlockSpec(array.shape, lambda *_: (0,) * len(array.shape))


def level_ids(ids, group):
    masks = [0]
    for bit in group:
        masks += [mask | bit for mask in masks]
    return jnp.concatenate([ids] + [swap(ids, "fsdp", mask) for mask in masks[1:]], axis=0)


def with_lead(ids):
    tok_len = ids.shape[1]
    place = lax.axis_index("ctx")
    one = jnp.where(place >= 1, from_behind(ids, "ctx", 1), -1)
    two = jnp.where(place >= 2, from_behind(ids, "ctx", 2), -1)
    return jnp.concatenate([two[:, tok_len - LEAD :], one, ids], axis=1)


def table_kernel(rows_hbm, weight_hbm, gain_ref, table_ref, rows, weight, row_sems, weight_sems):
    count, width, panel_width = weight.shape
    parts, blocks = row_sems.shape[0], weight_sems.shape[1]
    each, deep = rows.shape[0] // parts, width // blocks
    row_copies = [
        pltpu.make_async_copy(rows_hbm.at[pl.ds(r * each, each)], rows.at[pl.ds(r * each, each)], row_sems.at[r])
        for r in range(parts)
    ]
    weight_copies = [
        [
            pltpu.make_async_copy(
                weight_hbm.at[i, pl.ds(k * deep, deep)], weight.at[i, pl.ds(k * deep, deep)], weight_sems.at[i, k]
            )
            for k in range(blocks)
        ]
        for i in range(count)
    ]
    for copy in row_copies + sum(weight_copies, []):
        copy.start()
    for r in range(parts):
        row_copies[r].wait()
        at = pl.ds(r * each, each)
        values = rows[at, :].astype(jnp.float32)
        inverse_rms = lax.rsqrt(jnp.mean(values * values, axis=-1, keepdims=True) + 1e-06)
        rows[at, :] = (values * inverse_rms * gain_ref[...]).astype(jnp.bfloat16)
    cols = min(256, panel_width)
    for i in range(count):
        for copy in weight_copies[i]:
            copy.wait()
        for first in range(0, panel_width, cols):
            at = slice(first, first + cols)
            part = jnp.dot(rows[...], weight[i, :, at], preferred_element_type=jnp.float32)
            table_ref[i, :, at] = part.astype(jnp.bfloat16)


def project(embedding, norm_gain, in_proj):
    vocab, width = embedding.shape
    count, _, panel_width = in_proj.shape
    hbm = pl.BlockSpec(memory_space=pltpu.HBM)
    shape = jax.ShapeDtypeStruct((count, vocab, panel_width), jnp.bfloat16)
    return pl.pallas_call(
        table_kernel,
        grid=(1,),
        in_specs=[hbm, hbm, pl.BlockSpec((1, width), lambda s: (0, 0))],
        out_specs=whole(shape),
        out_shape=shape,
        scratch_shapes=[
            pltpu.VMEM(embedding.shape, jnp.bfloat16),
            pltpu.VMEM(in_proj.shape, jnp.bfloat16),
            pltpu.SemaphoreType.DMA((8,)),
            pltpu.SemaphoreType.DMA((count, 4)),
        ],
        compiler_params=params(59),
        cost_estimate=cost(3_000_000_000, 0),
    )(embedding, in_proj, norm_gain.reshape(1, width))


def mixer_kernel(ids_ref, table_ref, short_ref, toeplitz, gated_ref, held_query, held):
    tok_len, panel_width = gated_ref.shape[1:]
    vocab = table_ref.shape[1]
    rows = ids_ref.shape[2]
    reach = 2 * tok_len
    lead = rows - reach
    tiles = panel_width // LANES
    per_tile = LANES // GROUP
    names = lax.broadcasted_iota(jnp.int32, (vocab, rows), 0)
    lane_group = lax.broadcasted_iota(jnp.int32, (tok_len, 2 * LANES), 1) % LANES // GROUP

    def look_up(one_hot, table):
        found = lax.dot_general(one_hot, table, (((0,), (0,)), ((), ())), preferred_element_type=jnp.float32)
        return found.astype(jnp.bfloat16).astype(jnp.float32)

    for v in range(2):
        one_hot = (names == ids_ref[v]).astype(jnp.float32).astype(jnp.bfloat16)
        held[v, 0] = look_up(one_hot, table_ref[1])
        held[v, 1] = look_up(one_hot, table_ref[2])
        held_query[v] = look_up(one_hot[:, rows - lead - tok_len :], table_ref[0])

    def featured(source, i, count, cols):
        total = short_ref[0, i : i + 1, cols] * source[pl.ds(lead, count), cols]
        for j in range(1, SHORT):
            total += short_ref[j, i : i + 1, cols] * source[pl.ds(lead - j, count), cols]
        return total

    for tile in range(tiles):
        cols = slice(tile * LANES, (tile + 1) * LANES)
        products = []
        for v in range(2):
            key = featured(held.at[v, 0], 1, reach, cols)
            value = featured(held.at[v, 1], 2, reach, cols)
            products.append((key * value).astype(jnp.bfloat16))
        both = jnp.concatenate(products, axis=1)
        filtered = None
        for k in range(per_tile):
            one = jnp.dot(
                toeplitz[tile, pl.ds(k * tok_len, tok_len), :], both, preferred_element_type=jnp.float32
            )
            filtered = one if k == 0 else jnp.where(lane_group == k, one, filtered)
        for v in range(2):
            query = featured(held_query.at[v], 0, tok_len, cols)
            gated_ref[v, :, cols] = (query * filtered[:, v * LANES : (v + 1) * LANES]).astype(jnp.bfloat16)


def mix(ids, table, short_taps, toeplitz, tok_len):
    windows, rows = ids.shape
    panel_width = table.shape[2]
    return pl.pallas_call(
        mixer_kernel,
        grid=(windows // 2,),
        in_specs=[pl.BlockSpec((2, 1, rows), lambda p: (p, 0, 0))]
        + [whole(array) for array in (table, short_taps, toeplitz)],
        out_specs=pl.BlockSpec((2, tok_len, panel_width), lambda p: (p, 0, 0)),
        out_shape=jax.ShapeDtypeStruct((windows, tok_len, panel_width), jnp.bfloat16),
        scratch_shapes=[
            pltpu.VMEM((2, LEAD + tok_len, panel_width), jnp.float32),
            pltpu.VMEM((2, 2, rows, panel_width), jnp.float32),
        ],
        compiler_params=params(),
        cost_estimate=cost(1_500_000_000, 0),
    )(ids.reshape(windows, 1, rows), table, short_taps, toeplitz)


def cut_kernel(place_ref, *refs):
    count = len(refs) // 2
    for source, piece in zip(refs[:count], refs[count:]):
        piece[...] = source[...]


def cut_pieces(place, out_proj):
    depth, width = out_proj.shape
    unit = width // SIXTEENTHS
    ins, outs, shapes = [], [], []
    for first, extent, order, _ in SPLITS:
        sharers = len(order)
        cols = extent * unit // sharers
        start = first * unit // cols
        ins.append(pl.BlockSpec((depth, cols), lambda s, place, start=start, n=sharers: (0, start + place[0] % n)))
        outs.append(pl.BlockSpec((depth, cols), lambda s, place: (0, 0)))
        shapes.append(jax.ShapeDtypeStruct((depth, cols), out_proj.dtype))
    return pl.pallas_call(
        cut_kernel,
        grid_spec=pltpu.PrefetchScalarGridSpec(num_scalar_prefetch=1, grid=(1,), in_specs=ins, out_specs=outs),
        out_shape=shapes,
        compiler_params=params(60),
        cost_estimate=cost(0, 2_000_000),
    )(place, *[out_proj] * len(SPLITS))


def toeplitz_kernel(base_ref, toeplitz_ref):
    tiles, stacked, reach = toeplitz_ref.shape
    per_tile = base_ref.shape[0] // tiles
    tok_len = stacked // per_tile
    for tile in range(tiles):
        for k in range(per_tile):
            g = tile * per_tile + k
            wide = jnp.broadcast_to(base_ref[g : g + 1, :], (tok_len, reach))
            shifted = pltpu.roll(wide, 0, 1, stride=1, stride_axis=0)
            toeplitz_ref[tile, pl.ds(k * tok_len, tok_len), :] = shifted.astype(jnp.bfloat16)


def build_toeplitz(conv_taps, tok_len):
    reach = 2 * tok_len
    per_tile = LANES // GROUP
    tiles = conv_taps.shape[0] // per_tile
    base = jnp.pad(conv_taps[:, ::-1].astype(jnp.float32), ((0, 0), (1, reach - TAPS - 1)))
    shape = jax.ShapeDtypeStruct((tiles, per_tile * tok_len, reach), jnp.bfloat16)
    return pl.pallas_call(
        toeplitz_kernel,
        grid=(1,),
        in_specs=[whole(base)],
        out_specs=whole(shape),
        out_shape=shape,
        compiler_params=params(8),
        cost_estimate=cost(0, 2_000_000),
    )(base)


def panel_kernel(place_ref, mine_ref, other_ref, *refs):
    out_ref = refs[-1]
    count, sharers, tok_len, _ = out_ref.shape
    beside = [ref.at[i] for ref in refs[sharers:-1] for i in range(ref.shape[0])]
    for k in range(sharers):
        total = jnp.dot(mine_ref[...], refs[k][...], preferred_element_type=jnp.float32)
        total += jnp.dot(other_ref[...], beside[k][...], preferred_element_type=jnp.float32)
        for w in range(count):
            out_ref[w, k] = total[w * tok_len : (w + 1) * tok_len].astype(out_ref.dtype)


def panel(place, mine, other, out_proj, beside, split, step, begin=0):
    count, tok_len, depth = mine.shape
    rows = count * tok_len
    unit = out_proj.shape[1] // SIXTEENTHS
    base, extent, order, _ = split
    sharers = len(order)
    piece_cols = extent * unit // sharers
    offset, cols = (part * unit // sharers for part in step)
    fixed = lambda shape: pl.BlockSpec(shape, lambda s, place: (0,) * len(shape))

    def own(k):
        start, per = (base * unit + offset) // cols, piece_cols // cols
        return pl.BlockSpec((depth, cols), lambda s, place: (0, start + (place[0] % sharers ^ k) * per))

    near = lambda a: pl.BlockSpec((a.shape[0], depth, cols), lambda s, place: (0, 0, offset // cols - begin * unit // sharers // cols))
    return pl.pallas_call(
        panel_kernel,
        grid_spec=pltpu.PrefetchScalarGridSpec(
            num_scalar_prefetch=1,
            grid=(1,),
            in_specs=[fixed((rows, depth))] * 2 + [own(k) for k in order] + [near(a) for a in beside],
            out_specs=fixed((count, sharers, tok_len, cols)),
        ),
        out_shape=jax.ShapeDtypeStruct((count, sharers, tok_len, cols), jnp.bfloat16),
        compiler_params=params(),
        cost_estimate=cost(400_000_000, 0),
    )(place, mine.reshape(rows, depth), other.reshape(rows, depth), *[out_proj] * sharers, *beside)


def residual_kernel(ids_ref, rows_ref, out_ref):
    names = lax.broadcasted_iota(jnp.int32, (rows_ref.shape[0], ids_ref.shape[1]), 0)
    one_hot = (names == ids_ref[...]).astype(jnp.float32).astype(jnp.bfloat16)
    out_ref[...] = lax.dot_general(
        one_hot, rows_ref[...], (((0,), (0,)), ((), ())), preferred_element_type=jnp.float32
    ).astype(jnp.bfloat16)


def residual(token_ids, embedding):
    vocab, width = embedding.shape
    tok_len = token_ids.shape[1]
    cols = width // 4
    return pl.pallas_call(
        residual_kernel,
        grid=(4,),
        in_specs=[whole(token_ids), pl.BlockSpec((vocab, cols), lambda i: (0, i))],
        out_specs=pl.BlockSpec((tok_len, cols), lambda i: (0, i)),
        out_shape=jax.ShapeDtypeStruct((tok_len, width), jnp.bfloat16),
        compiler_params=params(),
        cost_estimate=cost(400_000_000, 0),
    )(token_ids, embedding)


def place_kernel(split, step, place_ref, so_far_ref, near_ref, far_ref, out_ref):
    _, sharers, _, cols = near_ref.shape
    piece_cols = so_far_ref.shape[1] // sharers
    offset = step[0] * cols // step[1]
    out_ref[...] = so_far_ref[...]
    for i, k in enumerate(split[2]):
        first = (place_ref[0] % sharers ^ k) * piece_cols + offset
        total = near_ref[0, i].astype(jnp.float32) + far_ref[0, i].astype(jnp.float32)
        at = pl.ds(pl.multiple_of(first, LANES), cols)
        out_ref[:, at] = (so_far_ref[:, at].astype(jnp.float32) + total).astype(jnp.bfloat16)


def place_pieces(place, so_far, near, far, split, step):
    tok_len, width = so_far.shape
    base, extent, _, _ = split
    part = pl.BlockSpec((tok_len, extent * width // SIXTEENTHS), lambda s, place: (0, base // extent))
    one = pl.BlockSpec(near.shape, lambda s, place: (0, 0, 0, 0))
    return pl.pallas_call(
        functools.partial(place_kernel, split, step),
        grid_spec=pltpu.PrefetchScalarGridSpec(
            num_scalar_prefetch=1, grid=(1,), in_specs=[part, one, one], out_specs=part
        ),
        out_shape=jax.ShapeDtypeStruct(so_far.shape, so_far.dtype),
        input_output_aliases={1: 0},
        compiler_params=params(),
        cost_estimate=cost(0, 1_000_000),
    )(place, so_far, near, far)


def add(a, b):
    return (a.astype(jnp.float32) + b.astype(jnp.float32)).astype(jnp.bfloat16)


def per_device(token_ids, embedding, norm_gain, in_proj, short_taps, conv_taps, out_proj):
    tok_len = token_ids.shape[1]
    at = lax.axis_index("ctx").reshape(1).astype(jnp.int32)
    bits = exchange_bits()
    tie = lax.optimization_barrier
    beside_bit = bits[-2]

    early, late = cut_pieces(at, out_proj)
    early, late, conv_taps = tie((early, late, conv_taps))
    toeplitz = build_toeplitz(conv_taps, tok_len)
    ids = level_ids(token_ids, bits[:2])
    ids, toeplitz = tie((ids, toeplitz))
    for group in [bits[i : i + 2] for i in range(2, len(bits), 2)]:
        ids = level_ids(ids, group)
    early, late = swap(early, "fsdp", beside_bit), swap(late, "fsdp", beside_bit)
    ids, embedding_then = tie((ids, embedding))
    ids = with_lead(ids)
    table = project(embedding_then, norm_gain, in_proj)
    table, early = tie((table, early))
    early_across = swap(early, "ctx", 2)

    part = ids.shape[0] // 4
    sent = mix(ids[3 * part :], table, short_taps, toeplitz, tok_len)
    ids, sent = tie((ids, sent))
    other = [swap(sent, "fsdp", beside_bit)]
    gated = mix(ids[: 3 * part], table, short_taps, toeplitz, tok_len)
    gated, other[0], early, early_across, late = tie((gated, other[0], early, early_across, late))
    mine = [gated[2 * part :], gated[:part]]
    sent = gated[part : 2 * part]
    pair = jnp.stack([early, early_across])
    beside = [(pair, swap(pair, "ctx", 1))]

    out = residual(token_ids, embedding)
    away, arrived, behind = [], [], []

    def send(shared, number, step, begin=0):
        part = panel(at, mine[0], other[0], out_proj, shared, SPLITS[number], step, begin)
        part, mine[0] = tie((part, mine[0]))
        away.append(part)
        arrived.append(swap(part, "fsdp", bits[-1]))

    def sum_up(shared, number, step, begin=0):
        got, total = arrived[len(behind)], panel(at, mine[1], other[1], out_proj, shared, SPLITS[number], step, begin)
        if behind:
            got, _ = tie((got, behind[-1][-1]))
        for bit in reversed(bits[:-2]):
            half = total.shape[0] // 2
            far = add(total[half:], got[half:])
            total, got = add(total[:half], got[:half]), swap(far, "fsdp", bit)
        behind.append((total, got, SPLITS[number], step, far))

    first, second = SPLITS[0][3]
    send(beside[0], 0, first)
    sent, late, out, _ = tie((sent, late, out, away[0]))
    other.append(swap(sent, "fsdp", beside_bit))
    pair = jnp.stack([late, swap(late, "ctx", 1)])
    middle = pair.shape[2] // 2
    send(beside[0], 0, second)
    other[1], out, _ = tie((other[1], out, away[1]))
    sum_up(beside[0], 0, first)
    sum_up(beside[0], 0, second)
    third, *rest = SPLITS[1][3]
    for columns, steps, begin in ((pair[:, :, :middle], [third], 0), (pair[:, :, middle:], rest, third[1])):
        shared = (columns, swap(columns, "ctx", 2))
        shared, _ = tie((shared, behind[0][-1] if begin == 0 else behind[0][1]))
        for step in steps:
            send(shared, 1, step, begin)
        for step in steps:
            sum_up(shared, 1, step, begin)
    for last in behind:
        out = place_pieces(at, out, *last[:-1])
    return out[None]


def solution(mesh):
    return jax.shard_map(
        per_device,
        mesh=mesh,
        in_specs=(
            P("fsdp", "ctx"),
            P(),
            P(),
            P(None, None, "fsdp"),
            P(None, None, "fsdp"),
            P("fsdp", None),
            P("fsdp", None),
        ),
        out_specs=P("fsdp", "ctx", None),
        check_vma=False,
    )
```

```python
import functools

import jax
import jax.numpy as jnp
from jax import lax
from jax.experimental import pallas as pl
from jax.experimental.pallas import tpu as pltpu
from jax.sharding import PartitionSpec as P

GROUP = 16
TAPS = 128
SHORT = 3
LANES = 128
LEAD = 16
SPLITS = ((0, 8, (0, 2, 1, 3), ((0, 4), (4, 4))), (8, 8, (0, 1, 2, 3), ((0, 4), (4, 4))))
SIXTEENTHS = 16


def from_behind(x, axis, by):
    peers = lax.axis_size(axis)
    return lax.ppermute(x, axis, [(i, (i + by) % peers) for i in range(peers)])


def swap(x, axis, mask):
    peers = lax.axis_size(axis)
    return lax.ppermute(x, axis, [(i, i ^ mask) for i in range(peers)])


def exchange_bits():
    peers = lax.axis_size("fsdp")
    return [1 << b for b in reversed(range(peers.bit_length() - 1))]


def params(mib=24):
    return pltpu.CompilerParams(vmem_limit_bytes=mib * 1024 * 1024)


def cost(flops, bytes_accessed):
    return pl.CostEstimate(flops=flops, bytes_accessed=bytes_accessed, transcendentals=0)


def whole(array):
    return pl.BlockSpec(array.shape, lambda *_: (0,) * len(array.shape))


def level_ids(ids, group):
    masks = [0]
    for bit in group:
        masks += [mask | bit for mask in masks]
    return jnp.concatenate([ids] + [swap(ids, "fsdp", mask) for mask in masks[1:]], axis=0)


def with_lead(ids):
    tok_len = ids.shape[1]
    place = lax.axis_index("ctx")
    one = jnp.where(place >= 1, from_behind(ids, "ctx", 1), -1)
    two = jnp.where(place >= 2, from_behind(ids, "ctx", 2), -1)
    return jnp.concatenate([two[:, tok_len - LEAD :], one, ids], axis=1)


def table_kernel(rows_hbm, weight_hbm, gain_ref, table_ref, rows, weight, row_sems, weight_sems):
    count, width, panel_width = weight.shape
    parts, blocks = row_sems.shape[0], weight_sems.shape[1]
    each, deep = rows.shape[0] // parts, width // blocks
    row_copies = [
        pltpu.make_async_copy(rows_hbm.at[pl.ds(r * each, each)], rows.at[pl.ds(r * each, each)], row_sems.at[r])
        for r in range(parts)
    ]
    weight_copies = [
        [
            pltpu.make_async_copy(
                weight_hbm.at[i, pl.ds(k * deep, deep)], weight.at[i, pl.ds(k * deep, deep)], weight_sems.at[i, k]
            )
            for k in range(blocks)
        ]
        for i in range(count)
    ]
    for copy in row_copies + sum(weight_copies, []):
        copy.start()
    for r in range(parts):
        row_copies[r].wait()
        at = pl.ds(r * each, each)
        values = rows[at, :].astype(jnp.float32)
        inverse_rms = lax.rsqrt(jnp.mean(values * values, axis=-1, keepdims=True) + 1e-06)
        rows[at, :] = (values * inverse_rms * gain_ref[...]).astype(jnp.bfloat16)
    cols = min(256, panel_width)
    for i in range(count):
        for copy in weight_copies[i]:
            copy.wait()
        for first in range(0, panel_width, cols):
            at = slice(first, first + cols)
            part = jnp.dot(rows[...], weight[i, :, at], preferred_element_type=jnp.float32)
            table_ref[i, :, at] = part.astype(jnp.bfloat16)


def project(embedding, norm_gain, in_proj):
    vocab, width = embedding.shape
    count, _, panel_width = in_proj.shape
    hbm = pl.BlockSpec(memory_space=pltpu.HBM)
    shape = jax.ShapeDtypeStruct((count, vocab, panel_width), jnp.bfloat16)
    return pl.pallas_call(
        table_kernel,
        grid=(1,),
        in_specs=[hbm, hbm, pl.BlockSpec((1, width), lambda s: (0, 0))],
        out_specs=whole(shape),
        out_shape=shape,
        scratch_shapes=[
            pltpu.VMEM(embedding.shape, jnp.bfloat16),
            pltpu.VMEM(in_proj.shape, jnp.bfloat16),
            pltpu.SemaphoreType.DMA((8,)),
            pltpu.SemaphoreType.DMA((count, 4)),
        ],
        compiler_params=params(40),
        cost_estimate=cost(3_000_000_000, 0),
    )(embedding, in_proj, norm_gain.reshape(1, width))


def mixer_kernel(ids_ref, table_ref, short_ref, toeplitz, gated_ref, held_query, held):
    tok_len, panel_width = gated_ref.shape[1:]
    vocab = table_ref.shape[1]
    rows = ids_ref.shape[2]
    reach = 2 * tok_len
    lead = rows - reach
    tiles = panel_width // LANES
    per_tile = LANES // GROUP
    names = lax.broadcasted_iota(jnp.int32, (vocab, rows), 0)
    lane_group = lax.broadcasted_iota(jnp.int32, (tok_len, 2 * LANES), 1) % LANES // GROUP

    def look_up(one_hot, table):
        found = lax.dot_general(one_hot, table, (((0,), (0,)), ((), ())), preferred_element_type=jnp.float32)
        return found.astype(jnp.bfloat16).astype(jnp.float32)

    for v in range(2):
        one_hot = (names == ids_ref[v]).astype(jnp.float32).astype(jnp.bfloat16)
        held[v, 0] = look_up(one_hot, table_ref[1])
        held[v, 1] = look_up(one_hot, table_ref[2])
        held_query[v] = look_up(one_hot[:, rows - lead - tok_len :], table_ref[0])

    def featured(source, i, count, cols):
        total = short_ref[0, i : i + 1, cols] * source[pl.ds(lead, count), cols]
        for j in range(1, SHORT):
            total += short_ref[j, i : i + 1, cols] * source[pl.ds(lead - j, count), cols]
        return total

    for tile in range(tiles):
        cols = slice(tile * LANES, (tile + 1) * LANES)
        products = []
        for v in range(2):
            key = featured(held.at[v, 0], 1, reach, cols)
            value = featured(held.at[v, 1], 2, reach, cols)
            products.append((key * value).astype(jnp.bfloat16))
        both = jnp.concatenate(products, axis=1)
        filtered = None
        for k in range(per_tile):
            one = jnp.dot(
                toeplitz[tile, pl.ds(k * tok_len, tok_len), :], both, preferred_element_type=jnp.float32
            )
            filtered = one if k == 0 else jnp.where(lane_group == k, one, filtered)
        for v in range(2):
            query = featured(held_query.at[v], 0, tok_len, cols)
            gated_ref[v, :, cols] = (query * filtered[:, v * LANES : (v + 1) * LANES]).astype(jnp.bfloat16)


def mix(ids, table, short_taps, toeplitz, tok_len):
    windows, rows = ids.shape
    panel_width = table.shape[2]
    return pl.pallas_call(
        mixer_kernel,
        grid=(windows // 2,),
        in_specs=[pl.BlockSpec((2, 1, rows), lambda p: (p, 0, 0))]
        + [whole(array) for array in (table, short_taps, toeplitz)],
        out_specs=pl.BlockSpec((2, tok_len, panel_width), lambda p: (p, 0, 0)),
        out_shape=jax.ShapeDtypeStruct((windows, tok_len, panel_width), jnp.bfloat16),
        scratch_shapes=[
            pltpu.VMEM((2, LEAD + tok_len, panel_width), jnp.float32),
            pltpu.VMEM((2, 2, rows, panel_width), jnp.float32),
        ],
        compiler_params=params(),
        cost_estimate=cost(1_500_000_000, 0),
    )(ids.reshape(windows, 1, rows), table, short_taps, toeplitz)


def cut_kernel(place_ref, *refs):
    count = len(refs) // 2
    for source, piece in zip(refs[:count], refs[count:]):
        piece[...] = source[...]


def cut_pieces(place, out_proj):
    depth, width = out_proj.shape
    unit = width // SIXTEENTHS
    ins, outs, shapes = [], [], []
    for first, extent, order, _ in SPLITS:
        sharers = len(order)
        cols = extent * unit // sharers
        start = first * unit // cols
        ins.append(pl.BlockSpec((depth, cols), lambda s, place, start=start, n=sharers: (0, start + place[0] % n)))
        outs.append(pl.BlockSpec((depth, cols), lambda s, place: (0, 0)))
        shapes.append(jax.ShapeDtypeStruct((depth, cols), out_proj.dtype))
    return pl.pallas_call(
        cut_kernel,
        grid_spec=pltpu.PrefetchScalarGridSpec(num_scalar_prefetch=1, grid=(1,), in_specs=ins, out_specs=outs),
        out_shape=shapes,
        compiler_params=params(60),
        cost_estimate=cost(0, 2_000_000),
    )(place, *[out_proj] * len(SPLITS))


def toeplitz_kernel(base_ref, toeplitz_ref):
    tiles, stacked, reach = toeplitz_ref.shape
    per_tile = base_ref.shape[0] // tiles
    tok_len = stacked // per_tile
    for tile in range(tiles):
        for k in range(per_tile):
            g = tile * per_tile + k
            wide = jnp.broadcast_to(base_ref[g : g + 1, :], (tok_len, reach))
            shifted = pltpu.roll(wide, 0, 1, stride=1, stride_axis=0)
            toeplitz_ref[tile, pl.ds(k * tok_len, tok_len), :] = shifted.astype(jnp.bfloat16)


def build_toeplitz(conv_taps, tok_len):
    reach = 2 * tok_len
    per_tile = LANES // GROUP
    tiles = conv_taps.shape[0] // per_tile
    base = jnp.pad(conv_taps[:, ::-1].astype(jnp.float32), ((0, 0), (1, reach - TAPS - 1)))
    shape = jax.ShapeDtypeStruct((tiles, per_tile * tok_len, reach), jnp.bfloat16)
    return pl.pallas_call(
        toeplitz_kernel,
        grid=(1,),
        in_specs=[whole(base)],
        out_specs=whole(shape),
        out_shape=shape,
        compiler_params=params(8),
        cost_estimate=cost(0, 2_000_000),
    )(base)


def panel_kernel(place_ref, mine_ref, other_ref, *refs):
    out_ref = refs[-1]
    count, sharers, tok_len, _ = out_ref.shape
    beside = [ref.at[i] for ref in refs[sharers:-1] for i in range(ref.shape[0])]
    for k in range(sharers):
        total = jnp.dot(mine_ref[...], refs[k][...], preferred_element_type=jnp.float32)
        total += jnp.dot(other_ref[...], beside[k][...], preferred_element_type=jnp.float32)
        for w in range(count):
            out_ref[w, k] = total[w * tok_len : (w + 1) * tok_len].astype(out_ref.dtype)


def panel(place, mine, other, out_proj, beside, split, step, begin=0):
    count, tok_len, depth = mine.shape
    rows = count * tok_len
    unit = out_proj.shape[1] // SIXTEENTHS
    base, extent, order, _ = split
    sharers = len(order)
    piece_cols = extent * unit // sharers
    offset, cols = (part * unit // sharers for part in step)
    fixed = lambda shape: pl.BlockSpec(shape, lambda s, place: (0,) * len(shape))

    def own(k):
        start, per = (base * unit + offset) // cols, piece_cols // cols
        return pl.BlockSpec((depth, cols), lambda s, place: (0, start + (place[0] % sharers ^ k) * per))

    near = lambda a: pl.BlockSpec((a.shape[0], depth, cols), lambda s, place: (0, 0, offset // cols - begin * unit // sharers // cols))
    return pl.pallas_call(
        panel_kernel,
        grid_spec=pltpu.PrefetchScalarGridSpec(
            num_scalar_prefetch=1,
            grid=(1,),
            in_specs=[fixed((rows, depth))] * 2 + [own(k) for k in order] + [near(a) for a in beside],
            out_specs=fixed((count, sharers, tok_len, cols)),
        ),
        out_shape=jax.ShapeDtypeStruct((count, sharers, tok_len, cols), jnp.bfloat16),
        compiler_params=params(),
        cost_estimate=cost(400_000_000, 0),
    )(place, mine.reshape(rows, depth), other.reshape(rows, depth), *[out_proj] * sharers, *beside)


def residual_kernel(ids_ref, rows_ref, out_ref):
    names = lax.broadcasted_iota(jnp.int32, (rows_ref.shape[0], ids_ref.shape[1]), 0)
    one_hot = (names == ids_ref[...]).astype(jnp.float32).astype(jnp.bfloat16)
    out_ref[...] = lax.dot_general(
        one_hot, rows_ref[...], (((0,), (0,)), ((), ())), preferred_element_type=jnp.float32
    ).astype(jnp.bfloat16)


def residual(token_ids, embedding):
    vocab, width = embedding.shape
    tok_len = token_ids.shape[1]
    cols = width // 4
    return pl.pallas_call(
        residual_kernel,
        grid=(4,),
        in_specs=[whole(token_ids), pl.BlockSpec((vocab, cols), lambda i: (0, i))],
        out_specs=pl.BlockSpec((tok_len, cols), lambda i: (0, i)),
        out_shape=jax.ShapeDtypeStruct((tok_len, width), jnp.bfloat16),
        compiler_params=params(),
        cost_estimate=cost(400_000_000, 0),
    )(token_ids, embedding)


def place_kernel(split, step, place_ref, so_far_ref, near_ref, far_ref, out_ref):
    _, sharers, _, cols = near_ref.shape
    piece_cols = so_far_ref.shape[1] // sharers
    offset = step[0] * cols // step[1]
    out_ref[...] = so_far_ref[...]
    for i, k in enumerate(split[2]):
        first = (place_ref[0] % sharers ^ k) * piece_cols + offset
        total = near_ref[0, i].astype(jnp.float32) + far_ref[0, i].astype(jnp.float32)
        at = pl.ds(pl.multiple_of(first, LANES), cols)
        out_ref[:, at] = (so_far_ref[:, at].astype(jnp.float32) + total).astype(jnp.bfloat16)


def place_pieces(place, so_far, near, far, split, step):
    tok_len, width = so_far.shape
    base, extent, _, _ = split
    part = pl.BlockSpec((tok_len, extent * width // SIXTEENTHS), lambda s, place: (0, base // extent))
    one = pl.BlockSpec(near.shape, lambda s, place: (0, 0, 0, 0))
    return pl.pallas_call(
        functools.partial(place_kernel, split, step),
        grid_spec=pltpu.PrefetchScalarGridSpec(
            num_scalar_prefetch=1, grid=(1,), in_specs=[part, one, one], out_specs=part
        ),
        out_shape=jax.ShapeDtypeStruct(so_far.shape, so_far.dtype),
        input_output_aliases={1: 0},
        compiler_params=params(),
        cost_estimate=cost(0, 1_000_000),
    )(place, so_far, near, far)


def add(a, b):
    return (a.astype(jnp.float32) + b.astype(jnp.float32)).astype(jnp.bfloat16)


def per_device(token_ids, embedding, norm_gain, in_proj, short_taps, conv_taps, out_proj):
    tok_len = token_ids.shape[1]
    at = lax.axis_index("ctx").reshape(1).astype(jnp.int32)
    bits = exchange_bits()
    tie = lax.optimization_barrier
    beside_bit = bits[-2]

    early, late = cut_pieces(at, out_proj)
    early, late, conv_taps = tie((early, late, conv_taps))
    toeplitz = build_toeplitz(conv_taps, tok_len)
    ids = level_ids(token_ids, bits[:2])
    ids, toeplitz = tie((ids, toeplitz))
    for group in [bits[i : i + 2] for i in range(2, len(bits), 2)]:
        ids = level_ids(ids, group)
    early, late = swap(early, "fsdp", beside_bit), swap(late, "fsdp", beside_bit)
    ids, embedding_then = tie((ids, embedding))
    ids = with_lead(ids)
    table = project(embedding_then, norm_gain, in_proj)
    table, early = tie((table, early))
    early_pair = jnp.stack([early, swap(early, "ctx", 2)])

    part = ids.shape[0] // 4
    quarters = [ids[n * part : (n + 1) * part] for n in range(4)]
    sent = mix(jnp.concatenate([quarters[3], quarters[1]], axis=0), table, short_taps, toeplitz, tok_len)
    kept, sent = tie((jnp.concatenate([quarters[2], quarters[0]], axis=0), sent))
    other = swap(sent, "fsdp", beside_bit)
    mine = mix(kept, table, short_taps, toeplitz, tok_len)
    middle = early.shape[1] // 2
    mine, early_pair = tie((mine, early_pair))
    pairs = [(columns, swap(columns, "ctx", 1)) for columns in (early_pair[:, :, :middle], early_pair[:, :, middle:])]
    late_pair = jnp.stack([late, swap(late, "ctx", 1)])
    halves = [late_pair[:, :, :middle], late_pair[:, :, middle:]]

    out = residual(token_ids, embedding)
    (head, body), tail = SPLITS[0][3], SPLITS[1][3]
    total = panel(at, mine, other, out_proj, pairs[0], SPLITS[0], head)
    mine, out, halves, total = tie((mine, out, halves, total))
    mine, other = (mine[:part], mine[part:]), (other[:part], other[part:])
    total = total.reshape(2, part, *total.shape[1:])
    for bit in reversed(bits[:-2]):
        half = total.shape[1] // 2
        total = add(total[:, :half], swap(total[:, half:], "fsdp", bit))
    head_sum = (total[1], swap(total[0], "fsdp", bits[-1]), SPLITS[0], head)

    behind = []
    pairs = pairs[1:] + [(columns, swap(columns, "ctx", 2)) for columns in halves]
    steps = [(SPLITS[0], body)] + [(SPLITS[1], step) for step in tail]
    for pair, (split, step) in zip(pairs, steps):
        begin = step[0]
        away = panel(at, mine[0], other[0], out_proj, pair, split, step, begin)
        away, mine = tie((away, mine))
        got = swap(away, "fsdp", bits[-1])
        if behind:
            got, _ = tie((got, behind[-1][-1]))
        total = panel(at, mine[1], other[1], out_proj, pair, split, step, begin)
        for bit in reversed(bits[:-2]):
            half = total.shape[0] // 2
            far = add(total[half:], got[half:])
            total, got = add(total[:half], got[:half]), swap(far, "fsdp", bit)
        behind.append((total, got, split, step, far))
    out = place_pieces(at, out, *head_sum)
    for last in behind:
        out = place_pieces(at, out, *last[:-1])
    return out[None]


def solution(mesh):
    return jax.shard_map(
        per_device,
        mesh=mesh,
        in_specs=(
            P("fsdp", "ctx"),
            P(),
            P(),
            P(None, None, "fsdp"),
            P(None, None, "fsdp"),
            P("fsdp", None),
            P("fsdp", None),
        ),
        out_specs=P("fsdp", "ctx", None),
        check_vma=False,
    )
```

```python
import functools

import jax
import jax.numpy as jnp
from jax import lax
from jax.experimental import pallas as pl
from jax.experimental.pallas import tpu as pltpu
from jax.sharding import PartitionSpec as P

GROUP = 16
TAPS = 128
SHORT = 3
LANES = 128
LEAD = 16
SPLITS = ((0, 8, (0, 2, 1, 3), ((0, 2), (4, 4), (2, 2))), (8, 8, (0, 1, 2, 3), ((0, 4), (4, 4))))
SIXTEENTHS = 16


def from_behind(x, axis, by):
    peers = lax.axis_size(axis)
    return lax.ppermute(x, axis, [(i, (i + by) % peers) for i in range(peers)])


def swap(x, axis, mask):
    peers = lax.axis_size(axis)
    return lax.ppermute(x, axis, [(i, i ^ mask) for i in range(peers)])


def exchange_bits():
    peers = lax.axis_size("fsdp")
    return [1 << b for b in reversed(range(peers.bit_length() - 1))]


def params(mib=24):
    return pltpu.CompilerParams(vmem_limit_bytes=mib * 1024 * 1024)


def cost(flops, bytes_accessed):
    return pl.CostEstimate(flops=flops, bytes_accessed=bytes_accessed, transcendentals=0)


def whole(array):
    return pl.BlockSpec(array.shape, lambda *_: (0,) * len(array.shape))


def level_ids(ids, group):
    masks = [0]
    for bit in group:
        masks += [mask | bit for mask in masks]
    return jnp.concatenate([ids] + [swap(ids, "fsdp", mask) for mask in masks[1:]], axis=0)


def with_lead(ids):
    tok_len = ids.shape[1]
    place = lax.axis_index("ctx")
    one = jnp.where(place >= 1, from_behind(ids, "ctx", 1), -1)
    two = jnp.where(place >= 2, from_behind(ids, "ctx", 2), -1)
    return jnp.concatenate([two[:, tok_len - LEAD :], one, ids], axis=1)


def table_kernel(rows_hbm, weight_hbm, gain_ref, table_ref, rows, weight, row_sems, weight_sems):
    count, width, panel_width = weight.shape
    parts, blocks = row_sems.shape[0], weight_sems.shape[1]
    each, deep = rows.shape[0] // parts, width // blocks
    row_copies = [
        pltpu.make_async_copy(rows_hbm.at[pl.ds(r * each, each)], rows.at[pl.ds(r * each, each)], row_sems.at[r])
        for r in range(parts)
    ]
    weight_copies = [
        [
            pltpu.make_async_copy(
                weight_hbm.at[i, pl.ds(k * deep, deep)], weight.at[i, pl.ds(k * deep, deep)], weight_sems.at[i, k]
            )
            for k in range(blocks)
        ]
        for i in range(count)
    ]
    for copy in row_copies + sum(weight_copies, []):
        copy.start()
    for r in range(parts):
        row_copies[r].wait()
        at = pl.ds(r * each, each)
        values = rows[at, :].astype(jnp.float32)
        inverse_rms = lax.rsqrt(jnp.mean(values * values, axis=-1, keepdims=True) + 1e-06)
        rows[at, :] = (values * inverse_rms * gain_ref[...]).astype(jnp.bfloat16)
    cols = min(256, panel_width)
    for i in range(count):
        for copy in weight_copies[i]:
            copy.wait()
        for first in range(0, panel_width, cols):
            at = slice(first, first + cols)
            part = jnp.dot(rows[...], weight[i, :, at], preferred_element_type=jnp.float32)
            table_ref[i, :, at] = part.astype(jnp.bfloat16)


def project(embedding, norm_gain, in_proj):
    vocab, width = embedding.shape
    count, _, panel_width = in_proj.shape
    hbm = pl.BlockSpec(memory_space=pltpu.HBM)
    shape = jax.ShapeDtypeStruct((count, vocab, panel_width), jnp.bfloat16)
    return pl.pallas_call(
        table_kernel,
        grid=(1,),
        in_specs=[hbm, hbm, pl.BlockSpec((1, width), lambda s: (0, 0))],
        out_specs=whole(shape),
        out_shape=shape,
        scratch_shapes=[
            pltpu.VMEM(embedding.shape, jnp.bfloat16),
            pltpu.VMEM(in_proj.shape, jnp.bfloat16),
            pltpu.SemaphoreType.DMA((8,)),
            pltpu.SemaphoreType.DMA((count, 4)),
        ],
        compiler_params=params(40),
        cost_estimate=cost(3_000_000_000, 0),
    )(embedding, in_proj, norm_gain.reshape(1, width))


def mixer_kernel(ids_ref, table_ref, short_ref, toeplitz, gated_ref, held_query, held):
    tok_len, panel_width = gated_ref.shape[1:]
    vocab = table_ref.shape[1]
    rows = ids_ref.shape[2]
    reach = 2 * tok_len
    lead = rows - reach
    tiles = panel_width // LANES
    per_tile = LANES // GROUP
    names = lax.broadcasted_iota(jnp.int32, (vocab, rows), 0)
    lane_group = lax.broadcasted_iota(jnp.int32, (tok_len, 2 * LANES), 1) % LANES // GROUP

    def look_up(one_hot, table):
        found = lax.dot_general(one_hot, table, (((0,), (0,)), ((), ())), preferred_element_type=jnp.float32)
        return found.astype(jnp.bfloat16).astype(jnp.float32)

    for v in range(2):
        one_hot = (names == ids_ref[v]).astype(jnp.float32).astype(jnp.bfloat16)
        held[v, 0] = look_up(one_hot, table_ref[1])
        held[v, 1] = look_up(one_hot, table_ref[2])
        held_query[v] = look_up(one_hot[:, rows - lead - tok_len :], table_ref[0])

    def featured(source, i, count, cols):
        total = short_ref[0, i : i + 1, cols] * source[pl.ds(lead, count), cols]
        for j in range(1, SHORT):
            total += short_ref[j, i : i + 1, cols] * source[pl.ds(lead - j, count), cols]
        return total

    for tile in range(tiles):
        cols = slice(tile * LANES, (tile + 1) * LANES)
        products = []
        for v in range(2):
            key = featured(held.at[v, 0], 1, reach, cols)
            value = featured(held.at[v, 1], 2, reach, cols)
            products.append((key * value).astype(jnp.bfloat16))
        both = jnp.concatenate(products, axis=1)
        filtered = None
        for k in range(per_tile):
            one = jnp.dot(
                toeplitz[tile, pl.ds(k * tok_len, tok_len), :], both, preferred_element_type=jnp.float32
            )
            filtered = one if k == 0 else jnp.where(lane_group == k, one, filtered)
        for v in range(2):
            query = featured(held_query.at[v], 0, tok_len, cols)
            gated_ref[v, :, cols] = (query * filtered[:, v * LANES : (v + 1) * LANES]).astype(jnp.bfloat16)


def mix(ids, table, short_taps, toeplitz, tok_len):
    windows, rows = ids.shape
    panel_width = table.shape[2]
    return pl.pallas_call(
        mixer_kernel,
        grid=(windows // 2,),
        in_specs=[pl.BlockSpec((2, 1, rows), lambda p: (p, 0, 0))]
        + [whole(array) for array in (table, short_taps, toeplitz)],
        out_specs=pl.BlockSpec((2, tok_len, panel_width), lambda p: (p, 0, 0)),
        out_shape=jax.ShapeDtypeStruct((windows, tok_len, panel_width), jnp.bfloat16),
        scratch_shapes=[
            pltpu.VMEM((2, LEAD + tok_len, panel_width), jnp.float32),
            pltpu.VMEM((2, 2, rows, panel_width), jnp.float32),
        ],
        compiler_params=params(),
        cost_estimate=cost(1_500_000_000, 0),
    )(ids.reshape(windows, 1, rows), table, short_taps, toeplitz)


def cut_kernel(place_ref, *refs):
    count = len(refs) // 2
    for source, piece in zip(refs[:count], refs[count:]):
        piece[...] = source[...]


def cut_pieces(place, out_proj):
    depth, width = out_proj.shape
    unit = width // SIXTEENTHS
    ins, outs, shapes = [], [], []
    for first, extent, order, _ in SPLITS:
        sharers = len(order)
        cols = extent * unit // sharers
        start = first * unit // cols
        ins.append(pl.BlockSpec((depth, cols), lambda s, place, start=start, n=sharers: (0, start + place[0] % n)))
        outs.append(pl.BlockSpec((depth, cols), lambda s, place: (0, 0)))
        shapes.append(jax.ShapeDtypeStruct((depth, cols), out_proj.dtype))
    return pl.pallas_call(
        cut_kernel,
        grid_spec=pltpu.PrefetchScalarGridSpec(num_scalar_prefetch=1, grid=(1,), in_specs=ins, out_specs=outs),
        out_shape=shapes,
        compiler_params=params(60),
        cost_estimate=cost(0, 2_000_000),
    )(place, *[out_proj] * len(SPLITS))


def toeplitz_kernel(base_ref, toeplitz_ref):
    tiles, stacked, reach = toeplitz_ref.shape
    per_tile = base_ref.shape[0] // tiles
    tok_len = stacked // per_tile
    for tile in range(tiles):
        for k in range(per_tile):
            g = tile * per_tile + k
            wide = jnp.broadcast_to(base_ref[g : g + 1, :], (tok_len, reach))
            shifted = pltpu.roll(wide, 0, 1, stride=1, stride_axis=0)
            toeplitz_ref[tile, pl.ds(k * tok_len, tok_len), :] = shifted.astype(jnp.bfloat16)


def build_toeplitz(conv_taps, tok_len):
    reach = 2 * tok_len
    per_tile = LANES // GROUP
    tiles = conv_taps.shape[0] // per_tile
    base = jnp.pad(conv_taps[:, ::-1].astype(jnp.float32), ((0, 0), (1, reach - TAPS - 1)))
    shape = jax.ShapeDtypeStruct((tiles, per_tile * tok_len, reach), jnp.bfloat16)
    return pl.pallas_call(
        toeplitz_kernel,
        grid=(1,),
        in_specs=[whole(base)],
        out_specs=whole(shape),
        out_shape=shape,
        compiler_params=params(8),
        cost_estimate=cost(0, 2_000_000),
    )(base)


def panel_kernel(place_ref, mine_ref, other_ref, *refs):
    out_ref = refs[-1]
    count, sharers, tok_len, _ = out_ref.shape
    beside = [ref.at[i] for ref in refs[sharers:-1] for i in range(ref.shape[0])]
    for k in range(sharers):
        total = jnp.dot(mine_ref[...], refs[k][...], preferred_element_type=jnp.float32)
        total += jnp.dot(other_ref[...], beside[k][...], preferred_element_type=jnp.float32)
        for w in range(count):
            out_ref[w, k] = total[w * tok_len : (w + 1) * tok_len].astype(out_ref.dtype)


def panel(place, mine, other, out_proj, beside, split, step, begin=0):
    count, tok_len, depth = mine.shape
    rows = count * tok_len
    unit = out_proj.shape[1] // SIXTEENTHS
    base, extent, order, _ = split
    sharers = len(order)
    piece_cols = extent * unit // sharers
    offset, cols = (part * unit // sharers for part in step)
    fixed = lambda shape: pl.BlockSpec(shape, lambda s, place: (0,) * len(shape))

    def own(k):
        start, per = (base * unit + offset) // cols, piece_cols // cols
        return pl.BlockSpec((depth, cols), lambda s, place: (0, start + (place[0] % sharers ^ k) * per))

    near = lambda a: pl.BlockSpec((a.shape[0], depth, cols), lambda s, place: (0, 0, offset // cols - begin * unit // sharers // cols))
    return pl.pallas_call(
        panel_kernel,
        grid_spec=pltpu.PrefetchScalarGridSpec(
            num_scalar_prefetch=1,
            grid=(1,),
            in_specs=[fixed((rows, depth))] * 2 + [own(k) for k in order] + [near(a) for a in beside],
            out_specs=fixed((count, sharers, tok_len, cols)),
        ),
        out_shape=jax.ShapeDtypeStruct((count, sharers, tok_len, cols), jnp.bfloat16),
        compiler_params=params(),
        cost_estimate=cost(400_000_000, 0),
    )(place, mine.reshape(rows, depth), other.reshape(rows, depth), *[out_proj] * sharers, *beside)


def residual_kernel(ids_ref, rows_ref, out_ref):
    names = lax.broadcasted_iota(jnp.int32, (rows_ref.shape[0], ids_ref.shape[1]), 0)
    one_hot = (names == ids_ref[...]).astype(jnp.float32).astype(jnp.bfloat16)
    out_ref[...] = lax.dot_general(
        one_hot, rows_ref[...], (((0,), (0,)), ((), ())), preferred_element_type=jnp.float32
    ).astype(jnp.bfloat16)


def residual(token_ids, embedding):
    vocab, width = embedding.shape
    tok_len = token_ids.shape[1]
    cols = width // 4
    return pl.pallas_call(
        residual_kernel,
        grid=(4,),
        in_specs=[whole(token_ids), pl.BlockSpec((vocab, cols), lambda i: (0, i))],
        out_specs=pl.BlockSpec((tok_len, cols), lambda i: (0, i)),
        out_shape=jax.ShapeDtypeStruct((tok_len, width), jnp.bfloat16),
        compiler_params=params(),
        cost_estimate=cost(400_000_000, 0),
    )(token_ids, embedding)


def place_kernel(split, step, place_ref, so_far_ref, near_ref, far_ref, out_ref):
    _, sharers, _, cols = near_ref.shape
    piece_cols = so_far_ref.shape[1] // sharers
    offset = step[0] * cols // step[1]
    out_ref[...] = so_far_ref[...]
    for i, k in enumerate(split[2]):
        first = (place_ref[0] % sharers ^ k) * piece_cols + offset
        total = near_ref[0, i].astype(jnp.float32) + far_ref[0, i].astype(jnp.float32)
        at = pl.ds(pl.multiple_of(first, LANES), cols)
        out_ref[:, at] = (so_far_ref[:, at].astype(jnp.float32) + total).astype(jnp.bfloat16)


def place_pieces(place, so_far, near, far, split, step):
    tok_len, width = so_far.shape
    base, extent, _, _ = split
    part = pl.BlockSpec((tok_len, extent * width // SIXTEENTHS), lambda s, place: (0, base // extent))
    one = pl.BlockSpec(near.shape, lambda s, place: (0, 0, 0, 0))
    return pl.pallas_call(
        functools.partial(place_kernel, split, step),
        grid_spec=pltpu.PrefetchScalarGridSpec(
            num_scalar_prefetch=1, grid=(1,), in_specs=[part, one, one], out_specs=part
        ),
        out_shape=jax.ShapeDtypeStruct(so_far.shape, so_far.dtype),
        input_output_aliases={1: 0},
        compiler_params=params(),
        cost_estimate=cost(0, 1_000_000),
    )(place, so_far, near, far)


def add(a, b):
    return (a.astype(jnp.float32) + b.astype(jnp.float32)).astype(jnp.bfloat16)


def per_device(token_ids, embedding, norm_gain, in_proj, short_taps, conv_taps, out_proj):
    tok_len = token_ids.shape[1]
    at = lax.axis_index("ctx").reshape(1).astype(jnp.int32)
    bits = exchange_bits()
    tie = lax.optimization_barrier
    beside_bit = bits[-2]

    early, late = cut_pieces(at, out_proj)
    early, late, conv_taps = tie((early, late, conv_taps))
    toeplitz = build_toeplitz(conv_taps, tok_len)
    ids = level_ids(token_ids, bits[:2])
    ids, toeplitz = tie((ids, toeplitz))
    for group in [bits[i : i + 2] for i in range(2, len(bits), 2)]:
        ids = level_ids(ids, group)
    early, late = swap(early, "fsdp", beside_bit), swap(late, "fsdp", beside_bit)
    ids, embedding_then = tie((ids, embedding))
    ids = with_lead(ids)
    table = project(embedding_then, norm_gain, in_proj)
    table, early = tie((table, early))
    early_pair = jnp.stack([early, swap(early, "ctx", 2)])

    part = ids.shape[0] // 4
    quarters = [ids[n * part : (n + 1) * part] for n in range(4)]
    sent = mix(jnp.concatenate([quarters[3], quarters[1]], axis=0), table, short_taps, toeplitz, tok_len)
    kept, sent = tie((jnp.concatenate([quarters[2], quarters[0]], axis=0), sent))
    other = swap(sent, "fsdp", beside_bit)
    mine = mix(kept, table, short_taps, toeplitz, tok_len)
    middle = early.shape[1] // 2
    mine, early_pair = tie((mine, early_pair))
    late_pair = jnp.stack([late, swap(late, "ctx", 1)])
    pairs = [(columns, swap(columns, "ctx", 1)) for columns in (early_pair[:, :, :middle], early_pair[:, :, middle:])]

    own_ids, mine = tie((token_ids, mine))
    out = residual(own_ids, embedding)
    late_pair, out = tie((late_pair, out))
    pairs.append((late_pair[:, :, :middle], swap(late_pair[:, :, :middle], "ctx", 2)))
    (head, body, foot), tail = SPLITS[0][3], SPLITS[1][3]
    total = panel(at, mine, other, out_proj, pairs[0], SPLITS[0], head)
    mine, out, total = tie((mine, out, total))
    mine, other = (mine[:part], mine[part:]), (other[:part], other[part:])
    total = total.reshape(2, part, *total.shape[1:])
    for bit in reversed(bits[:-2]):
        half = total.shape[1] // 2
        got = swap(total[:, half:], "fsdp", bit)
        total = add(total[:, :half], got)
    head_sum = (total[1], swap(total[0], "fsdp", bits[-1]), SPLITS[0], head)

    behind = [(got,)]
    for number in range(4):
        if number == 0:
            pair, split, step, begin = pairs[1], SPLITS[0], body, body[0]
        elif number < 3:
            pair, split, step = pairs[number + 1], SPLITS[1], tail[number - 1]
            begin = step[0]
        else:
            pair, split, step, begin = pairs[0], SPLITS[0], foot, 0
        if number:
            mine, _ = tie((mine, behind[number - 1][0]))
        away = panel(at, mine[0], other[0], out_proj, pair, split, step, begin)
        if number == 0:
            rest, _ = tie((late_pair[:, :, middle:], away))
            pairs.append((rest, swap(rest, "ctx", 2)))
        got = swap(away, "fsdp", bits[-1])
        total = panel(at, mine[1], other[1], out_proj, pair, split, step, begin)
        for bit in reversed(bits[:-2]):
            half = total.shape[0] // 2
            far = add(total[half:], got[half:])
            total, got = add(total[:half], got[:half]), swap(far, "fsdp", bit)
        behind.append((got, total, split, step))
    out = place_pieces(at, out, *head_sum)
    for far, near, split, step in behind[1:]:
        out = place_pieces(at, out, near, far, split, step)
    return out[None]


def solution(mesh):
    return jax.shard_map(
        per_device,
        mesh=mesh,
        in_specs=(
            P("fsdp", "ctx"),
            P(),
            P(),
            P(None, None, "fsdp"),
            P(None, None, "fsdp"),
            P("fsdp", None),
            P("fsdp", None),
        ),
        out_specs=P("fsdp", "ctx", None),
        check_vma=False,
    )
```

```python
import functools

import jax
import jax.numpy as jnp
from jax import lax
from jax.experimental import pallas as pl
from jax.experimental.pallas import tpu as pltpu
from jax.sharding import PartitionSpec as P

GROUP = 16
TAPS = 128
SHORT = 3
LANES = 128
LEAD = 16
SPLITS = ((0, 8, (0, 2, 1, 3), ((0, 2), (4, 4), (2, 2))), (8, 8, (0, 1, 2, 3), ((0, 4), (4, 4))))
SIXTEENTHS = 16


def from_behind(x, axis, by):
    peers = lax.axis_size(axis)
    return lax.ppermute(x, axis, [(i, (i + by) % peers) for i in range(peers)])


def swap(x, axis, mask):
    peers = lax.axis_size(axis)
    return lax.ppermute(x, axis, [(i, i ^ mask) for i in range(peers)])


def exchange_bits():
    peers = lax.axis_size("fsdp")
    return [1 << b for b in reversed(range(peers.bit_length() - 1))]


def params(mib=24):
    return pltpu.CompilerParams(vmem_limit_bytes=mib * 1024 * 1024)


def cost(flops, bytes_accessed):
    return pl.CostEstimate(flops=flops, bytes_accessed=bytes_accessed, transcendentals=0)


def whole(array):
    return pl.BlockSpec(array.shape, lambda *_: (0,) * len(array.shape))


def level_ids(ids, group):
    masks = [0]
    for bit in group:
        masks += [mask | bit for mask in masks]
    return jnp.concatenate([ids] + [swap(ids, "fsdp", mask) for mask in masks[1:]], axis=0)


def with_lead(ids):
    tok_len = ids.shape[1]
    place = lax.axis_index("ctx")
    one = jnp.where(place >= 1, from_behind(ids, "ctx", 1), -1)
    two = jnp.where(place >= 2, from_behind(ids, "ctx", 2), -1)
    return jnp.concatenate([two[:, tok_len - LEAD :], one, ids], axis=1)


def table_kernel(rows_hbm, weight_hbm, gain_ref, table_ref, rows, weight, row_sems, weight_sems):
    count, width, panel_width = weight.shape
    parts, blocks = row_sems.shape[0], weight_sems.shape[1]
    each, deep = rows.shape[0] // parts, width // blocks
    row_copies = [
        pltpu.make_async_copy(rows_hbm.at[pl.ds(r * each, each)], rows.at[pl.ds(r * each, each)], row_sems.at[r])
        for r in range(parts)
    ]
    weight_copies = [
        [
            pltpu.make_async_copy(
                weight_hbm.at[i, pl.ds(k * deep, deep)], weight.at[i, pl.ds(k * deep, deep)], weight_sems.at[i, k]
            )
            for k in range(blocks)
        ]
        for i in range(count)
    ]
    for copy in row_copies + sum(weight_copies, []):
        copy.start()
    for r in range(parts):
        row_copies[r].wait()
        at = pl.ds(r * each, each)
        values = rows[at, :].astype(jnp.float32)
        inverse_rms = lax.rsqrt(jnp.mean(values * values, axis=-1, keepdims=True) + 1e-06)
        rows[at, :] = (values * inverse_rms * gain_ref[...]).astype(jnp.bfloat16)
    cols = min(256, panel_width)
    for i in range(count):
        for copy in weight_copies[i]:
            copy.wait()
        for first in range(0, panel_width, cols):
            at = slice(first, first + cols)
            part = jnp.dot(rows[...], weight[i, :, at], preferred_element_type=jnp.float32)
            table_ref[i, :, at] = part.astype(jnp.bfloat16)


def project(embedding, norm_gain, in_proj):
    vocab, width = embedding.shape
    count, _, panel_width = in_proj.shape
    hbm = pl.BlockSpec(memory_space=pltpu.HBM)
    shape = jax.ShapeDtypeStruct((count, vocab, panel_width), jnp.bfloat16)
    return pl.pallas_call(
        table_kernel,
        grid=(1,),
        in_specs=[hbm, hbm, pl.BlockSpec((1, width), lambda s: (0, 0))],
        out_specs=whole(shape),
        out_shape=shape,
        scratch_shapes=[
            pltpu.VMEM(embedding.shape, jnp.bfloat16),
            pltpu.VMEM(in_proj.shape, jnp.bfloat16),
            pltpu.SemaphoreType.DMA((8,)),
            pltpu.SemaphoreType.DMA((count, 4)),
        ],
        compiler_params=params(40),
        cost_estimate=cost(3_000_000_000, 0),
    )(embedding, in_proj, norm_gain.reshape(1, width))


def mixer_kernel(ids_ref, table_ref, short_ref, toeplitz, gated_ref, held_query, held):
    tok_len, panel_width = gated_ref.shape[1:]
    vocab = table_ref.shape[1]
    rows = ids_ref.shape[2]
    reach = 2 * tok_len
    lead = rows - reach
    tiles = panel_width // LANES
    per_tile = LANES // GROUP
    names = lax.broadcasted_iota(jnp.int32, (vocab, rows), 0)
    lane_group = lax.broadcasted_iota(jnp.int32, (tok_len, 2 * LANES), 1) % LANES // GROUP

    def look_up(one_hot, table):
        found = lax.dot_general(one_hot, table, (((0,), (0,)), ((), ())), preferred_element_type=jnp.float32)
        return found.astype(jnp.bfloat16).astype(jnp.float32)

    for v in range(2):
        one_hot = (names == ids_ref[v]).astype(jnp.float32).astype(jnp.bfloat16)
        held[v, 0] = look_up(one_hot, table_ref[1])
        held[v, 1] = look_up(one_hot, table_ref[2])
        held_query[v] = look_up(one_hot[:, rows - lead - tok_len :], table_ref[0])

    def featured(source, i, count, cols):
        total = short_ref[0, i : i + 1, cols] * source[pl.ds(lead, count), cols]
        for j in range(1, SHORT):
            total += short_ref[j, i : i + 1, cols] * source[pl.ds(lead - j, count), cols]
        return total

    for tile in range(tiles):
        cols = slice(tile * LANES, (tile + 1) * LANES)
        products = []
        for v in range(2):
            key = featured(held.at[v, 0], 1, reach, cols)
            value = featured(held.at[v, 1], 2, reach, cols)
            products.append((key * value).astype(jnp.bfloat16))
        both = jnp.concatenate(products, axis=1)
        filtered = None
        for k in range(per_tile):
            one = jnp.dot(
                toeplitz[tile, pl.ds(k * tok_len, tok_len), :], both, preferred_element_type=jnp.float32
            )
            filtered = one if k == 0 else jnp.where(lane_group == k, one, filtered)
        for v in range(2):
            query = featured(held_query.at[v], 0, tok_len, cols)
            gated_ref[v, :, cols] = (query * filtered[:, v * LANES : (v + 1) * LANES]).astype(jnp.bfloat16)


def mix(ids, table, short_taps, toeplitz, tok_len):
    windows, rows = ids.shape
    panel_width = table.shape[2]
    return pl.pallas_call(
        mixer_kernel,
        grid=(windows // 2,),
        in_specs=[pl.BlockSpec((2, 1, rows), lambda p: (p, 0, 0))]
        + [whole(array) for array in (table, short_taps, toeplitz)],
        out_specs=pl.BlockSpec((2, tok_len, panel_width), lambda p: (p, 0, 0)),
        out_shape=jax.ShapeDtypeStruct((windows, tok_len, panel_width), jnp.bfloat16),
        scratch_shapes=[
            pltpu.VMEM((2, LEAD + tok_len, panel_width), jnp.float32),
            pltpu.VMEM((2, 2, rows, panel_width), jnp.float32),
        ],
        compiler_params=params(),
        cost_estimate=cost(1_500_000_000, 0),
    )(ids.reshape(windows, 1, rows), table, short_taps, toeplitz)


def cut_kernel(place_ref, *refs):
    count = len(refs) // 2
    for source, piece in zip(refs[:count], refs[count:]):
        piece[...] = source[...]


def cut_pieces(place, out_proj):
    depth, width = out_proj.shape
    unit = width // SIXTEENTHS
    ins, outs, shapes = [], [], []
    for first, extent, order, _ in SPLITS:
        sharers = len(order)
        cols = extent * unit // sharers
        start = first * unit // cols
        ins.append(pl.BlockSpec((depth, cols), lambda s, place, start=start, n=sharers: (0, start + place[0] % n)))
        outs.append(pl.BlockSpec((depth, cols), lambda s, place: (0, 0)))
        shapes.append(jax.ShapeDtypeStruct((depth, cols), out_proj.dtype))
    return pl.pallas_call(
        cut_kernel,
        grid_spec=pltpu.PrefetchScalarGridSpec(num_scalar_prefetch=1, grid=(1,), in_specs=ins, out_specs=outs),
        out_shape=shapes,
        compiler_params=params(60),
        cost_estimate=cost(0, 2_000_000),
    )(place, *[out_proj] * len(SPLITS))


def toeplitz_kernel(base_ref, toeplitz_ref):
    tiles, stacked, reach = toeplitz_ref.shape
    per_tile = base_ref.shape[0] // tiles
    tok_len = stacked // per_tile
    for tile in range(tiles):
        for k in range(per_tile):
            g = tile * per_tile + k
            wide = jnp.broadcast_to(base_ref[g : g + 1, :], (tok_len, reach))
            shifted = pltpu.roll(wide, 0, 1, stride=1, stride_axis=0)
            toeplitz_ref[tile, pl.ds(k * tok_len, tok_len), :] = shifted.astype(jnp.bfloat16)


def build_toeplitz(conv_taps, tok_len):
    reach = 2 * tok_len
    per_tile = LANES // GROUP
    tiles = conv_taps.shape[0] // per_tile
    base = jnp.pad(conv_taps[:, ::-1].astype(jnp.float32), ((0, 0), (1, reach - TAPS - 1)))
    shape = jax.ShapeDtypeStruct((tiles, per_tile * tok_len, reach), jnp.bfloat16)
    return pl.pallas_call(
        toeplitz_kernel,
        grid=(1,),
        in_specs=[whole(base)],
        out_specs=whole(shape),
        out_shape=shape,
        compiler_params=params(8),
        cost_estimate=cost(0, 2_000_000),
    )(base)


def panel_kernel(place_ref, mine_ref, other_ref, *refs):
    out_ref = refs[-1]
    count, sharers, tok_len, _ = out_ref.shape
    beside = [ref.at[i] for ref in refs[sharers:-1] for i in range(ref.shape[0])]
    for k in range(sharers):
        total = jnp.dot(mine_ref[...], refs[k][...], preferred_element_type=jnp.float32)
        total += jnp.dot(other_ref[...], beside[k][...], preferred_element_type=jnp.float32)
        for w in range(count):
            out_ref[w, k] = total[w * tok_len : (w + 1) * tok_len].astype(out_ref.dtype)


def panel(place, mine, other, out_proj, beside, split, step, begin=0):
    count, tok_len, depth = mine.shape
    rows = count * tok_len
    unit = out_proj.shape[1] // SIXTEENTHS
    base, extent, order, _ = split
    sharers = len(order)
    piece_cols = extent * unit // sharers
    offset, cols = (part * unit // sharers for part in step)
    fixed = lambda shape: pl.BlockSpec(shape, lambda s, place: (0,) * len(shape))

    def own(k):
        start, per = (base * unit + offset) // cols, piece_cols // cols
        return pl.BlockSpec((depth, cols), lambda s, place: (0, start + (place[0] % sharers ^ k) * per))

    near = lambda a: pl.BlockSpec((a.shape[0], depth, cols), lambda s, place: (0, 0, offset // cols - begin * unit // sharers // cols))
    return pl.pallas_call(
        panel_kernel,
        grid_spec=pltpu.PrefetchScalarGridSpec(
            num_scalar_prefetch=1,
            grid=(1,),
            in_specs=[fixed((rows, depth))] * 2 + [own(k) for k in order] + [near(a) for a in beside],
            out_specs=fixed((count, sharers, tok_len, cols)),
        ),
        out_shape=jax.ShapeDtypeStruct((count, sharers, tok_len, cols), jnp.bfloat16),
        compiler_params=params(),
        cost_estimate=cost(400_000_000, 0),
    )(place, mine.reshape(rows, depth), other.reshape(rows, depth), *[out_proj] * sharers, *beside)


def residual_kernel(ids_ref, rows_ref, out_ref):
    names = lax.broadcasted_iota(jnp.int32, (rows_ref.shape[0], ids_ref.shape[1]), 0)
    one_hot = (names == ids_ref[...]).astype(jnp.float32).astype(jnp.bfloat16)
    out_ref[...] = lax.dot_general(
        one_hot, rows_ref[...], (((0,), (0,)), ((), ())), preferred_element_type=jnp.float32
    ).astype(jnp.bfloat16)


def residual(token_ids, embedding):
    vocab, width = embedding.shape
    tok_len = token_ids.shape[1]
    cols = width // 4
    return pl.pallas_call(
        residual_kernel,
        grid=(4,),
        in_specs=[whole(token_ids), pl.BlockSpec((vocab, cols), lambda i: (0, i))],
        out_specs=pl.BlockSpec((tok_len, cols), lambda i: (0, i)),
        out_shape=jax.ShapeDtypeStruct((tok_len, width), jnp.bfloat16),
        compiler_params=params(),
        cost_estimate=cost(400_000_000, 0),
    )(token_ids, embedding)


def place_kernel(split, step, place_ref, so_far_ref, near_ref, far_ref, out_ref):
    _, sharers, _, cols = near_ref.shape
    piece_cols = so_far_ref.shape[1] // sharers
    offset = step[0] * cols // step[1]
    out_ref[...] = so_far_ref[...]
    for i, k in enumerate(split[2]):
        first = (place_ref[0] % sharers ^ k) * piece_cols + offset
        total = near_ref[0, i].astype(jnp.float32) + far_ref[0, i].astype(jnp.float32)
        at = pl.ds(pl.multiple_of(first, LANES), cols)
        out_ref[:, at] = (so_far_ref[:, at].astype(jnp.float32) + total).astype(jnp.bfloat16)


def place_pieces(place, so_far, near, far, split, step):
    tok_len, width = so_far.shape
    base, extent, _, _ = split
    part = pl.BlockSpec((tok_len, extent * width // SIXTEENTHS), lambda s, place: (0, base // extent))
    one = pl.BlockSpec(near.shape, lambda s, place: (0, 0, 0, 0))
    return pl.pallas_call(
        functools.partial(place_kernel, split, step),
        grid_spec=pltpu.PrefetchScalarGridSpec(
            num_scalar_prefetch=1, grid=(1,), in_specs=[part, one, one], out_specs=part
        ),
        out_shape=jax.ShapeDtypeStruct(so_far.shape, so_far.dtype),
        input_output_aliases={1: 0},
        compiler_params=params(),
        cost_estimate=cost(0, 1_000_000),
    )(place, so_far, near, far)


def add(a, b):
    return (a.astype(jnp.float32) + b.astype(jnp.float32)).astype(jnp.bfloat16)


def per_device(token_ids, embedding, norm_gain, in_proj, short_taps, conv_taps, out_proj):
    tok_len = token_ids.shape[1]
    at = lax.axis_index("ctx").reshape(1).astype(jnp.int32)
    bits = exchange_bits()
    tie = lax.optimization_barrier
    beside_bit = bits[-2]

    early, late = cut_pieces(at, out_proj)
    early, late, conv_taps = tie((early, late, conv_taps))
    toeplitz = build_toeplitz(conv_taps, tok_len)
    ids = level_ids(token_ids, bits[:2])
    ids, toeplitz = tie((ids, toeplitz))
    for group in [bits[i : i + 2] for i in range(2, len(bits), 2)]:
        ids = level_ids(ids, group)
    early, late = swap(early, "fsdp", beside_bit), swap(late, "fsdp", beside_bit)
    ids, embedding_then = tie((ids, embedding))
    ids = with_lead(ids)
    table = project(embedding_then, norm_gain, in_proj)
    table, early = tie((table, early))
    early_pair = jnp.stack([early, swap(early, "ctx", 2)])

    part = ids.shape[0] // 4
    quarters = [ids[n * part : (n + 1) * part] for n in range(4)]
    sent = mix(quarters[3], table, short_taps, toeplitz, tok_len)
    kept, sent = tie((jnp.concatenate([quarters[1], quarters[2], quarters[0]], axis=0), sent))
    other = [swap(sent, "fsdp", beside_bit)]
    gated = mix(kept, table, short_taps, toeplitz, tok_len)
    gated, early_pair = tie((gated, early_pair))
    other.append(swap(gated[:part], "fsdp", beside_bit))
    mine = [gated[part : 2 * part], gated[2 * part :]]
    middle = early.shape[1] // 2
    pairs = [(columns, swap(columns, "ctx", 1)) for columns in (early_pair[:, :, :middle], early_pair[:, :, middle:])]
    late_pair = jnp.stack([late, swap(late, "ctx", 1)])
    own_ids, gated = tie((token_ids, gated))
    out = residual(own_ids, embedding)
    late_pair, out = tie((late_pair, out))
    pairs += [(columns, swap(columns, "ctx", 2)) for columns in (late_pair[:, :, :middle],)]
    (head, body, foot), tail = SPLITS[0][3], SPLITS[1][3]

    def send(pair, split, step, begin):
        away = panel(at, mine[0], other[0], out_proj, pair, split, step, begin)
        return away, swap(away, "fsdp", bits[-1])

    def sum_up(pair, split, step, begin, got):
        total = panel(at, mine[1], other[1], out_proj, pair, split, step, begin)
        for bit in reversed(bits[:-2]):
            half = total.shape[0] // 2
            far = add(total[half:], got[half:])
            total, got = add(total[:half], got[:half]), swap(far, "fsdp", bit)
        return far, (total, got, split, step)

    chunk = (pairs[1], SPLITS[0], body, body[0])
    away, got = send(*chunk)
    other[1], late_rest, _ = tie((other[1], late_pair[:, :, middle:], away))
    pairs.append((late_rest, swap(late_rest, "ctx", 2)))

    all_mine, all_other = (jnp.concatenate(parts, axis=0) for parts in (mine, other))
    total = panel(at, all_mine, all_other, out_proj, pairs[0], SPLITS[0], head)
    other[1], total = tie((other[1], total))
    total = total.reshape(2, part, *total.shape[1:])
    head_got = swap(total[:, part // 2 :], "fsdp", bits[-3])

    far, first_sum = sum_up(*chunk, got)
    mine[0], _ = tie((mine[0], far))
    head_got, _ = tie((head_got, far))
    total = add(total[:, : part // 2], head_got)
    for bit in reversed(bits[:-3]):
        half = total.shape[1] // 2
        total = add(total[:, :half], swap(total[:, half:], "fsdp", bit))
    head_sum = (total[1], swap(total[0], "fsdp", bits[-1]), SPLITS[0], head)
    sums = [first_sum]
    for pair, split, step, begin in (
        (pairs[2], SPLITS[1], tail[0], tail[0][0]),
        (pairs[3], SPLITS[1], tail[1], tail[1][0]),
        (pairs[0], SPLITS[0], foot, 0),
    ):
        away, got = send(pair, split, step, begin)
        mine[0], away = tie((mine[0], away))
        got, _ = tie((got, far))
        far, one = sum_up(pair, split, step, begin, got)
        sums.append(one)
    out = place_pieces(at, out, *head_sum)
    for one in sums:
        out = place_pieces(at, out, *one)
    return out[None]


def solution(mesh):
    return jax.shard_map(
        per_device,
        mesh=mesh,
        in_specs=(
            P("fsdp", "ctx"),
            P(),
            P(),
            P(None, None, "fsdp"),
            P(None, None, "fsdp"),
            P("fsdp", None),
            P("fsdp", None),
        ),
        out_specs=P("fsdp", "ctx", None),
        check_vma=False,
    )
```

```python
import functools

import jax
import jax.numpy as jnp
from jax import lax
from jax.experimental import pallas as pl
from jax.experimental.pallas import tpu as pltpu
from jax.sharding import PartitionSpec as P

GROUP = 16
TAPS = 128
SHORT = 3
LANES = 128
LEAD = 16
SPLITS = ((0, 8, (0, 2, 1, 3), ((0, 2), (4, 4), (2, 2))), (8, 8, (0, 1, 2, 3), ((0, 4), (4, 4))))
SIXTEENTHS = 16


def from_behind(x, axis, by):
    peers = lax.axis_size(axis)
    return lax.ppermute(x, axis, [(i, (i + by) % peers) for i in range(peers)])


def swap(x, axis, mask):
    peers = lax.axis_size(axis)
    return lax.ppermute(x, axis, [(i, i ^ mask) for i in range(peers)])


def exchange_bits():
    peers = lax.axis_size("fsdp")
    return [1 << b for b in reversed(range(peers.bit_length() - 1))]


def params(mib=24):
    return pltpu.CompilerParams(vmem_limit_bytes=mib * 1024 * 1024)


def cost(flops, bytes_accessed):
    return pl.CostEstimate(flops=flops, bytes_accessed=bytes_accessed, transcendentals=0)


def whole(array):
    return pl.BlockSpec(array.shape, lambda *_: (0,) * len(array.shape))


def level_ids(ids, group):
    masks = [0]
    for bit in group:
        masks += [mask | bit for mask in masks]
    return jnp.concatenate([ids] + [swap(ids, "fsdp", mask) for mask in masks[1:]], axis=0)


def with_lead(ids):
    tok_len = ids.shape[1]
    place = lax.axis_index("ctx")
    one = jnp.where(place >= 1, from_behind(ids, "ctx", 1), -1)
    two = jnp.where(place >= 2, from_behind(ids, "ctx", 2), -1)
    return jnp.concatenate([two[:, tok_len - LEAD :], one, ids], axis=1)


def table_kernel(rows_hbm, weight_hbm, gain_ref, table_ref, rows, weight, row_sems, weight_sems):
    count, width, panel_width = weight.shape
    parts, blocks = row_sems.shape[0], weight_sems.shape[1]
    each, deep = rows.shape[0] // parts, width // blocks
    row_copies = [
        pltpu.make_async_copy(rows_hbm.at[pl.ds(r * each, each)], rows.at[pl.ds(r * each, each)], row_sems.at[r])
        for r in range(parts)
    ]
    weight_copies = [
        [
            pltpu.make_async_copy(
                weight_hbm.at[i, pl.ds(k * deep, deep)], weight.at[i, pl.ds(k * deep, deep)], weight_sems.at[i, k]
            )
            for k in range(blocks)
        ]
        for i in range(count)
    ]
    for copy in row_copies + sum(weight_copies, []):
        copy.start()
    for r in range(parts):
        row_copies[r].wait()
        at = pl.ds(r * each, each)
        values = rows[at, :].astype(jnp.float32)
        inverse_rms = lax.rsqrt(jnp.mean(values * values, axis=-1, keepdims=True) + 1e-06)
        rows[at, :] = (values * inverse_rms * gain_ref[...]).astype(jnp.bfloat16)
    cols = min(256, panel_width)
    for i in range(count):
        for copy in weight_copies[i]:
            copy.wait()
        for first in range(0, panel_width, cols):
            at = slice(first, first + cols)
            part = jnp.dot(rows[...], weight[i, :, at], preferred_element_type=jnp.float32)
            table_ref[i, :, at] = part.astype(jnp.bfloat16)


def project(embedding, norm_gain, in_proj):
    vocab, width = embedding.shape
    count, _, panel_width = in_proj.shape
    hbm = pl.BlockSpec(memory_space=pltpu.HBM)
    shape = jax.ShapeDtypeStruct((count, vocab, panel_width), jnp.bfloat16)
    return pl.pallas_call(
        table_kernel,
        grid=(1,),
        in_specs=[hbm, hbm, pl.BlockSpec((1, width), lambda s: (0, 0))],
        out_specs=whole(shape),
        out_shape=shape,
        scratch_shapes=[
            pltpu.VMEM(embedding.shape, jnp.bfloat16),
            pltpu.VMEM(in_proj.shape, jnp.bfloat16),
            pltpu.SemaphoreType.DMA((8,)),
            pltpu.SemaphoreType.DMA((count, 4)),
        ],
        compiler_params=params(40),
        cost_estimate=cost(3_000_000_000, 0),
    )(embedding, in_proj, norm_gain.reshape(1, width))


def mixer_kernel(ids_ref, table_ref, short_ref, toeplitz, gated_ref, held_query, held):
    tok_len, panel_width = gated_ref.shape[1:]
    vocab = table_ref.shape[1]
    rows = ids_ref.shape[2]
    reach = 2 * tok_len
    lead = rows - reach
    tiles = panel_width // LANES
    per_tile = LANES // GROUP
    names = lax.broadcasted_iota(jnp.int32, (vocab, rows), 0)
    lane_group = lax.broadcasted_iota(jnp.int32, (tok_len, 2 * LANES), 1) % LANES // GROUP

    def look_up(one_hot, table):
        found = lax.dot_general(one_hot, table, (((0,), (0,)), ((), ())), preferred_element_type=jnp.float32)
        return found.astype(jnp.bfloat16).astype(jnp.float32)

    for v in range(2):
        one_hot = (names == ids_ref[v]).astype(jnp.float32).astype(jnp.bfloat16)
        held[v, 0] = look_up(one_hot, table_ref[1])
        held[v, 1] = look_up(one_hot, table_ref[2])
        held_query[v] = look_up(one_hot[:, rows - lead - tok_len :], table_ref[0])

    def featured(source, i, count, cols):
        total = short_ref[0, i : i + 1, cols] * source[pl.ds(lead, count), cols]
        for j in range(1, SHORT):
            total += short_ref[j, i : i + 1, cols] * source[pl.ds(lead - j, count), cols]
        return total

    for tile in range(tiles):
        cols = slice(tile * LANES, (tile + 1) * LANES)
        products = []
        for v in range(2):
            key = featured(held.at[v, 0], 1, reach, cols)
            value = featured(held.at[v, 1], 2, reach, cols)
            products.append((key * value).astype(jnp.bfloat16))
        both = jnp.concatenate(products, axis=1)
        filtered = None
        for k in range(per_tile):
            one = jnp.dot(
                toeplitz[tile, pl.ds(k * tok_len, tok_len), :], both, preferred_element_type=jnp.float32
            )
            filtered = one if k == 0 else jnp.where(lane_group == k, one, filtered)
        for v in range(2):
            query = featured(held_query.at[v], 0, tok_len, cols)
            gated_ref[v, :, cols] = (query * filtered[:, v * LANES : (v + 1) * LANES]).astype(jnp.bfloat16)


def mix(ids, table, short_taps, toeplitz, tok_len):
    windows, rows = ids.shape
    panel_width = table.shape[2]
    return pl.pallas_call(
        mixer_kernel,
        grid=(windows // 2,),
        in_specs=[pl.BlockSpec((2, 1, rows), lambda p: (p, 0, 0))]
        + [whole(array) for array in (table, short_taps, toeplitz)],
        out_specs=pl.BlockSpec((2, tok_len, panel_width), lambda p: (p, 0, 0)),
        out_shape=jax.ShapeDtypeStruct((windows, tok_len, panel_width), jnp.bfloat16),
        scratch_shapes=[
            pltpu.VMEM((2, LEAD + tok_len, panel_width), jnp.float32),
            pltpu.VMEM((2, 2, rows, panel_width), jnp.float32),
        ],
        compiler_params=params(),
        cost_estimate=cost(1_500_000_000, 0),
    )(ids.reshape(windows, 1, rows), table, short_taps, toeplitz)


def cut_kernel(place_ref, *refs):
    count = len(refs) // 2
    for source, piece in zip(refs[:count], refs[count:]):
        piece[...] = source[...]


def cut_pieces(place, out_proj):
    depth, width = out_proj.shape
    unit = width // SIXTEENTHS
    ins, outs, shapes = [], [], []
    for first, extent, order, _ in SPLITS:
        sharers = len(order)
        cols = extent * unit // sharers
        start = first * unit // cols
        ins.append(pl.BlockSpec((depth, cols), lambda s, place, start=start, n=sharers: (0, start + place[0] % n)))
        outs.append(pl.BlockSpec((depth, cols), lambda s, place: (0, 0)))
        shapes.append(jax.ShapeDtypeStruct((depth, cols), out_proj.dtype))
    return pl.pallas_call(
        cut_kernel,
        grid_spec=pltpu.PrefetchScalarGridSpec(num_scalar_prefetch=1, grid=(1,), in_specs=ins, out_specs=outs),
        out_shape=shapes,
        compiler_params=params(60),
        cost_estimate=cost(0, 2_000_000),
    )(place, *[out_proj] * len(SPLITS))


def toeplitz_kernel(base_ref, toeplitz_ref):
    tiles, stacked, reach = toeplitz_ref.shape
    per_tile = base_ref.shape[0] // tiles
    tok_len = stacked // per_tile
    for tile in range(tiles):
        for k in range(per_tile):
            g = tile * per_tile + k
            wide = jnp.broadcast_to(base_ref[g : g + 1, :], (tok_len, reach))
            shifted = pltpu.roll(wide, 0, 1, stride=1, stride_axis=0)
            toeplitz_ref[tile, pl.ds(k * tok_len, tok_len), :] = shifted.astype(jnp.bfloat16)


def build_toeplitz(conv_taps, tok_len):
    reach = 2 * tok_len
    per_tile = LANES // GROUP
    tiles = conv_taps.shape[0] // per_tile
    base = jnp.pad(conv_taps[:, ::-1].astype(jnp.float32), ((0, 0), (1, reach - TAPS - 1)))
    shape = jax.ShapeDtypeStruct((tiles, per_tile * tok_len, reach), jnp.bfloat16)
    return pl.pallas_call(
        toeplitz_kernel,
        grid=(1,),
        in_specs=[whole(base)],
        out_specs=whole(shape),
        out_shape=shape,
        compiler_params=params(8),
        cost_estimate=cost(0, 2_000_000),
    )(base)


def panel_kernel(place_ref, mine_ref, other_ref, *refs):
    out_ref = refs[-1]
    count, sharers, tok_len, _ = out_ref.shape
    beside = [ref.at[i] for ref in refs[sharers:-1] for i in range(ref.shape[0])]
    for k in range(sharers):
        total = jnp.dot(mine_ref[...], refs[k][...], preferred_element_type=jnp.float32)
        total += jnp.dot(other_ref[...], beside[k][...], preferred_element_type=jnp.float32)
        for w in range(count):
            out_ref[w, k] = total[w * tok_len : (w + 1) * tok_len].astype(out_ref.dtype)


def panel(place, mine, other, out_proj, beside, split, step, begin=0):
    count, tok_len, depth = mine.shape
    rows = count * tok_len
    unit = out_proj.shape[1] // SIXTEENTHS
    base, extent, order, _ = split
    sharers = len(order)
    piece_cols = extent * unit // sharers
    offset, cols = (part * unit // sharers for part in step)
    fixed = lambda shape: pl.BlockSpec(shape, lambda s, place: (0,) * len(shape))

    def own(k):
        start, per = (base * unit + offset) // cols, piece_cols // cols
        return pl.BlockSpec((depth, cols), lambda s, place: (0, start + (place[0] % sharers ^ k) * per))

    near = lambda a: pl.BlockSpec((a.shape[0], depth, cols), lambda s, place: (0, 0, offset // cols - begin * unit // sharers // cols))
    return pl.pallas_call(
        panel_kernel,
        grid_spec=pltpu.PrefetchScalarGridSpec(
            num_scalar_prefetch=1,
            grid=(1,),
            in_specs=[fixed((rows, depth))] * 2 + [own(k) for k in order] + [near(a) for a in beside],
            out_specs=fixed((count, sharers, tok_len, cols)),
        ),
        out_shape=jax.ShapeDtypeStruct((count, sharers, tok_len, cols), jnp.bfloat16),
        compiler_params=params(),
        cost_estimate=cost(400_000_000, 0),
    )(place, mine.reshape(rows, depth), other.reshape(rows, depth), *[out_proj] * sharers, *beside)


def residual_kernel(ids_ref, rows_ref, out_ref):
    names = lax.broadcasted_iota(jnp.int32, (rows_ref.shape[0], ids_ref.shape[1]), 0)
    one_hot = (names == ids_ref[...]).astype(jnp.float32).astype(jnp.bfloat16)
    out_ref[...] = lax.dot_general(
        one_hot, rows_ref[...], (((0,), (0,)), ((), ())), preferred_element_type=jnp.float32
    ).astype(jnp.bfloat16)


def residual(token_ids, embedding):
    vocab, width = embedding.shape
    tok_len = token_ids.shape[1]
    cols = width // 4
    return pl.pallas_call(
        residual_kernel,
        grid=(4,),
        in_specs=[whole(token_ids), pl.BlockSpec((vocab, cols), lambda i: (0, i))],
        out_specs=pl.BlockSpec((tok_len, cols), lambda i: (0, i)),
        out_shape=jax.ShapeDtypeStruct((tok_len, width), jnp.bfloat16),
        compiler_params=params(),
        cost_estimate=cost(400_000_000, 0),
    )(token_ids, embedding)


def place_kernel(split, step, place_ref, so_far_ref, near_ref, far_ref, out_ref):
    _, sharers, _, cols = near_ref.shape
    piece_cols = so_far_ref.shape[1] // sharers
    offset = step[0] * cols // step[1]
    out_ref[...] = so_far_ref[...]
    for i, k in enumerate(split[2]):
        first = (place_ref[0] % sharers ^ k) * piece_cols + offset
        total = near_ref[0, i].astype(jnp.float32) + far_ref[0, i].astype(jnp.float32)
        at = pl.ds(pl.multiple_of(first, LANES), cols)
        out_ref[:, at] = (so_far_ref[:, at].astype(jnp.float32) + total).astype(jnp.bfloat16)


def place_pieces(place, so_far, near, far, split, step):
    tok_len, width = so_far.shape
    base, extent, _, _ = split
    part = pl.BlockSpec((tok_len, extent * width // SIXTEENTHS), lambda s, place: (0, base // extent))
    one = pl.BlockSpec(near.shape, lambda s, place: (0, 0, 0, 0))
    return pl.pallas_call(
        functools.partial(place_kernel, split, step),
        grid_spec=pltpu.PrefetchScalarGridSpec(
            num_scalar_prefetch=1, grid=(1,), in_specs=[part, one, one], out_specs=part
        ),
        out_shape=jax.ShapeDtypeStruct(so_far.shape, so_far.dtype),
        input_output_aliases={1: 0},
        compiler_params=params(),
        cost_estimate=cost(0, 1_000_000),
    )(place, so_far, near, far)


def add(a, b):
    return (a.astype(jnp.float32) + b.astype(jnp.float32)).astype(jnp.bfloat16)


def per_device(token_ids, embedding, norm_gain, in_proj, short_taps, conv_taps, out_proj):
    tok_len = token_ids.shape[1]
    at = lax.axis_index("ctx").reshape(1).astype(jnp.int32)
    bits = exchange_bits()
    tie = lax.optimization_barrier
    beside_bit = bits[-2]

    early, late = cut_pieces(at, out_proj)
    early, late, conv_taps = tie((early, late, conv_taps))
    toeplitz = build_toeplitz(conv_taps, tok_len)
    ids = level_ids(token_ids, bits[:2])
    ids, toeplitz = tie((ids, toeplitz))
    for group in [bits[i : i + 2] for i in range(2, len(bits), 2)]:
        ids = level_ids(ids, group)
    early = swap(early, "fsdp", beside_bit)
    ids, embedding_then, late = tie((ids, embedding, late))
    late = swap(late, "fsdp", beside_bit)
    ids = with_lead(ids)
    table = project(embedding_then, norm_gain, in_proj)
    table, early = tie((table, early))
    early_pair = jnp.stack([early, swap(early, "ctx", 2)])

    part = ids.shape[0] // 4
    quarters = [ids[n * part : (n + 1) * part] for n in range(4)]
    sent = mix(quarters[3], table, short_taps, toeplitz, tok_len)
    kept, sent = tie((jnp.concatenate([quarters[1], quarters[2], quarters[0]], axis=0), sent))
    other = [swap(sent, "fsdp", beside_bit)]
    gated = mix(kept, table, short_taps, toeplitz, tok_len)
    gated, early_pair = tie((gated, early_pair))
    other.append(swap(gated[:part], "fsdp", beside_bit))
    mine = [gated[part : 2 * part], gated[2 * part :]]
    middle = early.shape[1] // 2
    pairs = [(columns, swap(columns, "ctx", 1)) for columns in (early_pair[:, :, :middle], early_pair[:, :, middle:])]
    late_pair = jnp.stack([late, swap(late, "ctx", 1)])
    own_ids, gated = tie((token_ids, gated))
    out = residual(own_ids, embedding)
    late_pair, out = tie((late_pair, out))
    pairs += [(columns, swap(columns, "ctx", 2)) for columns in (late_pair[:, :, :middle],)]
    (head, body, foot), tail = SPLITS[0][3], SPLITS[1][3]

    def send(pair, split, step, begin):
        away = panel(at, mine[0], other[0], out_proj, pair, split, step, begin)
        return away, swap(away, "fsdp", bits[-1])

    def sum_up(pair, split, step, begin, got):
        total = panel(at, mine[1], other[1], out_proj, pair, split, step, begin)
        for bit in reversed(bits[:-2]):
            half = total.shape[0] // 2
            far = add(total[half:], got[half:])
            total, got = add(total[:half], got[:half]), swap(far, "fsdp", bit)
        return far, (total, got, split, step)

    chunk = (pairs[1], SPLITS[0], body, body[0])
    away, got = send(*chunk)
    other[1], late_rest, _ = tie((other[1], late_pair[:, :, middle:], away))
    pairs.append((late_rest, swap(late_rest, "ctx", 2)))

    all_mine, all_other = (jnp.concatenate(parts, axis=0) for parts in (mine, other))
    total = panel(at, all_mine, all_other, out_proj, pairs[0], SPLITS[0], head)
    other[1], total = tie((other[1], total))
    total = total.reshape(2, part, *total.shape[1:])
    head_got = swap(total[:, part // 2 :], "fsdp", bits[-3])

    far, first_sum = sum_up(*chunk, got)
    mine[0], _ = tie((mine[0], far))
    head_got, _ = tie((head_got, far))
    total = add(total[:, : part // 2], head_got)
    for bit in reversed(bits[:-3]):
        half = total.shape[1] // 2
        total = add(total[:, :half], swap(total[:, half:], "fsdp", bit))
    head_sum = (total[1], swap(total[0], "fsdp", bits[-1]), SPLITS[0], head)
    sums = [first_sum]
    for pair, split, step, begin in (
        (pairs[2], SPLITS[1], tail[0], tail[0][0]),
        (pairs[3], SPLITS[1], tail[1], tail[1][0]),
        (pairs[0], SPLITS[0], foot, 0),
    ):
        away, got = send(pair, split, step, begin)
        mine[0], away = tie((mine[0], away))
        got, _ = tie((got, far))
        far, one = sum_up(pair, split, step, begin, got)
        sums.append(one)
    out = place_pieces(at, out, *head_sum)
    for one in sums:
        out = place_pieces(at, out, *one)
    return out[None]


def solution(mesh):
    return jax.shard_map(
        per_device,
        mesh=mesh,
        in_specs=(
            P("fsdp", "ctx"),
            P(),
            P(),
            P(None, None, "fsdp"),
            P(None, None, "fsdp"),
            P("fsdp", None),
            P("fsdp", None),
        ),
        out_specs=P("fsdp", "ctx", None),
        check_vma=False,
    )
```

```python
import functools

import jax
import jax.numpy as jnp
from jax import lax
from jax.experimental import pallas as pl
from jax.experimental.pallas import tpu as pltpu
from jax.sharding import PartitionSpec as P

GROUP = 16
TAPS = 128
SHORT = 3
LANES = 128
LEAD = 16
SPLITS = ((0, 8, (0, 2, 1, 3), ((0, 2), (4, 4), (2, 2))), (8, 8, (0, 1, 2, 3), ((0, 4), (4, 4))))
SIXTEENTHS = 16


def from_behind(x, axis, by):
    peers = lax.axis_size(axis)
    return lax.ppermute(x, axis, [(i, (i + by) % peers) for i in range(peers)])


def swap(x, axis, mask):
    peers = lax.axis_size(axis)
    return lax.ppermute(x, axis, [(i, i ^ mask) for i in range(peers)])


def exchange_bits():
    peers = lax.axis_size("fsdp")
    return [1 << b for b in reversed(range(peers.bit_length() - 1))]


def params(mib=24):
    return pltpu.CompilerParams(vmem_limit_bytes=mib * 1024 * 1024)


def cost(flops, bytes_accessed):
    return pl.CostEstimate(flops=flops, bytes_accessed=bytes_accessed, transcendentals=0)


def whole(array):
    return pl.BlockSpec(array.shape, lambda *_: (0,) * len(array.shape))


def level_ids(ids, group):
    masks = [0]
    for bit in group:
        masks += [mask | bit for mask in masks]
    return jnp.concatenate([ids] + [swap(ids, "fsdp", mask) for mask in masks[1:]], axis=0)


def with_lead(ids):
    tok_len = ids.shape[1]
    place = lax.axis_index("ctx")
    one = jnp.where(place >= 1, from_behind(ids, "ctx", 1), -1)
    two = jnp.where(place >= 2, from_behind(ids, "ctx", 2), -1)
    return jnp.concatenate([two[:, tok_len - LEAD :], one, ids], axis=1)


def table_kernel(rows_hbm, weight_hbm, gain_ref, table_ref, rows, weight, row_sems, weight_sems):
    count, width, panel_width = weight.shape
    parts, blocks = row_sems.shape[0], weight_sems.shape[1]
    each, deep = rows.shape[0] // parts, width // blocks
    row_copies = [
        pltpu.make_async_copy(rows_hbm.at[pl.ds(r * each, each)], rows.at[pl.ds(r * each, each)], row_sems.at[r])
        for r in range(parts)
    ]
    weight_copies = [
        [
            pltpu.make_async_copy(
                weight_hbm.at[i, pl.ds(k * deep, deep)], weight.at[i, pl.ds(k * deep, deep)], weight_sems.at[i, k]
            )
            for k in range(blocks)
        ]
        for i in range(count)
    ]
    for copy in row_copies + sum(weight_copies, []):
        copy.start()
    for r in range(parts):
        row_copies[r].wait()
        at = pl.ds(r * each, each)
        values = rows[at, :].astype(jnp.float32)
        inverse_rms = lax.rsqrt(jnp.mean(values * values, axis=-1, keepdims=True) + 1e-06)
        rows[at, :] = (values * inverse_rms * gain_ref[...]).astype(jnp.bfloat16)
    cols = min(256, panel_width)
    for i in range(count):
        for copy in weight_copies[i]:
            copy.wait()
        for first in range(0, panel_width, cols):
            at = slice(first, first + cols)
            part = jnp.dot(rows[...], weight[i, :, at], preferred_element_type=jnp.float32)
            table_ref[i, :, at] = part.astype(jnp.bfloat16)


def project(embedding, norm_gain, in_proj):
    vocab, width = embedding.shape
    count, _, panel_width = in_proj.shape
    hbm = pl.BlockSpec(memory_space=pltpu.HBM)
    shape = jax.ShapeDtypeStruct((count, vocab, panel_width), jnp.bfloat16)
    return pl.pallas_call(
        table_kernel,
        grid=(1,),
        in_specs=[hbm, hbm, pl.BlockSpec((1, width), lambda s: (0, 0))],
        out_specs=whole(shape),
        out_shape=shape,
        scratch_shapes=[
            pltpu.VMEM(embedding.shape, jnp.bfloat16),
            pltpu.VMEM(in_proj.shape, jnp.bfloat16),
            pltpu.SemaphoreType.DMA((8,)),
            pltpu.SemaphoreType.DMA((count, 4)),
        ],
        compiler_params=params(40),
        cost_estimate=cost(3_000_000_000, 0),
    )(embedding, in_proj, norm_gain.reshape(1, width))


def mixer_kernel(ids_ref, table_ref, short_ref, toeplitz, gated_ref, held_query, held):
    tok_len, panel_width = gated_ref.shape[1:]
    vocab = table_ref.shape[1]
    rows = ids_ref.shape[2]
    reach = 2 * tok_len
    lead = rows - reach
    tiles = panel_width // LANES
    per_tile = LANES // GROUP
    names = lax.broadcasted_iota(jnp.int32, (vocab, rows), 0)
    lane_group = lax.broadcasted_iota(jnp.int32, (tok_len, 2 * LANES), 1) % LANES // GROUP

    def look_up(one_hot, table):
        found = lax.dot_general(one_hot, table, (((0,), (0,)), ((), ())), preferred_element_type=jnp.float32)
        return found.astype(jnp.bfloat16).astype(jnp.float32)

    for v in range(2):
        one_hot = (names == ids_ref[v]).astype(jnp.float32).astype(jnp.bfloat16)
        held[v, 0] = look_up(one_hot, table_ref[1])
        held[v, 1] = look_up(one_hot, table_ref[2])
        held_query[v] = look_up(one_hot[:, rows - lead - tok_len :], table_ref[0])

    def featured(source, i, count, cols):
        total = short_ref[0, i : i + 1, cols] * source[pl.ds(lead, count), cols]
        for j in range(1, SHORT):
            total += short_ref[j, i : i + 1, cols] * source[pl.ds(lead - j, count), cols]
        return total

    for tile in range(tiles):
        cols = slice(tile * LANES, (tile + 1) * LANES)
        products = []
        for v in range(2):
            key = featured(held.at[v, 0], 1, reach, cols)
            value = featured(held.at[v, 1], 2, reach, cols)
            products.append((key * value).astype(jnp.bfloat16))
        both = jnp.concatenate(products, axis=1)
        filtered = None
        for k in range(per_tile):
            one = jnp.dot(
                toeplitz[tile, pl.ds(k * tok_len, tok_len), :], both, preferred_element_type=jnp.float32
            )
            filtered = one if k == 0 else jnp.where(lane_group == k, one, filtered)
        for v in range(2):
            query = featured(held_query.at[v], 0, tok_len, cols)
            gated_ref[v, :, cols] = (query * filtered[:, v * LANES : (v + 1) * LANES]).astype(jnp.bfloat16)


def mix(ids, table, short_taps, toeplitz, tok_len):
    windows, rows = ids.shape
    panel_width = table.shape[2]
    return pl.pallas_call(
        mixer_kernel,
        grid=(windows // 2,),
        in_specs=[pl.BlockSpec((2, 1, rows), lambda p: (p, 0, 0))]
        + [whole(array) for array in (table, short_taps, toeplitz)],
        out_specs=pl.BlockSpec((2, tok_len, panel_width), lambda p: (p, 0, 0)),
        out_shape=jax.ShapeDtypeStruct((windows, tok_len, panel_width), jnp.bfloat16),
        scratch_shapes=[
            pltpu.VMEM((2, LEAD + tok_len, panel_width), jnp.float32),
            pltpu.VMEM((2, 2, rows, panel_width), jnp.float32),
        ],
        compiler_params=params(),
        cost_estimate=cost(1_500_000_000, 0),
    )(ids.reshape(windows, 1, rows), table, short_taps, toeplitz)


def cut_kernel(place_ref, *refs):
    count = len(refs) // 2
    for source, piece in zip(refs[:count], refs[count:]):
        piece[...] = source[...]


def cut_pieces(place, out_proj):
    depth, width = out_proj.shape
    unit = width // SIXTEENTHS
    ins, outs, shapes = [], [], []
    for first, extent, order, _ in SPLITS:
        sharers = len(order)
        cols = extent * unit // sharers
        start = first * unit // cols
        ins.append(pl.BlockSpec((depth, cols), lambda s, place, start=start, n=sharers: (0, start + place[0] % n)))
        outs.append(pl.BlockSpec((depth, cols), lambda s, place: (0, 0)))
        shapes.append(jax.ShapeDtypeStruct((depth, cols), out_proj.dtype))
    return pl.pallas_call(
        cut_kernel,
        grid_spec=pltpu.PrefetchScalarGridSpec(num_scalar_prefetch=1, grid=(1,), in_specs=ins, out_specs=outs),
        out_shape=shapes,
        compiler_params=params(60),
        cost_estimate=cost(0, 2_000_000),
    )(place, *[out_proj] * len(SPLITS))


def toeplitz_kernel(base_ref, toeplitz_ref):
    tiles, stacked, reach = toeplitz_ref.shape
    per_tile = base_ref.shape[0] // tiles
    tok_len = stacked // per_tile
    for tile in range(tiles):
        for k in range(per_tile):
            g = tile * per_tile + k
            wide = jnp.broadcast_to(base_ref[g : g + 1, :], (tok_len, reach))
            shifted = pltpu.roll(wide, 0, 1, stride=1, stride_axis=0)
            toeplitz_ref[tile, pl.ds(k * tok_len, tok_len), :] = shifted.astype(jnp.bfloat16)


def build_toeplitz(conv_taps, tok_len):
    reach = 2 * tok_len
    per_tile = LANES // GROUP
    tiles = conv_taps.shape[0] // per_tile
    base = jnp.pad(conv_taps[:, ::-1].astype(jnp.float32), ((0, 0), (1, reach - TAPS - 1)))
    shape = jax.ShapeDtypeStruct((tiles, per_tile * tok_len, reach), jnp.bfloat16)
    return pl.pallas_call(
        toeplitz_kernel,
        grid=(1,),
        in_specs=[whole(base)],
        out_specs=whole(shape),
        out_shape=shape,
        compiler_params=params(8),
        cost_estimate=cost(0, 2_000_000),
    )(base)


def panel_kernel(place_ref, mine_ref, other_ref, *refs):
    out_ref = refs[-1]
    count, sharers, tok_len, _ = out_ref.shape
    beside = [ref.at[i] for ref in refs[sharers:-1] for i in range(ref.shape[0])]
    for k in range(sharers):
        total = jnp.dot(mine_ref[...], refs[k][...], preferred_element_type=jnp.float32)
        total += jnp.dot(other_ref[...], beside[k][...], preferred_element_type=jnp.float32)
        for w in range(count):
            out_ref[w, k] = total[w * tok_len : (w + 1) * tok_len].astype(out_ref.dtype)


def panel(place, mine, other, out_proj, beside, split, step, begin=0):
    count, tok_len, depth = mine.shape
    rows = count * tok_len
    unit = out_proj.shape[1] // SIXTEENTHS
    base, extent, order, _ = split
    sharers = len(order)
    piece_cols = extent * unit // sharers
    offset, cols = (part * unit // sharers for part in step)
    fixed = lambda shape: pl.BlockSpec(shape, lambda s, place: (0,) * len(shape))

    def own(k):
        start, per = (base * unit + offset) // cols, piece_cols // cols
        return pl.BlockSpec((depth, cols), lambda s, place: (0, start + (place[0] % sharers ^ k) * per))

    near = lambda a: pl.BlockSpec((a.shape[0], depth, cols), lambda s, place: (0, 0, offset // cols - begin * unit // sharers // cols))
    return pl.pallas_call(
        panel_kernel,
        grid_spec=pltpu.PrefetchScalarGridSpec(
            num_scalar_prefetch=1,
            grid=(1,),
            in_specs=[fixed((rows, depth))] * 2 + [own(k) for k in order] + [near(a) for a in beside],
            out_specs=fixed((count, sharers, tok_len, cols)),
        ),
        out_shape=jax.ShapeDtypeStruct((count, sharers, tok_len, cols), jnp.bfloat16),
        compiler_params=params(),
        cost_estimate=cost(400_000_000, 0),
    )(place, mine.reshape(rows, depth), other.reshape(rows, depth), *[out_proj] * sharers, *beside)


def residual_kernel(ids_ref, rows_ref, out_ref):
    names = lax.broadcasted_iota(jnp.int32, (rows_ref.shape[0], ids_ref.shape[1]), 0)
    one_hot = (names == ids_ref[...]).astype(jnp.float32).astype(jnp.bfloat16)
    out_ref[...] = lax.dot_general(
        one_hot, rows_ref[...], (((0,), (0,)), ((), ())), preferred_element_type=jnp.float32
    ).astype(jnp.bfloat16)


def residual(token_ids, embedding):
    vocab, width = embedding.shape
    tok_len = token_ids.shape[1]
    cols = width // 4
    return pl.pallas_call(
        residual_kernel,
        grid=(4,),
        in_specs=[whole(token_ids), pl.BlockSpec((vocab, cols), lambda i: (0, i))],
        out_specs=pl.BlockSpec((tok_len, cols), lambda i: (0, i)),
        out_shape=jax.ShapeDtypeStruct((tok_len, width), jnp.bfloat16),
        compiler_params=params(),
        cost_estimate=cost(400_000_000, 0),
    )(token_ids, embedding)


def place_kernel(split, step, place_ref, so_far_ref, near_ref, far_ref, out_ref):
    _, sharers, _, cols = near_ref.shape
    piece_cols = so_far_ref.shape[1] // sharers
    offset = step[0] * cols // step[1]
    out_ref[...] = so_far_ref[...]
    for i, k in enumerate(split[2]):
        first = (place_ref[0] % sharers ^ k) * piece_cols + offset
        total = near_ref[0, i].astype(jnp.float32) + far_ref[0, i].astype(jnp.float32)
        at = pl.ds(pl.multiple_of(first, LANES), cols)
        out_ref[:, at] = (so_far_ref[:, at].astype(jnp.float32) + total).astype(jnp.bfloat16)


def place_pieces(place, so_far, near, far, split, step):
    tok_len, width = so_far.shape
    base, extent, _, _ = split
    part = pl.BlockSpec((tok_len, extent * width // SIXTEENTHS), lambda s, place: (0, base // extent))
    one = pl.BlockSpec(near.shape, lambda s, place: (0, 0, 0, 0))
    return pl.pallas_call(
        functools.partial(place_kernel, split, step),
        grid_spec=pltpu.PrefetchScalarGridSpec(
            num_scalar_prefetch=1, grid=(1,), in_specs=[part, one, one], out_specs=part
        ),
        out_shape=jax.ShapeDtypeStruct(so_far.shape, so_far.dtype),
        input_output_aliases={1: 0},
        compiler_params=params(),
        cost_estimate=cost(0, 1_000_000),
    )(place, so_far, near, far)


def add(a, b):
    return (a.astype(jnp.float32) + b.astype(jnp.float32)).astype(jnp.bfloat16)


def per_device(token_ids, embedding, norm_gain, in_proj, short_taps, conv_taps, out_proj):
    tok_len = token_ids.shape[1]
    at = lax.axis_index("ctx").reshape(1).astype(jnp.int32)
    bits = exchange_bits()
    tie = lax.optimization_barrier
    beside_bit = bits[-2]

    early, late = cut_pieces(at, out_proj)
    early, late, conv_taps = tie((early, late, conv_taps))
    toeplitz = build_toeplitz(conv_taps, tok_len)
    ids = level_ids(token_ids, bits[:2])
    ids, toeplitz = tie((ids, toeplitz))
    for group in [bits[i : i + 2] for i in range(2, len(bits), 2)]:
        ids = level_ids(ids, group)
    early = swap(early, "fsdp", beside_bit)
    ids, in_proj, late = tie((ids, in_proj, late))
    late = swap(late, "fsdp", beside_bit)
    ids = with_lead(ids)
    table = project(embedding, norm_gain, in_proj)
    table, early = tie((table, early))
    middle = early.shape[1] // 2
    body_columns, head_columns = early[:, middle:], early[:, :middle]
    body_pair = jnp.stack([body_columns, swap(body_columns, "ctx", 2)])

    part = ids.shape[0] // 4
    quarters = [ids[n * part : (n + 1) * part] for n in range(4)]
    sent = mix(quarters[3], table, short_taps, toeplitz, tok_len)
    kept, sent = tie((jnp.concatenate([quarters[1], quarters[2], quarters[0]], axis=0), sent))
    other = [swap(sent, "fsdp", beside_bit)]
    head_columns, sent = tie((head_columns, sent))
    head_pair = jnp.stack([head_columns, swap(head_columns, "ctx", 2)])
    gated = mix(kept, table, short_taps, toeplitz, tok_len)
    gated, body_pair = tie((gated, body_pair))
    other.append(swap(gated[:part], "fsdp", beside_bit))
    mine = [gated[part : 2 * part], gated[2 * part :]]
    pairs = [None, (body_pair, swap(body_pair, "ctx", 1))]
    late_pair = jnp.stack([late, swap(late, "ctx", 1)])
    own_ids, gated = tie((token_ids, gated))
    out = residual(own_ids, embedding)
    late_pair, head_pair, out = tie((late_pair, head_pair, out))
    pairs[0] = (head_pair, swap(head_pair, "ctx", 1))
    pairs += [(columns, swap(columns, "ctx", 2)) for columns in (late_pair[:, :, :middle],)]
    (head, body, foot), tail = SPLITS[0][3], SPLITS[1][3]

    def send(pair, split, step, begin):
        away = panel(at, mine[0], other[0], out_proj, pair, split, step, begin)
        return away, swap(away, "fsdp", bits[-1])

    def sum_up(pair, split, step, begin, got):
        total = panel(at, mine[1], other[1], out_proj, pair, split, step, begin)
        for bit in reversed(bits[:-2]):
            half = total.shape[0] // 2
            far = add(total[half:], got[half:])
            total, got = add(total[:half], got[:half]), swap(far, "fsdp", bit)
        return far, (total, got, split, step)

    chunk = (pairs[1], SPLITS[0], body, body[0])
    away, got = send(*chunk)
    other[1], late_rest, _ = tie((other[1], late_pair[:, :, middle:], away))
    pairs.append((late_rest, swap(late_rest, "ctx", 2)))

    all_mine, all_other = (jnp.concatenate(parts, axis=0) for parts in (mine, other))
    total = panel(at, all_mine, all_other, out_proj, pairs[0], SPLITS[0], head)
    other[1], total = tie((other[1], total))
    total = total.reshape(2, part, *total.shape[1:])
    head_got = swap(total[:, part // 2 :], "fsdp", bits[-3])

    far, first_sum = sum_up(*chunk, got)
    mine[0], _ = tie((mine[0], far))
    head_got, _ = tie((head_got, far))
    total = add(total[:, : part // 2], head_got)
    for bit in reversed(bits[:-3]):
        half = total.shape[1] // 2
        total = add(total[:, :half], swap(total[:, half:], "fsdp", bit))
    head_sum = (total[1], swap(total[0], "fsdp", bits[-1]), SPLITS[0], head)
    sums = [first_sum]
    for pair, split, step, begin in (
        (pairs[2], SPLITS[1], tail[0], tail[0][0]),
        (pairs[3], SPLITS[1], tail[1], tail[1][0]),
        (pairs[0], SPLITS[0], foot, 0),
    ):
        away, got = send(pair, split, step, begin)
        mine[0], away = tie((mine[0], away))
        got, _ = tie((got, far))
        far, one = sum_up(pair, split, step, begin, got)
        sums.append(one)
    out = place_pieces(at, out, *head_sum)
    for one in sums:
        out = place_pieces(at, out, *one)
    return out[None]


def solution(mesh):
    return jax.shard_map(
        per_device,
        mesh=mesh,
        in_specs=(
            P("fsdp", "ctx"),
            P(),
            P(),
            P(None, None, "fsdp"),
            P(None, None, "fsdp"),
            P("fsdp", None),
            P("fsdp", None),
        ),
        out_specs=P("fsdp", "ctx", None),
        check_vma=False,
    )
```

```python
import functools

import jax
import jax.numpy as jnp
from jax import lax
from jax.experimental import pallas as pl
from jax.experimental.pallas import tpu as pltpu
from jax.sharding import PartitionSpec as P

GROUP = 16
TAPS = 128
SHORT = 3
LANES = 128
LEAD = 16
SPLITS = ((0, 8, (0, 2, 1, 3), ((0, 2), (4, 4), (2, 2))), (8, 8, (0, 1, 2, 3), ((0, 4), (4, 4))))
SIXTEENTHS = 16


def from_behind(x, axis, by):
    peers = lax.axis_size(axis)
    return lax.ppermute(x, axis, [(i, (i + by) % peers) for i in range(peers)])


def swap(x, axis, mask):
    peers = lax.axis_size(axis)
    return lax.ppermute(x, axis, [(i, i ^ mask) for i in range(peers)])


def exchange_bits():
    peers = lax.axis_size("fsdp")
    return [1 << b for b in reversed(range(peers.bit_length() - 1))]


def params(mib=24):
    return pltpu.CompilerParams(vmem_limit_bytes=mib * 1024 * 1024)


def cost(flops, bytes_accessed):
    return pl.CostEstimate(flops=flops, bytes_accessed=bytes_accessed, transcendentals=0)


def whole(array):
    return pl.BlockSpec(array.shape, lambda *_: (0,) * len(array.shape))


def level_ids(ids, group):
    masks = [0]
    for bit in group:
        masks += [mask | bit for mask in masks]
    return jnp.concatenate([ids] + [swap(ids, "fsdp", mask) for mask in masks[1:]], axis=0)


def with_lead(ids):
    tok_len = ids.shape[1]
    place = lax.axis_index("ctx")
    one = jnp.where(place >= 1, from_behind(ids, "ctx", 1), -1)
    two = jnp.where(place >= 2, from_behind(ids, "ctx", 2), -1)
    return jnp.concatenate([two[:, tok_len - LEAD :], one, ids], axis=1)


def table_kernel(rows_hbm, weight_hbm, gain_ref, table_ref, rows, weight, row_sems, weight_sems):
    count, width, panel_width = weight.shape
    parts, blocks = row_sems.shape[0], weight_sems.shape[1]
    each, deep = rows.shape[0] // parts, width // blocks
    row_copies = [
        pltpu.make_async_copy(rows_hbm.at[pl.ds(r * each, each)], rows.at[pl.ds(r * each, each)], row_sems.at[r])
        for r in range(parts)
    ]
    weight_copies = [
        [
            pltpu.make_async_copy(
                weight_hbm.at[i, pl.ds(k * deep, deep)], weight.at[i, pl.ds(k * deep, deep)], weight_sems.at[i, k]
            )
            for k in range(blocks)
        ]
        for i in range(count)
    ]
    for copy in row_copies + sum(weight_copies, []):
        copy.start()
    for r in range(parts):
        row_copies[r].wait()
        at = pl.ds(r * each, each)
        values = rows[at, :].astype(jnp.float32)
        inverse_rms = lax.rsqrt(jnp.mean(values * values, axis=-1, keepdims=True) + 1e-06)
        rows[at, :] = (values * inverse_rms * gain_ref[...]).astype(jnp.bfloat16)
    cols = min(256, panel_width)
    for i in range(count):
        for copy in weight_copies[i]:
            copy.wait()
        for first in range(0, panel_width, cols):
            at = slice(first, first + cols)
            part = jnp.dot(rows[...], weight[i, :, at], preferred_element_type=jnp.float32)
            table_ref[i, :, at] = part.astype(jnp.bfloat16)


def project(embedding, norm_gain, in_proj):
    vocab, width = embedding.shape
    count, _, panel_width = in_proj.shape
    hbm = pl.BlockSpec(memory_space=pltpu.HBM)
    shape = jax.ShapeDtypeStruct((count, vocab, panel_width), jnp.bfloat16)
    return pl.pallas_call(
        table_kernel,
        grid=(1,),
        in_specs=[hbm, hbm, pl.BlockSpec((1, width), lambda s: (0, 0))],
        out_specs=whole(shape),
        out_shape=shape,
        scratch_shapes=[
            pltpu.VMEM(embedding.shape, jnp.bfloat16),
            pltpu.VMEM(in_proj.shape, jnp.bfloat16),
            pltpu.SemaphoreType.DMA((8,)),
            pltpu.SemaphoreType.DMA((count, 4)),
        ],
        compiler_params=params(40),
        cost_estimate=cost(3_000_000_000, 0),
    )(embedding, in_proj, norm_gain.reshape(1, width))


def mixer_kernel(ids_ref, table_ref, short_ref, toeplitz, gated_ref, held_query, held):
    tok_len, panel_width = gated_ref.shape[1:]
    vocab = table_ref.shape[1]
    rows = ids_ref.shape[2]
    reach = 2 * tok_len
    lead = rows - reach
    tiles = panel_width // LANES
    per_tile = LANES // GROUP
    names = lax.broadcasted_iota(jnp.int32, (vocab, rows), 0)
    lane_group = lax.broadcasted_iota(jnp.int32, (tok_len, 2 * LANES), 1) % LANES // GROUP

    def look_up(one_hot, table):
        found = lax.dot_general(one_hot, table, (((0,), (0,)), ((), ())), preferred_element_type=jnp.float32)
        return found.astype(jnp.bfloat16).astype(jnp.float32)

    for v in range(2):
        one_hot = (names == ids_ref[v]).astype(jnp.float32).astype(jnp.bfloat16)
        held[v, 0] = look_up(one_hot, table_ref[1])
        held[v, 1] = look_up(one_hot, table_ref[2])
        held_query[v] = look_up(one_hot[:, rows - lead - tok_len :], table_ref[0])

    def featured(source, i, count, cols):
        total = short_ref[0, i : i + 1, cols] * source[pl.ds(lead, count), cols]
        for j in range(1, SHORT):
            total += short_ref[j, i : i + 1, cols] * source[pl.ds(lead - j, count), cols]
        return total

    for tile in range(tiles):
        cols = slice(tile * LANES, (tile + 1) * LANES)
        products = []
        for v in range(2):
            key = featured(held.at[v, 0], 1, reach, cols)
            value = featured(held.at[v, 1], 2, reach, cols)
            products.append((key * value).astype(jnp.bfloat16))
        both = jnp.concatenate(products, axis=1)
        filtered = None
        for k in range(per_tile):
            one = jnp.dot(
                toeplitz[tile, pl.ds(k * tok_len, tok_len), :], both, preferred_element_type=jnp.float32
            )
            filtered = one if k == 0 else jnp.where(lane_group == k, one, filtered)
        for v in range(2):
            query = featured(held_query.at[v], 0, tok_len, cols)
            gated_ref[v, :, cols] = (query * filtered[:, v * LANES : (v + 1) * LANES]).astype(jnp.bfloat16)


def mix(ids, table, short_taps, toeplitz, tok_len):
    windows, rows = ids.shape
    panel_width = table.shape[2]
    return pl.pallas_call(
        mixer_kernel,
        grid=(windows // 2,),
        in_specs=[pl.BlockSpec((2, 1, rows), lambda p: (p, 0, 0))]
        + [whole(array) for array in (table, short_taps, toeplitz)],
        out_specs=pl.BlockSpec((2, tok_len, panel_width), lambda p: (p, 0, 0)),
        out_shape=jax.ShapeDtypeStruct((windows, tok_len, panel_width), jnp.bfloat16),
        scratch_shapes=[
            pltpu.VMEM((2, LEAD + tok_len, panel_width), jnp.float32),
            pltpu.VMEM((2, 2, rows, panel_width), jnp.float32),
        ],
        compiler_params=params(),
        cost_estimate=cost(1_500_000_000, 0),
    )(ids.reshape(windows, 1, rows), table, short_taps, toeplitz)


def cut_kernel(place_ref, *refs):
    count = len(refs) // 2
    for source, piece in zip(refs[:count], refs[count:]):
        piece[...] = source[...]


def cut_pieces(place, out_proj):
    depth, width = out_proj.shape
    unit = width // SIXTEENTHS
    ins, outs, shapes = [], [], []
    for first, extent, order, _ in SPLITS:
        sharers = len(order)
        cols = extent * unit // sharers
        start = first * unit // cols
        ins.append(pl.BlockSpec((depth, cols), lambda s, place, start=start, n=sharers: (0, start + place[0] % n)))
        outs.append(pl.BlockSpec((depth, cols), lambda s, place: (0, 0)))
        shapes.append(jax.ShapeDtypeStruct((depth, cols), out_proj.dtype))
    return pl.pallas_call(
        cut_kernel,
        grid_spec=pltpu.PrefetchScalarGridSpec(num_scalar_prefetch=1, grid=(1,), in_specs=ins, out_specs=outs),
        out_shape=shapes,
        compiler_params=params(60),
        cost_estimate=cost(0, 2_000_000),
    )(place, *[out_proj] * len(SPLITS))


def toeplitz_kernel(base_ref, toeplitz_ref):
    tiles, stacked, reach = toeplitz_ref.shape
    per_tile = base_ref.shape[0] // tiles
    tok_len = stacked // per_tile
    for tile in range(tiles):
        for k in range(per_tile):
            g = tile * per_tile + k
            wide = jnp.broadcast_to(base_ref[g : g + 1, :], (tok_len, reach))
            shifted = pltpu.roll(wide, 0, 1, stride=1, stride_axis=0)
            toeplitz_ref[tile, pl.ds(k * tok_len, tok_len), :] = shifted.astype(jnp.bfloat16)


def build_toeplitz(conv_taps, tok_len):
    reach = 2 * tok_len
    per_tile = LANES // GROUP
    tiles = conv_taps.shape[0] // per_tile
    base = jnp.pad(conv_taps[:, ::-1].astype(jnp.float32), ((0, 0), (1, reach - TAPS - 1)))
    shape = jax.ShapeDtypeStruct((tiles, per_tile * tok_len, reach), jnp.bfloat16)
    return pl.pallas_call(
        toeplitz_kernel,
        grid=(1,),
        in_specs=[whole(base)],
        out_specs=whole(shape),
        out_shape=shape,
        compiler_params=params(8),
        cost_estimate=cost(4_000_000_000, 0),
    )(base)


def panel_kernel(place_ref, mine_ref, other_ref, *refs):
    out_ref = refs[-1]
    count, sharers, tok_len, _ = out_ref.shape
    beside = [ref.at[i] for ref in refs[sharers:-1] for i in range(ref.shape[0])]
    for k in range(sharers):
        total = jnp.dot(mine_ref[...], refs[k][...], preferred_element_type=jnp.float32)
        total += jnp.dot(other_ref[...], beside[k][...], preferred_element_type=jnp.float32)
        for w in range(count):
            out_ref[w, k] = total[w * tok_len : (w + 1) * tok_len].astype(out_ref.dtype)


def panel(place, mine, other, out_proj, beside, split, step, begin=0):
    count, tok_len, depth = mine.shape
    rows = count * tok_len
    unit = out_proj.shape[1] // SIXTEENTHS
    base, extent, order, _ = split
    sharers = len(order)
    piece_cols = extent * unit // sharers
    offset, cols = (part * unit // sharers for part in step)
    fixed = lambda shape: pl.BlockSpec(shape, lambda s, place: (0,) * len(shape))

    def own(k):
        start, per = (base * unit + offset) // cols, piece_cols // cols
        return pl.BlockSpec((depth, cols), lambda s, place: (0, start + (place[0] % sharers ^ k) * per))

    near = lambda a: pl.BlockSpec((a.shape[0], depth, cols), lambda s, place: (0, 0, offset // cols - begin * unit // sharers // cols))
    return pl.pallas_call(
        panel_kernel,
        grid_spec=pltpu.PrefetchScalarGridSpec(
            num_scalar_prefetch=1,
            grid=(1,),
            in_specs=[fixed((rows, depth))] * 2 + [own(k) for k in order] + [near(a) for a in beside],
            out_specs=fixed((count, sharers, tok_len, cols)),
        ),
        out_shape=jax.ShapeDtypeStruct((count, sharers, tok_len, cols), jnp.bfloat16),
        compiler_params=params(),
        cost_estimate=cost(400_000_000, 0),
    )(place, mine.reshape(rows, depth), other.reshape(rows, depth), *[out_proj] * sharers, *beside)


def residual_kernel(ids_ref, rows_ref, out_ref):
    names = lax.broadcasted_iota(jnp.int32, (rows_ref.shape[0], ids_ref.shape[1]), 0)
    one_hot = (names == ids_ref[...]).astype(jnp.float32).astype(jnp.bfloat16)
    out_ref[...] = lax.dot_general(
        one_hot, rows_ref[...], (((0,), (0,)), ((), ())), preferred_element_type=jnp.float32
    ).astype(jnp.bfloat16)


def residual(token_ids, embedding):
    vocab, width = embedding.shape
    tok_len = token_ids.shape[1]
    cols = width // 4
    return pl.pallas_call(
        residual_kernel,
        grid=(4,),
        in_specs=[whole(token_ids), pl.BlockSpec((vocab, cols), lambda i: (0, i))],
        out_specs=pl.BlockSpec((tok_len, cols), lambda i: (0, i)),
        out_shape=jax.ShapeDtypeStruct((tok_len, width), jnp.bfloat16),
        compiler_params=params(),
        cost_estimate=cost(400_000_000, 0),
    )(token_ids, embedding)


def place_kernel(split, step, place_ref, so_far_ref, near_ref, far_ref, out_ref):
    _, sharers, _, cols = near_ref.shape
    piece_cols = so_far_ref.shape[1] // sharers
    offset = step[0] * cols // step[1]
    out_ref[...] = so_far_ref[...]
    for i, k in enumerate(split[2]):
        first = (place_ref[0] % sharers ^ k) * piece_cols + offset
        total = near_ref[0, i].astype(jnp.float32) + far_ref[0, i].astype(jnp.float32)
        at = pl.ds(pl.multiple_of(first, LANES), cols)
        out_ref[:, at] = (so_far_ref[:, at].astype(jnp.float32) + total).astype(jnp.bfloat16)


def place_pieces(place, so_far, near, far, split, step):
    tok_len, width = so_far.shape
    base, extent, _, _ = split
    part = pl.BlockSpec((tok_len, extent * width // SIXTEENTHS), lambda s, place: (0, base // extent))
    one = pl.BlockSpec(near.shape, lambda s, place: (0, 0, 0, 0))
    return pl.pallas_call(
        functools.partial(place_kernel, split, step),
        grid_spec=pltpu.PrefetchScalarGridSpec(
            num_scalar_prefetch=1, grid=(1,), in_specs=[part, one, one], out_specs=part
        ),
        out_shape=jax.ShapeDtypeStruct(so_far.shape, so_far.dtype),
        input_output_aliases={1: 0},
        compiler_params=params(),
        cost_estimate=cost(0, 1_000_000),
    )(place, so_far, near, far)


def add(a, b):
    return (a.astype(jnp.float32) + b.astype(jnp.float32)).astype(jnp.bfloat16)


def per_device(token_ids, embedding, norm_gain, in_proj, short_taps, conv_taps, out_proj):
    tok_len = token_ids.shape[1]
    at = lax.axis_index("ctx").reshape(1).astype(jnp.int32)
    bits = exchange_bits()
    tie = lax.optimization_barrier
    beside_bit = bits[-2]

    early, late = cut_pieces(at, out_proj)
    early, late, conv_taps = tie((early, late, conv_taps))
    toeplitz = build_toeplitz(conv_taps, tok_len)
    ids = level_ids(token_ids, bits[:2])
    ids, toeplitz = tie((ids, toeplitz))
    for group in [bits[i : i + 2] for i in range(2, len(bits), 2)]:
        ids = level_ids(ids, group)
    early = swap(early, "fsdp", beside_bit)
    ids, in_proj, late = tie((ids, in_proj, late))
    late = swap(late, "fsdp", beside_bit)
    ids = with_lead(ids)
    table = project(embedding, norm_gain, in_proj)
    table, early = tie((table, early))
    middle = early.shape[1] // 2
    body_columns, head_columns = early[:, middle:], early[:, :middle]
    body_pair = jnp.stack([body_columns, swap(body_columns, "ctx", 2)])

    part = ids.shape[0] // 4
    quarters = [ids[n * part : (n + 1) * part] for n in range(4)]
    sent = mix(quarters[3], table, short_taps, toeplitz, tok_len)
    kept, sent = tie((jnp.concatenate([quarters[1], quarters[2], quarters[0]], axis=0), sent))
    other = [swap(sent, "fsdp", beside_bit)]
    head_columns, sent = tie((head_columns, sent))
    head_pair = jnp.stack([head_columns, swap(head_columns, "ctx", 2)])
    gated = mix(kept, table, short_taps, toeplitz, tok_len)
    gated, body_pair = tie((gated, body_pair))
    other.append(swap(gated[:part], "fsdp", beside_bit))
    mine = [gated[part : 2 * part], gated[2 * part :]]
    pairs = [None, (body_pair, swap(body_pair, "ctx", 1))]
    late_pair = jnp.stack([late, swap(late, "ctx", 1)])
    own_ids, gated = tie((token_ids, gated))
    out = residual(own_ids, embedding)
    late_pair, head_pair, out = tie((late_pair, head_pair, out))
    pairs[0] = (head_pair, swap(head_pair, "ctx", 1))
    pairs += [(columns, swap(columns, "ctx", 2)) for columns in (late_pair[:, :, :middle],)]
    (head, body, foot), tail = SPLITS[0][3], SPLITS[1][3]

    def send(pair, split, step, begin):
        away = panel(at, mine[0], other[0], out_proj, pair, split, step, begin)
        return away, swap(away, "fsdp", bits[-1])

    def sum_up(pair, split, step, begin, got):
        total = panel(at, mine[1], other[1], out_proj, pair, split, step, begin)
        for bit in reversed(bits[:-2]):
            half = total.shape[0] // 2
            far = add(total[half:], got[half:])
            total, got = add(total[:half], got[:half]), swap(far, "fsdp", bit)
        return far, (total, got, split, step)

    chunk = (pairs[1], SPLITS[0], body, body[0])
    away, got = send(*chunk)
    other[1], late_rest, _ = tie((other[1], late_pair[:, :, middle:], away))
    pairs.append((late_rest, swap(late_rest, "ctx", 2)))

    all_mine, all_other = (jnp.concatenate(parts, axis=0) for parts in (mine, other))
    total = panel(at, all_mine, all_other, out_proj, pairs[0], SPLITS[0], head)
    other[1], total = tie((other[1], total))
    total = total.reshape(2, part, *total.shape[1:])
    head_got = swap(total[:, part // 2 :], "fsdp", bits[-3])

    far, first_sum = sum_up(*chunk, got)
    mine[0], _ = tie((mine[0], far))
    head_got, _ = tie((head_got, far))
    total = add(total[:, : part // 2], head_got)
    for bit in reversed(bits[:-3]):
        half = total.shape[1] // 2
        total = add(total[:, :half], swap(total[:, half:], "fsdp", bit))
    head_sum = (total[1], swap(total[0], "fsdp", bits[-1]), SPLITS[0], head)
    sums = [first_sum]
    for pair, split, step, begin in (
        (pairs[2], SPLITS[1], tail[0], tail[0][0]),
        (pairs[3], SPLITS[1], tail[1], tail[1][0]),
        (pairs[0], SPLITS[0], foot, 0),
    ):
        away, got = send(pair, split, step, begin)
        mine[0], away = tie((mine[0], away))
        got, _ = tie((got, far))
        far, one = sum_up(pair, split, step, begin, got)
        sums.append(one)
    out = place_pieces(at, out, *head_sum)
    for one in sums:
        out = place_pieces(at, out, *one)
    return out[None]


def solution(mesh):
    return jax.shard_map(
        per_device,
        mesh=mesh,
        in_specs=(
            P("fsdp", "ctx"),
            P(),
            P(),
            P(None, None, "fsdp"),
            P(None, None, "fsdp"),
            P("fsdp", None),
            P("fsdp", None),
        ),
        out_specs=P("fsdp", "ctx", None),
        check_vma=False,
    )
```

```python
import functools

import jax
import jax.numpy as jnp
from jax import lax
from jax.experimental import pallas as pl
from jax.experimental.pallas import tpu as pltpu
from jax.sharding import PartitionSpec as P

GROUP = 16
TAPS = 128
SHORT = 3
LANES = 128
LEAD = 16
SPLITS = ((0, 8, (0, 2, 1, 3), ((0, 2), (4, 4), (2, 2))), (8, 8, (0, 1, 2, 3), ((0, 4), (4, 4))))
SIXTEENTHS = 16


def from_behind(x, axis, by):
    peers = lax.axis_size(axis)
    return lax.ppermute(x, axis, [(i, (i + by) % peers) for i in range(peers)])


def swap(x, axis, mask):
    peers = lax.axis_size(axis)
    return lax.ppermute(x, axis, [(i, i ^ mask) for i in range(peers)])


def exchange_bits():
    peers = lax.axis_size("fsdp")
    return [1 << b for b in reversed(range(peers.bit_length() - 1))]


def params(mib=24):
    return pltpu.CompilerParams(vmem_limit_bytes=mib * 1024 * 1024)


def cost(flops, bytes_accessed):
    return pl.CostEstimate(flops=flops, bytes_accessed=bytes_accessed, transcendentals=0)


def whole(array):
    return pl.BlockSpec(array.shape, lambda *_: (0,) * len(array.shape))


def level_ids(ids, group):
    masks = [0]
    for bit in group:
        masks += [mask | bit for mask in masks]
    return jnp.concatenate([ids] + [swap(ids, "fsdp", mask) for mask in masks[1:]], axis=0)


def with_lead(ids):
    tok_len = ids.shape[1]
    place = lax.axis_index("ctx")
    one = jnp.where(place >= 1, from_behind(ids, "ctx", 1), -1)
    two = jnp.where(place >= 2, from_behind(ids, "ctx", 2), -1)
    return jnp.concatenate([two[:, tok_len - LEAD :], one, ids], axis=1)


def table_kernel(rows_hbm, weight_hbm, gain_ref, table_ref, rows, weight, row_sems, weight_sems):
    count, width, panel_width = weight.shape
    parts, blocks = row_sems.shape[0], weight_sems.shape[1]
    each, deep = rows.shape[0] // parts, width // blocks
    row_copies = [
        pltpu.make_async_copy(rows_hbm.at[pl.ds(r * each, each)], rows.at[pl.ds(r * each, each)], row_sems.at[r])
        for r in range(parts)
    ]
    weight_copies = [
        [
            pltpu.make_async_copy(
                weight_hbm.at[i, pl.ds(k * deep, deep)], weight.at[i, pl.ds(k * deep, deep)], weight_sems.at[i, k]
            )
            for k in range(blocks)
        ]
        for i in range(count)
    ]
    for copy in row_copies + sum(weight_copies, []):
        copy.start()
    for r in range(parts):
        row_copies[r].wait()
        at = pl.ds(r * each, each)
        values = rows[at, :].astype(jnp.float32)
        inverse_rms = lax.rsqrt(jnp.mean(values * values, axis=-1, keepdims=True) + 1e-06)
        rows[at, :] = (values * inverse_rms * gain_ref[...]).astype(jnp.bfloat16)
    cols = min(256, panel_width)
    for i in range(count):
        for copy in weight_copies[i]:
            copy.wait()
        for first in range(0, panel_width, cols):
            at = slice(first, first + cols)
            part = jnp.dot(rows[...], weight[i, :, at], preferred_element_type=jnp.float32)
            table_ref[i, :, at] = part.astype(jnp.bfloat16)


def project(embedding, norm_gain, in_proj):
    vocab, width = embedding.shape
    count, _, panel_width = in_proj.shape
    hbm = pl.BlockSpec(memory_space=pltpu.HBM)
    shape = jax.ShapeDtypeStruct((count, vocab, panel_width), jnp.bfloat16)
    return pl.pallas_call(
        table_kernel,
        grid=(1,),
        in_specs=[hbm, hbm, pl.BlockSpec((1, width), lambda s: (0, 0))],
        out_specs=whole(shape),
        out_shape=shape,
        scratch_shapes=[
            pltpu.VMEM(embedding.shape, jnp.bfloat16),
            pltpu.VMEM(in_proj.shape, jnp.bfloat16),
            pltpu.SemaphoreType.DMA((8,)),
            pltpu.SemaphoreType.DMA((count, 4)),
        ],
        compiler_params=params(40),
        cost_estimate=cost(3_000_000_000, 0),
    )(embedding, in_proj, norm_gain.reshape(1, width))


def mixer_kernel(ids_ref, table_ref, short_ref, toeplitz, gated_ref, held_query, held):
    tok_len, panel_width = gated_ref.shape[1:]
    vocab = table_ref.shape[1]
    rows = ids_ref.shape[2]
    reach = 2 * tok_len
    lead = rows - reach
    tiles = panel_width // LANES
    per_tile = LANES // GROUP
    names = lax.broadcasted_iota(jnp.int32, (vocab, rows), 0)
    lane_group = lax.broadcasted_iota(jnp.int32, (tok_len, 2 * LANES), 1) % LANES // GROUP

    def look_up(one_hot, table):
        found = lax.dot_general(one_hot, table, (((0,), (0,)), ((), ())), preferred_element_type=jnp.float32)
        return found.astype(jnp.bfloat16).astype(jnp.float32)

    for v in range(2):
        one_hot = (names == ids_ref[v]).astype(jnp.float32).astype(jnp.bfloat16)
        held[v, 0] = look_up(one_hot, table_ref[1])
        held[v, 1] = look_up(one_hot, table_ref[2])
        held_query[v] = look_up(one_hot[:, rows - lead - tok_len :], table_ref[0])

    def featured(source, i, count, cols):
        total = short_ref[0, i : i + 1, cols] * source[pl.ds(lead, count), cols]
        for j in range(1, SHORT):
            total += short_ref[j, i : i + 1, cols] * source[pl.ds(lead - j, count), cols]
        return total

    for tile in range(tiles):
        cols = slice(tile * LANES, (tile + 1) * LANES)
        products = []
        for v in range(2):
            key = featured(held.at[v, 0], 1, reach, cols)
            value = featured(held.at[v, 1], 2, reach, cols)
            products.append((key * value).astype(jnp.bfloat16))
        both = jnp.concatenate(products, axis=1)
        filtered = None
        for k in range(per_tile):
            one = jnp.dot(
                toeplitz[tile, pl.ds(k * tok_len, tok_len), :], both, preferred_element_type=jnp.float32
            )
            filtered = one if k == 0 else jnp.where(lane_group == k, one, filtered)
        for v in range(2):
            query = featured(held_query.at[v], 0, tok_len, cols)
            gated_ref[v, :, cols] = (query * filtered[:, v * LANES : (v + 1) * LANES]).astype(jnp.bfloat16)


def mix(ids, table, short_taps, toeplitz, tok_len):
    windows, rows = ids.shape
    panel_width = table.shape[2]
    return pl.pallas_call(
        mixer_kernel,
        grid=(windows // 2,),
        in_specs=[pl.BlockSpec((2, 1, rows), lambda p: (p, 0, 0))]
        + [whole(array) for array in (table, short_taps, toeplitz)],
        out_specs=pl.BlockSpec((2, tok_len, panel_width), lambda p: (p, 0, 0)),
        out_shape=jax.ShapeDtypeStruct((windows, tok_len, panel_width), jnp.bfloat16),
        scratch_shapes=[
            pltpu.VMEM((2, LEAD + tok_len, panel_width), jnp.float32),
            pltpu.VMEM((2, 2, rows, panel_width), jnp.float32),
        ],
        compiler_params=params(),
        cost_estimate=cost(1_500_000_000, 0),
    )(ids.reshape(windows, 1, rows), table, short_taps, toeplitz)


def cut_kernel(place_ref, *refs):
    count = len(refs) // 2
    for source, piece in zip(refs[:count], refs[count:]):
        piece[...] = source[...]


def cut_pieces(place, out_proj):
    depth, width = out_proj.shape
    unit = width // SIXTEENTHS
    ins, outs, shapes = [], [], []
    for first, extent, order, _ in SPLITS:
        sharers = len(order)
        cols = extent * unit // sharers
        start = first * unit // cols
        ins.append(pl.BlockSpec((depth, cols), lambda s, place, start=start, n=sharers: (0, start + place[0] % n)))
        outs.append(pl.BlockSpec((depth, cols), lambda s, place: (0, 0)))
        shapes.append(jax.ShapeDtypeStruct((depth, cols), out_proj.dtype))
    return pl.pallas_call(
        cut_kernel,
        grid_spec=pltpu.PrefetchScalarGridSpec(num_scalar_prefetch=1, grid=(1,), in_specs=ins, out_specs=outs),
        out_shape=shapes,
        compiler_params=params(60),
        cost_estimate=cost(0, 2_000_000),
    )(place, *[out_proj] * len(SPLITS))


def toeplitz_kernel(base_ref, toeplitz_ref):
    tiles, stacked, reach = toeplitz_ref.shape
    per_tile = base_ref.shape[0] // tiles
    tok_len = stacked // per_tile
    for tile in range(tiles):
        for k in range(per_tile):
            g = tile * per_tile + k
            wide = jnp.broadcast_to(base_ref[g : g + 1, :], (tok_len, reach))
            shifted = pltpu.roll(wide, 0, 1, stride=1, stride_axis=0)
            toeplitz_ref[tile, pl.ds(k * tok_len, tok_len), :] = shifted.astype(jnp.bfloat16)


def build_toeplitz(conv_taps, tok_len):
    reach = 2 * tok_len
    per_tile = LANES // GROUP
    tiles = conv_taps.shape[0] // per_tile
    base = jnp.pad(conv_taps[:, ::-1].astype(jnp.float32), ((0, 0), (1, reach - TAPS - 1)))
    shape = jax.ShapeDtypeStruct((tiles, per_tile * tok_len, reach), jnp.bfloat16)
    return pl.pallas_call(
        toeplitz_kernel,
        grid=(1,),
        in_specs=[whole(base)],
        out_specs=whole(shape),
        out_shape=shape,
        compiler_params=params(8),
        cost_estimate=cost(0, 2_000_000),
    )(base)


def panel_kernel(place_ref, mine_ref, other_ref, *refs):
    out_ref = refs[-1]
    count, sharers, tok_len, _ = out_ref.shape
    beside = [ref.at[i] for ref in refs[sharers:-1] for i in range(ref.shape[0])]
    for k in range(sharers):
        total = jnp.dot(mine_ref[...], refs[k][...], preferred_element_type=jnp.float32)
        total += jnp.dot(other_ref[...], beside[k][...], preferred_element_type=jnp.float32)
        for w in range(count):
            out_ref[w, k] = total[w * tok_len : (w + 1) * tok_len].astype(out_ref.dtype)


def panel(place, mine, other, out_proj, beside, split, step, begin=0):
    count, tok_len, depth = mine.shape
    rows = count * tok_len
    unit = out_proj.shape[1] // SIXTEENTHS
    base, extent, order, _ = split
    sharers = len(order)
    piece_cols = extent * unit // sharers
    offset, cols = (part * unit // sharers for part in step)
    fixed = lambda shape: pl.BlockSpec(shape, lambda s, place: (0,) * len(shape))

    def own(k):
        start, per = (base * unit + offset) // cols, piece_cols // cols
        return pl.BlockSpec((depth, cols), lambda s, place: (0, start + (place[0] % sharers ^ k) * per))

    near = lambda a: pl.BlockSpec((a.shape[0], depth, cols), lambda s, place: (0, 0, offset // cols - begin * unit // sharers // cols))
    return pl.pallas_call(
        panel_kernel,
        grid_spec=pltpu.PrefetchScalarGridSpec(
            num_scalar_prefetch=1,
            grid=(1,),
            in_specs=[fixed((rows, depth))] * 2 + [own(k) for k in order] + [near(a) for a in beside],
            out_specs=fixed((count, sharers, tok_len, cols)),
        ),
        out_shape=jax.ShapeDtypeStruct((count, sharers, tok_len, cols), jnp.bfloat16),
        compiler_params=params(),
        cost_estimate=cost(400_000_000, 0),
    )(place, mine.reshape(rows, depth), other.reshape(rows, depth), *[out_proj] * sharers, *beside)


def residual_kernel(ids_ref, rows_ref, out_ref):
    names = lax.broadcasted_iota(jnp.int32, (rows_ref.shape[0], ids_ref.shape[1]), 0)
    one_hot = (names == ids_ref[...]).astype(jnp.float32).astype(jnp.bfloat16)
    out_ref[...] = lax.dot_general(
        one_hot, rows_ref[...], (((0,), (0,)), ((), ())), preferred_element_type=jnp.float32
    ).astype(jnp.bfloat16)


def residual(token_ids, embedding):
    vocab, width = embedding.shape
    tok_len = token_ids.shape[1]
    cols = width // 4
    return pl.pallas_call(
        residual_kernel,
        grid=(4,),
        in_specs=[whole(token_ids), pl.BlockSpec((vocab, cols), lambda i: (0, i))],
        out_specs=pl.BlockSpec((tok_len, cols), lambda i: (0, i)),
        out_shape=jax.ShapeDtypeStruct((tok_len, width), jnp.bfloat16),
        compiler_params=params(),
        cost_estimate=cost(400_000_000, 0),
    )(token_ids, embedding)


def place_kernel(split, step, place_ref, so_far_ref, near_ref, far_ref, out_ref):
    _, sharers, _, cols = near_ref.shape
    piece_cols = so_far_ref.shape[1] // sharers
    offset = step[0] * cols // step[1]
    out_ref[...] = so_far_ref[...]
    for i, k in enumerate(split[2]):
        first = (place_ref[0] % sharers ^ k) * piece_cols + offset
        total = near_ref[0, i].astype(jnp.float32) + far_ref[0, i].astype(jnp.float32)
        at = pl.ds(pl.multiple_of(first, LANES), cols)
        out_ref[:, at] = (so_far_ref[:, at].astype(jnp.float32) + total).astype(jnp.bfloat16)


def place_pieces(place, so_far, near, far, split, step):
    tok_len, width = so_far.shape
    base, extent, _, _ = split
    part = pl.BlockSpec((tok_len, extent * width // SIXTEENTHS), lambda s, place: (0, base // extent))
    one = pl.BlockSpec(near.shape, lambda s, place: (0, 0, 0, 0))
    return pl.pallas_call(
        functools.partial(place_kernel, split, step),
        grid_spec=pltpu.PrefetchScalarGridSpec(
            num_scalar_prefetch=1, grid=(1,), in_specs=[part, one, one], out_specs=part
        ),
        out_shape=jax.ShapeDtypeStruct(so_far.shape, so_far.dtype),
        input_output_aliases={1: 0},
        compiler_params=params(),
        cost_estimate=cost(0, 1_000_000),
    )(place, so_far, near, far)


def add(a, b):
    return (a.astype(jnp.float32) + b.astype(jnp.float32)).astype(jnp.bfloat16)


def per_device(token_ids, embedding, norm_gain, in_proj, short_taps, conv_taps, out_proj):
    tok_len = token_ids.shape[1]
    at = lax.axis_index("ctx").reshape(1).astype(jnp.int32)
    bits = exchange_bits()
    tie = lax.optimization_barrier
    beside_bit = bits[-2]

    early, late = cut_pieces(at, out_proj)
    early, late, conv_taps = tie((early, late, conv_taps))
    toeplitz = build_toeplitz(conv_taps, tok_len)
    ids = level_ids(token_ids, bits[:2])
    ids, toeplitz = tie((ids, toeplitz))
    for group in [bits[i : i + 2] for i in range(2, len(bits), 2)]:
        ids = level_ids(ids, group)
    early = swap(early, "fsdp", beside_bit)
    ids, in_proj, late = tie((ids, in_proj, late))
    late = swap(late, "fsdp", beside_bit)
    ids = with_lead(ids)
    table = project(embedding, norm_gain, in_proj)
    table, early = tie((table, early))
    middle = early.shape[1] // 2
    body_columns, head_columns = early[:, middle:], early[:, :middle]
    body_pair = jnp.stack([body_columns, swap(body_columns, "ctx", 2)])

    part = ids.shape[0] // 4
    quarters = [ids[n * part : (n + 1) * part] for n in range(4)]
    sent = mix(quarters[3], table, short_taps, toeplitz, tok_len)
    kept, sent = tie((jnp.concatenate([quarters[1], quarters[2], quarters[0]], axis=0), sent))
    other = [swap(sent, "fsdp", beside_bit)]
    head_columns, sent = tie((head_columns, sent))
    head_pair = jnp.stack([head_columns, swap(head_columns, "ctx", 2)])
    gated = mix(kept, table, short_taps, toeplitz, tok_len)
    gated, body_pair = tie((gated, body_pair))
    other.append(swap(gated[:part], "fsdp", beside_bit))
    mine = [gated[part : 2 * part], gated[2 * part :]]
    pairs = [None, (body_pair, swap(body_pair, "ctx", 1))]
    late_pair = jnp.stack([late, swap(late, "ctx", 1)])
    own_ids, gated = tie((token_ids, gated))
    out = residual(own_ids, embedding)
    late_pair, head_pair, out = tie((late_pair, head_pair, out))
    pairs[0] = (head_pair, swap(head_pair, "ctx", 1))
    pairs += [(columns, swap(columns, "ctx", 2)) for columns in (late_pair[:, :, :middle],)]
    (head, body, foot), tail = SPLITS[0][3], SPLITS[1][3]

    def send(pair, split, step, begin):
        away = panel(at, mine[0], other[0], out_proj, pair, split, step, begin)
        return away, swap(away, "fsdp", bits[-1])

    def sum_up(pair, split, step, begin, got):
        total = panel(at, mine[1], other[1], out_proj, pair, split, step, begin)
        for bit in reversed(bits[:-2]):
            half = total.shape[0] // 2
            far = add(total[half:], got[half:])
            total, got = add(total[:half], got[:half]), swap(far, "fsdp", bit)
        return far, (total, got, split, step)

    chunk = (pairs[1], SPLITS[0], body, body[0])
    away, got = send(*chunk)
    other[1], _ = tie((other[1], away))

    all_mine, all_other = (jnp.concatenate(parts, axis=0) for parts in (mine, other))
    total = panel(at, all_mine, all_other, out_proj, pairs[0], SPLITS[0], head)
    other[1], late_rest, total = tie((other[1], late_pair[:, :, middle:], total))
    pairs.append((late_rest, swap(late_rest, "ctx", 2)))
    total = total.reshape(2, part, *total.shape[1:])
    head_got = swap(total[:, part // 2 :], "fsdp", bits[-3])

    far, first_sum = sum_up(*chunk, got)
    mine[0], _ = tie((mine[0], far))
    head_got, _ = tie((head_got, far))
    total = add(total[:, : part // 2], head_got)
    for bit in reversed(bits[:-3]):
        half = total.shape[1] // 2
        total = add(total[:, :half], swap(total[:, half:], "fsdp", bit))
    head_sum = (total[1], swap(total[0], "fsdp", bits[-1]), SPLITS[0], head)
    sums = [first_sum]
    for pair, split, step, begin in (
        (pairs[2], SPLITS[1], tail[0], tail[0][0]),
        (pairs[3], SPLITS[1], tail[1], tail[1][0]),
        (pairs[0], SPLITS[0], foot, 0),
    ):
        away, got = send(pair, split, step, begin)
        mine[0], away = tie((mine[0], away))
        got, _ = tie((got, far))
        far, one = sum_up(pair, split, step, begin, got)
        sums.append(one)
    out = place_pieces(at, out, *head_sum)
    for one in sums:
        out = place_pieces(at, out, *one)
    return out[None]


def solution(mesh):
    return jax.shard_map(
        per_device,
        mesh=mesh,
        in_specs=(
            P("fsdp", "ctx"),
            P(),
            P(),
            P(None, None, "fsdp"),
            P(None, None, "fsdp"),
            P("fsdp", None),
            P("fsdp", None),
        ),
        out_specs=P("fsdp", "ctx", None),
        check_vma=False,
    )
```

```python
import functools

import jax
import jax.numpy as jnp
from jax import lax
from jax.experimental import pallas as pl
from jax.experimental.pallas import tpu as pltpu
from jax.sharding import PartitionSpec as P

GROUP = 16
TAPS = 128
SHORT = 3
LANES = 128
LEAD = 16
SPLITS = ((0, 8, (0, 2, 1, 3), ((0, 2), (4, 4), (2, 2))), (8, 8, (0, 1, 2, 3), ((0, 4), (4, 4))))
SIXTEENTHS = 16


def from_behind(x, axis, by):
    peers = lax.axis_size(axis)
    return lax.ppermute(x, axis, [(i, (i + by) % peers) for i in range(peers)])


def swap(x, axis, mask):
    peers = lax.axis_size(axis)
    return lax.ppermute(x, axis, [(i, i ^ mask) for i in range(peers)])


def exchange_bits():
    peers = lax.axis_size("fsdp")
    return [1 << b for b in reversed(range(peers.bit_length() - 1))]


def params(mib=24):
    return pltpu.CompilerParams(vmem_limit_bytes=mib * 1024 * 1024)


def cost(flops, bytes_accessed):
    return pl.CostEstimate(flops=flops, bytes_accessed=bytes_accessed, transcendentals=0)


def whole(array):
    return pl.BlockSpec(array.shape, lambda *_: (0,) * len(array.shape))


def level_ids(ids, group):
    masks = [0]
    for bit in group:
        masks += [mask | bit for mask in masks]
    return jnp.concatenate([ids] + [swap(ids, "fsdp", mask) for mask in masks[1:]], axis=0)


def with_lead(ids):
    tok_len = ids.shape[1]
    place = lax.axis_index("ctx")
    one = jnp.where(place >= 1, from_behind(ids, "ctx", 1), -1)
    two = jnp.where(place >= 2, from_behind(ids, "ctx", 2), -1)
    return jnp.concatenate([two[:, tok_len - LEAD :], one, ids], axis=1)


def table_kernel(rows_hbm, weight_hbm, gain_ref, table_ref, rows, weight, row_sems, weight_sems):
    count, width, panel_width = weight.shape
    parts, blocks = row_sems.shape[0], weight_sems.shape[1]
    each, deep = rows.shape[0] // parts, width // blocks
    row_copies = [
        pltpu.make_async_copy(rows_hbm.at[pl.ds(r * each, each)], rows.at[pl.ds(r * each, each)], row_sems.at[r])
        for r in range(parts)
    ]
    weight_copies = [
        [
            pltpu.make_async_copy(
                weight_hbm.at[i, pl.ds(k * deep, deep)], weight.at[i, pl.ds(k * deep, deep)], weight_sems.at[i, k]
            )
            for k in range(blocks)
        ]
        for i in range(count)
    ]
    for copy in row_copies + sum(weight_copies, []):
        copy.start()
    for r in range(parts):
        row_copies[r].wait()
        at = pl.ds(r * each, each)
        values = rows[at, :].astype(jnp.float32)
        inverse_rms = lax.rsqrt(jnp.mean(values * values, axis=-1, keepdims=True) + 1e-06)
        rows[at, :] = (values * inverse_rms * gain_ref[...]).astype(jnp.bfloat16)
    cols = min(256, panel_width)
    for i in range(count):
        for copy in weight_copies[i]:
            copy.wait()
        for first in range(0, panel_width, cols):
            at = slice(first, first + cols)
            part = jnp.dot(rows[...], weight[i, :, at], preferred_element_type=jnp.float32)
            table_ref[i, :, at] = part.astype(jnp.bfloat16)


def project(embedding, norm_gain, in_proj):
    vocab, width = embedding.shape
    count, _, panel_width = in_proj.shape
    hbm = pl.BlockSpec(memory_space=pltpu.HBM)
    shape = jax.ShapeDtypeStruct((count, vocab, panel_width), jnp.bfloat16)
    return pl.pallas_call(
        table_kernel,
        grid=(1,),
        in_specs=[hbm, hbm, pl.BlockSpec((1, width), lambda s: (0, 0))],
        out_specs=whole(shape),
        out_shape=shape,
        scratch_shapes=[
            pltpu.VMEM(embedding.shape, jnp.bfloat16),
            pltpu.VMEM(in_proj.shape, jnp.bfloat16),
            pltpu.SemaphoreType.DMA((8,)),
            pltpu.SemaphoreType.DMA((count, 4)),
        ],
        compiler_params=params(40),
        cost_estimate=cost(3_000_000_000, 0),
    )(embedding, in_proj, norm_gain.reshape(1, width))


def mixer_kernel(ids_ref, table_ref, short_ref, toeplitz, gated_ref, held_query, held):
    tok_len, panel_width = gated_ref.shape[1:]
    vocab = table_ref.shape[1]
    rows = ids_ref.shape[2]
    reach = 2 * tok_len
    lead = rows - reach
    tiles = panel_width // LANES
    per_tile = LANES // GROUP
    names = lax.broadcasted_iota(jnp.int32, (vocab, rows), 0)
    lane_group = lax.broadcasted_iota(jnp.int32, (tok_len, 2 * LANES), 1) % LANES // GROUP

    for v in range(2):
        one_hot = (names == ids_ref[v]).astype(jnp.float32).T.astype(jnp.bfloat16)
        held[v, 0] = jnp.dot(one_hot, table_ref[1], preferred_element_type=jnp.float32)
        held[v, 1] = jnp.dot(one_hot, table_ref[2], preferred_element_type=jnp.float32)
        held_query[v] = jnp.dot(one_hot[rows - lead - tok_len :], table_ref[0], preferred_element_type=jnp.float32)

    def featured(source, i, count, cols):
        total = short_ref[0, i : i + 1, cols] * source[pl.ds(lead, count), cols]
        for j in range(1, SHORT):
            total += short_ref[j, i : i + 1, cols] * source[pl.ds(lead - j, count), cols]
        return total

    for tile in range(tiles):
        cols = slice(tile * LANES, (tile + 1) * LANES)
        products = []
        for v in range(2):
            key = featured(held.at[v, 0], 1, reach, cols)
            value = featured(held.at[v, 1], 2, reach, cols)
            products.append((key * value).astype(jnp.bfloat16))
        both = jnp.concatenate(products, axis=1)
        filtered = None
        for k in range(per_tile):
            one = jnp.dot(
                toeplitz[tile, pl.ds(k * tok_len, tok_len), :], both, preferred_element_type=jnp.float32
            )
            filtered = one if k == 0 else jnp.where(lane_group == k, one, filtered)
        for v in range(2):
            query = featured(held_query.at[v], 0, tok_len, cols)
            gated_ref[v, :, cols] = (query * filtered[:, v * LANES : (v + 1) * LANES]).astype(jnp.bfloat16)


def mix(ids, table, short_taps, toeplitz, tok_len):
    windows, rows = ids.shape
    panel_width = table.shape[2]
    return pl.pallas_call(
        mixer_kernel,
        grid=(windows // 2,),
        in_specs=[pl.BlockSpec((2, 1, rows), lambda p: (p, 0, 0))]
        + [whole(array) for array in (table, short_taps, toeplitz)],
        out_specs=pl.BlockSpec((2, tok_len, panel_width), lambda p: (p, 0, 0)),
        out_shape=jax.ShapeDtypeStruct((windows, tok_len, panel_width), jnp.bfloat16),
        scratch_shapes=[
            pltpu.VMEM((2, LEAD + tok_len, panel_width), jnp.float32),
            pltpu.VMEM((2, 2, rows, panel_width), jnp.float32),
        ],
        compiler_params=params(),
        cost_estimate=cost(1_500_000_000, 0),
    )(ids.reshape(windows, 1, rows), table, short_taps, toeplitz)


def cut_kernel(place_ref, *refs):
    count = len(refs) // 2
    for source, piece in zip(refs[:count], refs[count:]):
        piece[...] = source[...]


def cut_pieces(place, out_proj):
    depth, width = out_proj.shape
    unit = width // SIXTEENTHS
    ins, outs, shapes = [], [], []
    for first, extent, order, _ in SPLITS:
        sharers = len(order)
        cols = extent * unit // sharers
        start = first * unit // cols
        ins.append(pl.BlockSpec((depth, cols), lambda s, place, start=start, n=sharers: (0, start + place[0] % n)))
        outs.append(pl.BlockSpec((depth, cols), lambda s, place: (0, 0)))
        shapes.append(jax.ShapeDtypeStruct((depth, cols), out_proj.dtype))
    return pl.pallas_call(
        cut_kernel,
        grid_spec=pltpu.PrefetchScalarGridSpec(num_scalar_prefetch=1, grid=(1,), in_specs=ins, out_specs=outs),
        out_shape=shapes,
        compiler_params=params(60),
        cost_estimate=cost(0, 2_000_000),
    )(place, *[out_proj] * len(SPLITS))


def toeplitz_kernel(base_ref, toeplitz_ref):
    tiles, stacked, reach = toeplitz_ref.shape
    per_tile = base_ref.shape[0] // tiles
    tok_len = stacked // per_tile
    for tile in range(tiles):
        for k in range(per_tile):
            g = tile * per_tile + k
            wide = jnp.broadcast_to(base_ref[g : g + 1, :], (tok_len, reach))
            shifted = pltpu.roll(wide, 0, 1, stride=1, stride_axis=0)
            toeplitz_ref[tile, pl.ds(k * tok_len, tok_len), :] = shifted.astype(jnp.bfloat16)


def build_toeplitz(conv_taps, tok_len):
    reach = 2 * tok_len
    per_tile = LANES // GROUP
    tiles = conv_taps.shape[0] // per_tile
    base = jnp.pad(conv_taps[:, ::-1].astype(jnp.float32), ((0, 0), (1, reach - TAPS - 1)))
    shape = jax.ShapeDtypeStruct((tiles, per_tile * tok_len, reach), jnp.bfloat16)
    return pl.pallas_call(
        toeplitz_kernel,
        grid=(1,),
        in_specs=[whole(base)],
        out_specs=whole(shape),
        out_shape=shape,
        compiler_params=params(8),
        cost_estimate=cost(0, 2_000_000),
    )(base)


def panel_kernel(place_ref, mine_ref, other_ref, *refs):
    out_ref = refs[-1]
    count, sharers, tok_len, _ = out_ref.shape
    beside = [ref.at[i] for ref in refs[sharers:-1] for i in range(ref.shape[0])]
    for k in range(sharers):
        total = jnp.dot(mine_ref[...], refs[k][...], preferred_element_type=jnp.float32)
        total += jnp.dot(other_ref[...], beside[k][...], preferred_element_type=jnp.float32)
        for w in range(count):
            out_ref[w, k] = total[w * tok_len : (w + 1) * tok_len].astype(out_ref.dtype)


def panel(place, mine, other, out_proj, beside, split, step, begin=0):
    count, tok_len, depth = mine.shape
    rows = count * tok_len
    unit = out_proj.shape[1] // SIXTEENTHS
    base, extent, order, _ = split
    sharers = len(order)
    piece_cols = extent * unit // sharers
    offset, cols = (part * unit // sharers for part in step)
    fixed = lambda shape: pl.BlockSpec(shape, lambda s, place: (0,) * len(shape))

    def own(k):
        start, per = (base * unit + offset) // cols, piece_cols // cols
        return pl.BlockSpec((depth, cols), lambda s, place: (0, start + (place[0] % sharers ^ k) * per))

    near = lambda a: pl.BlockSpec((a.shape[0], depth, cols), lambda s, place: (0, 0, offset // cols - begin * unit // sharers // cols))
    return pl.pallas_call(
        panel_kernel,
        grid_spec=pltpu.PrefetchScalarGridSpec(
            num_scalar_prefetch=1,
            grid=(1,),
            in_specs=[fixed((rows, depth))] * 2 + [own(k) for k in order] + [near(a) for a in beside],
            out_specs=fixed((count, sharers, tok_len, cols)),
        ),
        out_shape=jax.ShapeDtypeStruct((count, sharers, tok_len, cols), jnp.bfloat16),
        compiler_params=params(),
        cost_estimate=cost(400_000_000, 0),
    )(place, mine.reshape(rows, depth), other.reshape(rows, depth), *[out_proj] * sharers, *beside)


def residual_kernel(ids_ref, rows_ref, out_ref):
    names = lax.broadcasted_iota(jnp.int32, (rows_ref.shape[0], ids_ref.shape[1]), 0)
    one_hot = (names == ids_ref[...]).astype(jnp.float32).astype(jnp.bfloat16)
    out_ref[...] = lax.dot_general(
        one_hot, rows_ref[...], (((0,), (0,)), ((), ())), preferred_element_type=jnp.float32
    ).astype(jnp.bfloat16)


def residual(token_ids, embedding):
    vocab, width = embedding.shape
    tok_len = token_ids.shape[1]
    cols = width // 4
    return pl.pallas_call(
        residual_kernel,
        grid=(4,),
        in_specs=[whole(token_ids), pl.BlockSpec((vocab, cols), lambda i: (0, i))],
        out_specs=pl.BlockSpec((tok_len, cols), lambda i: (0, i)),
        out_shape=jax.ShapeDtypeStruct((tok_len, width), jnp.bfloat16),
        compiler_params=params(),
        cost_estimate=cost(400_000_000, 0),
    )(token_ids, embedding)


def place_kernel(split, step, place_ref, so_far_ref, near_ref, far_ref, out_ref):
    _, sharers, _, cols = near_ref.shape
    piece_cols = so_far_ref.shape[1] // sharers
    offset = step[0] * cols // step[1]
    out_ref[...] = so_far_ref[...]
    for i, k in enumerate(split[2]):
        first = (place_ref[0] % sharers ^ k) * piece_cols + offset
        total = near_ref[0, i].astype(jnp.float32) + far_ref[0, i].astype(jnp.float32)
        at = pl.ds(pl.multiple_of(first, LANES), cols)
        out_ref[:, at] = (so_far_ref[:, at].astype(jnp.float32) + total).astype(jnp.bfloat16)


def place_pieces(place, so_far, near, far, split, step):
    tok_len, width = so_far.shape
    base, extent, _, _ = split
    part = pl.BlockSpec((tok_len, extent * width // SIXTEENTHS), lambda s, place: (0, base // extent))
    one = pl.BlockSpec(near.shape, lambda s, place: (0, 0, 0, 0))
    return pl.pallas_call(
        functools.partial(place_kernel, split, step),
        grid_spec=pltpu.PrefetchScalarGridSpec(
            num_scalar_prefetch=1, grid=(1,), in_specs=[part, one, one], out_specs=part
        ),
        out_shape=jax.ShapeDtypeStruct(so_far.shape, so_far.dtype),
        input_output_aliases={1: 0},
        compiler_params=params(),
        cost_estimate=cost(0, 1_000_000),
    )(place, so_far, near, far)


def add(a, b):
    return (a.astype(jnp.float32) + b.astype(jnp.float32)).astype(jnp.bfloat16)


def per_device(token_ids, embedding, norm_gain, in_proj, short_taps, conv_taps, out_proj):
    tok_len = token_ids.shape[1]
    at = lax.axis_index("ctx").reshape(1).astype(jnp.int32)
    bits = exchange_bits()
    tie = lax.optimization_barrier
    beside_bit = bits[-2]

    early, late = cut_pieces(at, out_proj)
    early, late, conv_taps = tie((early, late, conv_taps))
    toeplitz = build_toeplitz(conv_taps, tok_len)
    ids = level_ids(token_ids, bits[:2])
    ids, toeplitz = tie((ids, toeplitz))
    for group in [bits[i : i + 2] for i in range(2, len(bits), 2)]:
        ids = level_ids(ids, group)
    early = swap(early, "fsdp", beside_bit)
    ids, in_proj, late = tie((ids, in_proj, late))
    late = swap(late, "fsdp", beside_bit)
    ids = with_lead(ids)
    table = project(embedding, norm_gain, in_proj)
    table, early = tie((table, early))
    middle = early.shape[1] // 2
    body_columns, head_columns = early[:, middle:], early[:, :middle]
    body_pair = jnp.stack([body_columns, swap(body_columns, "ctx", 2)])

    part = ids.shape[0] // 4
    quarters = [ids[n * part : (n + 1) * part] for n in range(4)]
    sent = mix(quarters[3], table, short_taps, toeplitz, tok_len)
    kept, sent = tie((jnp.concatenate([quarters[1], quarters[2], quarters[0]], axis=0), sent))
    other = [swap(sent, "fsdp", beside_bit)]
    head_columns, sent = tie((head_columns, sent))
    head_pair = jnp.stack([head_columns, swap(head_columns, "ctx", 2)])
    gated = mix(kept, table, short_taps, toeplitz, tok_len)
    gated, body_pair = tie((gated, body_pair))
    other.append(swap(gated[:part], "fsdp", beside_bit))
    mine = [gated[part : 2 * part], gated[2 * part :]]
    pairs = [None, (body_pair, swap(body_pair, "ctx", 1))]
    late_pair = jnp.stack([late, swap(late, "ctx", 1)])
    own_ids, gated = tie((token_ids, gated))
    out = residual(own_ids, embedding)
    late_pair, head_pair, out = tie((late_pair, head_pair, out))
    pairs[0] = (head_pair, swap(head_pair, "ctx", 1))
    pairs += [(columns, swap(columns, "ctx", 2)) for columns in (late_pair[:, :, :middle],)]
    (head, body, foot), tail = SPLITS[0][3], SPLITS[1][3]

    def send(pair, split, step, begin):
        away = panel(at, mine[0], other[0], out_proj, pair, split, step, begin)
        return away, swap(away, "fsdp", bits[-1])

    def sum_up(pair, split, step, begin, got):
        total = panel(at, mine[1], other[1], out_proj, pair, split, step, begin)
        for bit in reversed(bits[:-2]):
            half = total.shape[0] // 2
            far = add(total[half:], got[half:])
            total, got = add(total[:half], got[:half]), swap(far, "fsdp", bit)
        return far, (total, got, split, step)

    chunk = (pairs[1], SPLITS[0], body, body[0])
    away, got = send(*chunk)
    other[1], late_rest, _ = tie((other[1], late_pair[:, :, middle:], away))
    pairs.append((late_rest, swap(late_rest, "ctx", 2)))

    all_mine, all_other = (jnp.concatenate(parts, axis=0) for parts in (mine, other))
    total = panel(at, all_mine, all_other, out_proj, pairs[0], SPLITS[0], head)
    other[1], total = tie((other[1], total))
    total = total.reshape(2, part, *total.shape[1:])
    head_got = swap(total[:, part // 2 :], "fsdp", bits[-3])

    far, first_sum = sum_up(*chunk, got)
    mine[0], _ = tie((mine[0], far))
    head_got, _ = tie((head_got, far))
    total = add(total[:, : part // 2], head_got)
    for bit in reversed(bits[:-3]):
        half = total.shape[1] // 2
        total = add(total[:, :half], swap(total[:, half:], "fsdp", bit))
    head_sum = (total[1], swap(total[0], "fsdp", bits[-1]), SPLITS[0], head)
    sums = [first_sum]
    for pair, split, step, begin in (
        (pairs[2], SPLITS[1], tail[0], tail[0][0]),
        (pairs[3], SPLITS[1], tail[1], tail[1][0]),
        (pairs[0], SPLITS[0], foot, 0),
    ):
        away, got = send(pair, split, step, begin)
        mine[0], away = tie((mine[0], away))
        got, _ = tie((got, far))
        far, one = sum_up(pair, split, step, begin, got)
        sums.append(one)
    out = place_pieces(at, out, *head_sum)
    for one in sums:
        out = place_pieces(at, out, *one)
    return out[None]


def solution(mesh):
    return jax.shard_map(
        per_device,
        mesh=mesh,
        in_specs=(
            P("fsdp", "ctx"),
            P(),
            P(),
            P(None, None, "fsdp"),
            P(None, None, "fsdp"),
            P("fsdp", None),
            P("fsdp", None),
        ),
        out_specs=P("fsdp", "ctx", None),
        check_vma=False,
    )
```

```python
import functools

import jax
import jax.numpy as jnp
from jax import lax
from jax.experimental import pallas as pl
from jax.experimental.pallas import tpu as pltpu
from jax.sharding import PartitionSpec as P

GROUP = 16
TAPS = 128
SHORT = 3
LANES = 128
LEAD = 16
SPLITS = ((0, 8, (0, 2, 1, 3), ((0, 2), (4, 4), (2, 2))), (8, 8, (0, 1, 2, 3), ((0, 4), (4, 4))))
SIXTEENTHS = 16


def from_behind(x, axis, by):
    peers = lax.axis_size(axis)
    return lax.ppermute(x, axis, [(i, (i + by) % peers) for i in range(peers)])


def swap(x, axis, mask):
    peers = lax.axis_size(axis)
    return lax.ppermute(x, axis, [(i, i ^ mask) for i in range(peers)])


def exchange_bits():
    peers = lax.axis_size("fsdp")
    return [1 << b for b in reversed(range(peers.bit_length() - 1))]


def params(mib=24):
    return pltpu.CompilerParams(vmem_limit_bytes=mib * 1024 * 1024)


def cost(flops, bytes_accessed):
    return pl.CostEstimate(flops=flops, bytes_accessed=bytes_accessed, transcendentals=0)


def whole(array):
    return pl.BlockSpec(array.shape, lambda *_: (0,) * len(array.shape))


def level_ids(ids, group):
    masks = [0]
    for bit in group:
        masks += [mask | bit for mask in masks]
    return jnp.concatenate([ids] + [swap(ids, "fsdp", mask) for mask in masks[1:]], axis=0)


def with_lead(ids):
    tok_len = ids.shape[1]
    place = lax.axis_index("ctx")
    one = jnp.where(place >= 1, from_behind(ids, "ctx", 1), -1)
    two = jnp.where(place >= 2, from_behind(ids, "ctx", 2), -1)
    return jnp.concatenate([two[:, tok_len - LEAD :], one, ids], axis=1)


def table_kernel(rows_hbm, weight_hbm, gain_ref, table_ref, rows, weight, row_sems, weight_sems):
    count, width, panel_width = weight.shape
    parts, blocks = row_sems.shape[0], weight_sems.shape[1]
    each, deep = rows.shape[0] // parts, width // blocks
    row_copies = [
        pltpu.make_async_copy(rows_hbm.at[pl.ds(r * each, each)], rows.at[pl.ds(r * each, each)], row_sems.at[r])
        for r in range(parts)
    ]
    weight_copies = [
        [
            pltpu.make_async_copy(
                weight_hbm.at[i, pl.ds(k * deep, deep)], weight.at[i, pl.ds(k * deep, deep)], weight_sems.at[i, k]
            )
            for k in range(blocks)
        ]
        for i in range(count)
    ]
    for copy in row_copies + sum(weight_copies, []):
        copy.start()
    for r in range(parts):
        row_copies[r].wait()
        at = pl.ds(r * each, each)
        values = rows[at, :].astype(jnp.float32)
        inverse_rms = lax.rsqrt(jnp.mean(values * values, axis=-1, keepdims=True) + 1e-06)
        rows[at, :] = (values * inverse_rms * gain_ref[...]).astype(jnp.bfloat16)
    cols = min(256, panel_width)
    for i in range(count):
        for copy in weight_copies[i]:
            copy.wait()
        for first in range(0, panel_width, cols):
            at = slice(first, first + cols)
            part = jnp.dot(rows[...], weight[i, :, at], preferred_element_type=jnp.float32)
            table_ref[i, :, at] = part.astype(jnp.bfloat16)


def project(embedding, norm_gain, in_proj):
    vocab, width = embedding.shape
    count, _, panel_width = in_proj.shape
    hbm = pl.BlockSpec(memory_space=pltpu.HBM)
    shape = jax.ShapeDtypeStruct((count, vocab, panel_width), jnp.bfloat16)
    return pl.pallas_call(
        table_kernel,
        grid=(1,),
        in_specs=[hbm, hbm, pl.BlockSpec((1, width), lambda s: (0, 0))],
        out_specs=whole(shape),
        out_shape=shape,
        scratch_shapes=[
            pltpu.VMEM(embedding.shape, jnp.bfloat16),
            pltpu.VMEM(in_proj.shape, jnp.bfloat16),
            pltpu.SemaphoreType.DMA((8,)),
            pltpu.SemaphoreType.DMA((count, 4)),
        ],
        compiler_params=params(40),
        cost_estimate=cost(3_000_000_000, 0),
    )(embedding, in_proj, norm_gain.reshape(1, width))


def mixer_kernel(ids_ref, table_ref, short_ref, toeplitz, gated_ref, held_query, held):
    tok_len, panel_width = gated_ref.shape[1:]
    vocab = table_ref.shape[1]
    rows = ids_ref.shape[2]
    reach = 2 * tok_len
    lead = rows - reach
    tiles = panel_width // LANES
    per_tile = LANES // GROUP
    names = lax.broadcasted_iota(jnp.int32, (vocab, rows), 0)
    lane_group = lax.broadcasted_iota(jnp.int32, (tok_len, 2 * LANES), 1) % LANES // GROUP

    for v in range(2):
        one_hot = (names == ids_ref[v]).astype(jnp.float32).T.astype(jnp.bfloat16)
        held[v, 0] = jnp.dot(one_hot, table_ref[1], preferred_element_type=jnp.float32)
        held[v, 1] = jnp.dot(one_hot, table_ref[2], preferred_element_type=jnp.float32)
        held_query[v] = jnp.dot(one_hot[rows - lead - tok_len :], table_ref[0], preferred_element_type=jnp.float32)

    def featured(source, i, count, cols):
        total = short_ref[0, i : i + 1, cols] * source[pl.ds(lead, count), cols]
        for j in range(1, SHORT):
            total += short_ref[j, i : i + 1, cols] * source[pl.ds(lead - j, count), cols]
        return total

    for tile in range(tiles):
        cols = slice(tile * LANES, (tile + 1) * LANES)
        products = []
        for v in range(2):
            key = featured(held.at[v, 0], 1, reach, cols)
            value = featured(held.at[v, 1], 2, reach, cols)
            products.append((key * value).astype(jnp.bfloat16))
        both = jnp.concatenate(products, axis=1)
        stacked = jnp.dot(toeplitz[tile], both, preferred_element_type=jnp.float32)
        filtered = stacked[:tok_len]
        for k in range(1, per_tile):
            filtered = jnp.where(lane_group == k, stacked[k * tok_len : (k + 1) * tok_len], filtered)
        for v in range(2):
            query = featured(held_query.at[v], 0, tok_len, cols)
            gated_ref[v, :, cols] = (query * filtered[:, v * LANES : (v + 1) * LANES]).astype(jnp.bfloat16)


def mix(ids, table, short_taps, toeplitz, tok_len):
    windows, rows = ids.shape
    panel_width = table.shape[2]
    return pl.pallas_call(
        mixer_kernel,
        grid=(windows // 2,),
        in_specs=[pl.BlockSpec((2, 1, rows), lambda p: (p, 0, 0))]
        + [whole(array) for array in (table, short_taps, toeplitz)],
        out_specs=pl.BlockSpec((2, tok_len, panel_width), lambda p: (p, 0, 0)),
        out_shape=jax.ShapeDtypeStruct((windows, tok_len, panel_width), jnp.bfloat16),
        scratch_shapes=[
            pltpu.VMEM((2, LEAD + tok_len, panel_width), jnp.float32),
            pltpu.VMEM((2, 2, rows, panel_width), jnp.float32),
        ],
        compiler_params=params(),
        cost_estimate=cost(1_500_000_000, 0),
    )(ids.reshape(windows, 1, rows), table, short_taps, toeplitz)


def cut_kernel(place_ref, *refs):
    count = len(refs) // 2
    for source, piece in zip(refs[:count], refs[count:]):
        piece[...] = source[...]


def cut_pieces(place, out_proj):
    depth, width = out_proj.shape
    unit = width // SIXTEENTHS
    ins, outs, shapes = [], [], []
    for first, extent, order, _ in SPLITS:
        sharers = len(order)
        cols = extent * unit // sharers
        start = first * unit // cols
        ins.append(pl.BlockSpec((depth, cols), lambda s, place, start=start, n=sharers: (0, start + place[0] % n)))
        outs.append(pl.BlockSpec((depth, cols), lambda s, place: (0, 0)))
        shapes.append(jax.ShapeDtypeStruct((depth, cols), out_proj.dtype))
    return pl.pallas_call(
        cut_kernel,
        grid_spec=pltpu.PrefetchScalarGridSpec(num_scalar_prefetch=1, grid=(1,), in_specs=ins, out_specs=outs),
        out_shape=shapes,
        compiler_params=params(60),
        cost_estimate=cost(0, 2_000_000),
    )(place, *[out_proj] * len(SPLITS))


def toeplitz_kernel(base_ref, toeplitz_ref):
    tiles, stacked, reach = toeplitz_ref.shape
    per_tile = base_ref.shape[0] // tiles
    tok_len = stacked // per_tile
    for tile in range(tiles):
        for k in range(per_tile):
            g = tile * per_tile + k
            wide = jnp.broadcast_to(base_ref[g : g + 1, :], (tok_len, reach))
            shifted = pltpu.roll(wide, 0, 1, stride=1, stride_axis=0)
            toeplitz_ref[tile, pl.ds(k * tok_len, tok_len), :] = shifted.astype(jnp.bfloat16)


def build_toeplitz(conv_taps, tok_len):
    reach = 2 * tok_len
    per_tile = LANES // GROUP
    tiles = conv_taps.shape[0] // per_tile
    base = jnp.pad(conv_taps[:, ::-1].astype(jnp.float32), ((0, 0), (1, reach - TAPS - 1)))
    shape = jax.ShapeDtypeStruct((tiles, per_tile * tok_len, reach), jnp.bfloat16)
    return pl.pallas_call(
        toeplitz_kernel,
        grid=(1,),
        in_specs=[whole(base)],
        out_specs=whole(shape),
        out_shape=shape,
        compiler_params=params(8),
        cost_estimate=cost(0, 2_000_000),
    )(base)


def panel_kernel(place_ref, mine_ref, other_ref, *refs):
    out_ref = refs[-1]
    count, sharers, tok_len, _ = out_ref.shape
    beside = [ref.at[i] for ref in refs[sharers:-1] for i in range(ref.shape[0])]
    for k in range(sharers):
        total = jnp.dot(mine_ref[...], refs[k][...], preferred_element_type=jnp.float32)
        total += jnp.dot(other_ref[...], beside[k][...], preferred_element_type=jnp.float32)
        for w in range(count):
            out_ref[w, k] = total[w * tok_len : (w + 1) * tok_len].astype(out_ref.dtype)


def panel(place, mine, other, out_proj, beside, split, step, begin=0):
    count, tok_len, depth = mine.shape
    rows = count * tok_len
    unit = out_proj.shape[1] // SIXTEENTHS
    base, extent, order, _ = split
    sharers = len(order)
    piece_cols = extent * unit // sharers
    offset, cols = (part * unit // sharers for part in step)
    fixed = lambda shape: pl.BlockSpec(shape, lambda s, place: (0,) * len(shape))

    def own(k):
        start, per = (base * unit + offset) // cols, piece_cols // cols
        return pl.BlockSpec((depth, cols), lambda s, place: (0, start + (place[0] % sharers ^ k) * per))

    near = lambda a: pl.BlockSpec((a.shape[0], depth, cols), lambda s, place: (0, 0, offset // cols - begin * unit // sharers // cols))
    return pl.pallas_call(
        panel_kernel,
        grid_spec=pltpu.PrefetchScalarGridSpec(
            num_scalar_prefetch=1,
            grid=(1,),
            in_specs=[fixed((rows, depth))] * 2 + [own(k) for k in order] + [near(a) for a in beside],
            out_specs=fixed((count, sharers, tok_len, cols)),
        ),
        out_shape=jax.ShapeDtypeStruct((count, sharers, tok_len, cols), jnp.bfloat16),
        compiler_params=params(),
        cost_estimate=cost(400_000_000, 0),
    )(place, mine.reshape(rows, depth), other.reshape(rows, depth), *[out_proj] * sharers, *beside)


def residual_kernel(ids_ref, rows_ref, out_ref):
    names = lax.broadcasted_iota(jnp.int32, (rows_ref.shape[0], ids_ref.shape[1]), 0)
    one_hot = (names == ids_ref[...]).astype(jnp.float32).astype(jnp.bfloat16)
    out_ref[...] = lax.dot_general(
        one_hot, rows_ref[...], (((0,), (0,)), ((), ())), preferred_element_type=jnp.float32
    ).astype(jnp.bfloat16)


def residual(token_ids, embedding):
    vocab, width = embedding.shape
    tok_len = token_ids.shape[1]
    cols = width // 4
    return pl.pallas_call(
        residual_kernel,
        grid=(4,),
        in_specs=[whole(token_ids), pl.BlockSpec((vocab, cols), lambda i: (0, i))],
        out_specs=pl.BlockSpec((tok_len, cols), lambda i: (0, i)),
        out_shape=jax.ShapeDtypeStruct((tok_len, width), jnp.bfloat16),
        compiler_params=params(),
        cost_estimate=cost(400_000_000, 0),
    )(token_ids, embedding)


def place_kernel(split, step, place_ref, so_far_ref, near_ref, far_ref, out_ref):
    _, sharers, _, cols = near_ref.shape
    piece_cols = so_far_ref.shape[1] // sharers
    offset = step[0] * cols // step[1]
    out_ref[...] = so_far_ref[...]
    for i, k in enumerate(split[2]):
        first = (place_ref[0] % sharers ^ k) * piece_cols + offset
        total = near_ref[0, i].astype(jnp.float32) + far_ref[0, i].astype(jnp.float32)
        at = pl.ds(pl.multiple_of(first, LANES), cols)
        out_ref[:, at] = (so_far_ref[:, at].astype(jnp.float32) + total).astype(jnp.bfloat16)


def place_pieces(place, so_far, near, far, split, step):
    tok_len, width = so_far.shape
    base, extent, _, _ = split
    part = pl.BlockSpec((tok_len, extent * width // SIXTEENTHS), lambda s, place: (0, base // extent))
    one = pl.BlockSpec(near.shape, lambda s, place: (0, 0, 0, 0))
    return pl.pallas_call(
        functools.partial(place_kernel, split, step),
        grid_spec=pltpu.PrefetchScalarGridSpec(
            num_scalar_prefetch=1, grid=(1,), in_specs=[part, one, one], out_specs=part
        ),
        out_shape=jax.ShapeDtypeStruct(so_far.shape, so_far.dtype),
        input_output_aliases={1: 0},
        compiler_params=params(),
        cost_estimate=cost(0, 1_000_000),
    )(place, so_far, near, far)


def add(a, b):
    return (a.astype(jnp.float32) + b.astype(jnp.float32)).astype(jnp.bfloat16)


def per_device(token_ids, embedding, norm_gain, in_proj, short_taps, conv_taps, out_proj):
    tok_len = token_ids.shape[1]
    at = lax.axis_index("ctx").reshape(1).astype(jnp.int32)
    bits = exchange_bits()
    tie = lax.optimization_barrier
    beside_bit = bits[-2]

    early, late = cut_pieces(at, out_proj)
    early, late, conv_taps = tie((early, late, conv_taps))
    toeplitz = build_toeplitz(conv_taps, tok_len)
    ids = level_ids(token_ids, bits[:2])
    ids, toeplitz = tie((ids, toeplitz))
    for group in [bits[i : i + 2] for i in range(2, len(bits), 2)]:
        ids = level_ids(ids, group)
    early = swap(early, "fsdp", beside_bit)
    ids, in_proj, late = tie((ids, in_proj, late))
    late = swap(late, "fsdp", beside_bit)
    ids = with_lead(ids)
    table = project(embedding, norm_gain, in_proj)
    table, early = tie((table, early))
    middle = early.shape[1] // 2
    body_columns, head_columns = early[:, middle:], early[:, :middle]
    body_pair = jnp.stack([body_columns, swap(body_columns, "ctx", 2)])

    part = ids.shape[0] // 4
    quarters = [ids[n * part : (n + 1) * part] for n in range(4)]
    sent = mix(quarters[3], table, short_taps, toeplitz, tok_len)
    kept, sent = tie((jnp.concatenate([quarters[1], quarters[2], quarters[0]], axis=0), sent))
    other = [swap(sent, "fsdp", beside_bit)]
    head_columns, sent = tie((head_columns, sent))
    head_pair = jnp.stack([head_columns, swap(head_columns, "ctx", 2)])
    gated = mix(kept, table, short_taps, toeplitz, tok_len)
    gated, body_pair = tie((gated, body_pair))
    other.append(swap(gated[:part], "fsdp", beside_bit))
    mine = [gated[part : 2 * part], gated[2 * part :]]
    pairs = [None, (body_pair, swap(body_pair, "ctx", 1))]
    late_pair = jnp.stack([late, swap(late, "ctx", 1)])
    own_ids, gated = tie((token_ids, gated))
    out = residual(own_ids, embedding)
    late_pair, head_pair, out = tie((late_pair, head_pair, out))
    pairs[0] = (head_pair, swap(head_pair, "ctx", 1))
    pairs += [(columns, swap(columns, "ctx", 2)) for columns in (late_pair[:, :, :middle],)]
    (head, body, foot), tail = SPLITS[0][3], SPLITS[1][3]

    def send(pair, split, step, begin):
        away = panel(at, mine[0], other[0], out_proj, pair, split, step, begin)
        return away, swap(away, "fsdp", bits[-1])

    def sum_up(pair, split, step, begin, got):
        total = panel(at, mine[1], other[1], out_proj, pair, split, step, begin)
        for bit in reversed(bits[:-2]):
            half = total.shape[0] // 2
            far = add(total[half:], got[half:])
            total, got = add(total[:half], got[:half]), swap(far, "fsdp", bit)
        return far, (total, got, split, step)

    chunk = (pairs[1], SPLITS[0], body, body[0])
    away, got = send(*chunk)
    other[1], late_rest, _ = tie((other[1], late_pair[:, :, middle:], away))
    pairs.append((late_rest, swap(late_rest, "ctx", 2)))

    all_mine, all_other = (jnp.concatenate(parts, axis=0) for parts in (mine, other))
    total = panel(at, all_mine, all_other, out_proj, pairs[0], SPLITS[0], head)
    other[1], total = tie((other[1], total))
    total = total.reshape(2, part, *total.shape[1:])
    head_got = swap(total[:, part // 2 :], "fsdp", bits[-3])

    far, first_sum = sum_up(*chunk, got)
    mine[0], _ = tie((mine[0], far))
    head_got, _ = tie((head_got, far))
    total = add(total[:, : part // 2], head_got)
    for bit in reversed(bits[:-3]):
        half = total.shape[1] // 2
        total = add(total[:, :half], swap(total[:, half:], "fsdp", bit))
    head_sum = (total[1], swap(total[0], "fsdp", bits[-1]), SPLITS[0], head)
    sums = [first_sum]
    for pair, split, step, begin in (
        (pairs[2], SPLITS[1], tail[0], tail[0][0]),
        (pairs[3], SPLITS[1], tail[1], tail[1][0]),
        (pairs[0], SPLITS[0], foot, 0),
    ):
        away, got = send(pair, split, step, begin)
        mine[0], away = tie((mine[0], away))
        got, _ = tie((got, far))
        far, one = sum_up(pair, split, step, begin, got)
        sums.append(one)
    out = place_pieces(at, out, *head_sum)
    for one in sums:
        out = place_pieces(at, out, *one)
    return out[None]


def solution(mesh):
    return jax.shard_map(
        per_device,
        mesh=mesh,
        in_specs=(
            P("fsdp", "ctx"),
            P(),
            P(),
            P(None, None, "fsdp"),
            P(None, None, "fsdp"),
            P("fsdp", None),
            P("fsdp", None),
        ),
        out_specs=P("fsdp", "ctx", None),
        check_vma=False,
    )
```
